32 devices in a mesh: ctx: 16 (over z, y, x), tp: 2 (over core).
Axes of the slice: x: 2, y: 2, z: 4, core: 2. Of those that a mesh axis runs over, the one named last changes fastest.
Arguments:
- k_feature: bfloat16 [8, 524288], P('tp', 'ctx'), may hold values from -6 to 6
- v_feature: bfloat16 [8, 524288], P('tp', 'ctx'), may hold values from -6 to 6
- q_feature: bfloat16 [8, 524288], P('tp', 'ctx'), may hold values from -6 to 6
- spectrum: bfloat16 [2, 8, 1024, 1024], P(None, 'tp', 'ctx'), may hold values from -6 to 6
- skip_gain: float32 [8], P('tp'), may hold values from -1 to 1
- out_weight: bfloat16 [8, 16], replicated, may hold values from -2 to 2
Outputs:
- mixed: bfloat16 [16, 524288], P('tp', 'ctx')
The draws below stay inside these ranges and needn't reach their ends.
All inputs are finite; a program needn't handle non-finite values.
Results may differ from the reference program's by a relative error of at most 0.015.
Values may be sent and summed in bfloat16 or wider, within the bound.
No kernel may reach another device: no remote copies, remote signals or barrier semaphores. Data moves between devices by JAX's collectives and lax.ppermute only.
A program may use at most 64 MiB of HBM per device.

```python
import math
import jax
import jax.numpy as jnp
from jax import lax

BLOCK = 1024
SEQ = 524288
CHANNELS = 8
OUTS = 16


def block_levels(own_key, dims, cuts, smallest, largest):
    gain = 1.0
    for position, shards_of in cuts:
        steps = jax.random.uniform(jax.random.fold_in(jax.random.fold_in(own_key, 6), position), (shards_of,), jnp.float32, smallest / len(cuts), largest / len(cuts))
        gain = gain * jnp.repeat(jnp.exp(steps), dims[position] // shards_of).reshape((-1,) + (1,) * (len(dims) - 1 - position))
    return gain


def bell_draw(key, shape, width, most, cuts=(), kind=jnp.bfloat16):
    values = width * jax.random.normal(key, shape, jnp.float32)
    if cuts:
        values = values * block_levels(key, shape, cuts, -0.22, 0.18)
    return jnp.clip(values, -most, most).astype(kind)


def setup_inputs(seed: int = 0) -> dict:
    streams_of = jax.random.split(jax.random.key(seed), 7)
    k_feature = bell_draw(streams_of[0], (CHANNELS, SEQ), 1.0, 6.0, ((0, 2), (1, 16)))
    v_feature = bell_draw(streams_of[1], (CHANNELS, SEQ), 1.0, 6.0, ((0, 2), (1, 16)))
    q_feature = bell_draw(streams_of[2], (CHANNELS, SEQ), 1.0, 6.0, ((0, 2), (1, 16)))
    spectrum = bell_draw(streams_of[3], (2, CHANNELS, BLOCK, BLOCK), 1.0, 6.0, ((1, 2), (2, 16)))
    skip_gain = jnp.clip(jax.random.uniform(streams_of[4], (CHANNELS,), jnp.float32, -1.0, 1.0) * block_levels(streams_of[4], (CHANNELS,), ((0, 2),), -0.4, 0.0), -1.0, 1.0)
    out_weight = bell_draw(streams_of[5], (CHANNELS, OUTS), CHANNELS ** -0.5, 2.0)
    return dict(k_feature=k_feature, v_feature=v_feature, q_feature=q_feature, spectrum=spectrum, skip_gain=skip_gain, out_weight=out_weight)


def fourier_tables(length_all):
    positions = jnp.arange(length_all, dtype=jnp.int32)
    phase_index = (positions[:, None] * positions[None, :]) % length_all
    angles = phase_index.astype(jnp.float32) * (2.0 * math.pi / length_all)
    return jnp.cos(angles).astype(jnp.bfloat16), jnp.sin(angles).astype(jnp.bfloat16)


def twist_tables(left_index, right_index, length_all):
    phase_index = (left_index[:, None] * right_index[None, :]) % length_all
    angles = phase_index.astype(jnp.float32) * (2.0 * math.pi / length_all)
    return jnp.cos(angles), jnp.sin(angles)


def reference(k_feature, v_feature, q_feature, spectrum, skip_gain, out_weight):
    length_all = BLOCK * BLOCK
    product = (k_feature.astype(jnp.float32) * v_feature.astype(jnp.float32)).astype(jnp.bfloat16)
    cosine_full, sine_full = fourier_tables(BLOCK)
    cosine_half = cosine_full[: BLOCK // 2]
    sine_half = sine_full[: BLOCK // 2]
    positions = jnp.arange(BLOCK, dtype=jnp.int32)
    twist_cosine, twist_sine = twist_tables(positions, positions, length_all)

    def convolve(members):
        signal, response = members
        grid_rows = signal.reshape(BLOCK // 2, BLOCK)
        first_real = jnp.dot(cosine_half.T, grid_rows, preferred_element_type=jnp.float32)
        first_imag = -jnp.dot(sine_half.T, grid_rows, preferred_element_type=jnp.float32)
        spread_real = (first_real * twist_cosine + first_imag * twist_sine).astype(jnp.bfloat16)
        spread_imag = (first_imag * twist_cosine - first_real * twist_sine).astype(jnp.bfloat16)
        freq_real = jnp.dot(spread_real, cosine_full, preferred_element_type=jnp.float32) + jnp.dot(spread_imag, sine_full, preferred_element_type=jnp.float32)
        freq_imag = jnp.dot(spread_imag, cosine_full, preferred_element_type=jnp.float32) - jnp.dot(spread_real, sine_full, preferred_element_type=jnp.float32)
        resp_real = response[0].astype(jnp.float32)
        resp_imag = response[1].astype(jnp.float32)
        shaped_real = (freq_real * resp_real - freq_imag * resp_imag).astype(jnp.bfloat16)
        shaped_imag = (freq_real * resp_imag + freq_imag * resp_real).astype(jnp.bfloat16)
        inner_real = jnp.dot(shaped_real, cosine_full, preferred_element_type=jnp.float32) - jnp.dot(shaped_imag, sine_full, preferred_element_type=jnp.float32)
        inner_imag = jnp.dot(shaped_imag, cosine_full, preferred_element_type=jnp.float32) + jnp.dot(shaped_real, sine_full, preferred_element_type=jnp.float32)
        back_real = (inner_real * twist_cosine - inner_imag * twist_sine).astype(jnp.bfloat16)
        back_imag = (inner_imag * twist_cosine + inner_real * twist_sine).astype(jnp.bfloat16)
        summed = jnp.dot(cosine_half, back_real, preferred_element_type=jnp.float32) - jnp.dot(sine_half, back_imag, preferred_element_type=jnp.float32)
        return (summed * (1.0 / length_all)).astype(jnp.bfloat16).reshape(SEQ)

    convolved = lax.map(convolve, (product, jnp.moveaxis(spectrum, 1, 0)))
    gated_rows = (q_feature.astype(jnp.float32) * (convolved.astype(jnp.float32) + skip_gain[:, None] * product.astype(jnp.float32))).astype(jnp.bfloat16)
    return jnp.dot(out_weight.T, gated_rows, preferred_element_type=jnp.float32).astype(jnp.bfloat16)
```

```python
import functools
import math

import numpy as np
import ml_dtypes
import jax
import jax.numpy as jnp
from jax import lax
from jax.experimental import pallas as pl
from jax.experimental.pallas import tpu as pltpu
from jax.sharding import PartitionSpec as P

F32 = jnp.float32
BF16 = jnp.bfloat16
VMEM = pl.BlockSpec(memory_space=pltpu.VMEM)
MIB = 1 << 20


def fourier_tables(length_all):
    positions = jnp.arange(length_all, dtype=jnp.int32)
    phase_index = positions[:, None] * positions[None, :] % length_all
    angles = phase_index.astype(jnp.float32) * (2.0 * math.pi / length_all)
    return (jnp.cos(angles).astype(jnp.bfloat16), jnp.sin(angles).astype(jnp.bfloat16))


def twist_tables(left_index, right_index, length_all):
    phase_index = left_index[:, None] * right_index[None, :] % length_all
    angles = phase_index.astype(jnp.float32) * (2.0 * math.pi / length_all)
    return (jnp.cos(angles), jnp.sin(angles))


def contract(form, left, right):
    return jnp.einsum(form, left, right, preferred_element_type=jnp.float32)


def local_general(k_feature, v_feature, q_feature, spectrum, skip_gain, out_weight):
    channels, tokens = k_feature.shape
    block_order = spectrum.shape[3]
    length_all = block_order * block_order
    ctx_count = lax.axis_size("ctx")
    slab_width = block_order // ctx_count
    rows_here = tokens // block_order
    ctx_index = lax.axis_index("ctx")
    product = (k_feature.astype(jnp.float32) * v_feature.astype(jnp.float32)).astype(jnp.bfloat16)
    cosine_full, sine_full = fourier_tables(block_order)
    cosine_half = cosine_full[: block_order // 2]
    sine_half = sine_full[: block_order // 2]
    positions = jnp.arange(block_order, dtype=jnp.int32)
    local_ticks = ctx_index * slab_width + jnp.arange(slab_width, dtype=jnp.int32)
    grid_rows = lax.all_to_all(
        product.reshape(channels, rows_here, block_order),
        "ctx",
        split_axis=2,
        concat_axis=1,
        tiled=True,
    )
    first_real = contract("cij,ia->caj", grid_rows, cosine_half)
    first_imag = -contract("cij,ia->caj", grid_rows, sine_half)
    twist_cosine, twist_sine = twist_tables(positions, local_ticks, length_all)
    spread_real = (first_real * twist_cosine + first_imag * twist_sine).astype(jnp.bfloat16)
    spread_imag = (first_imag * twist_cosine - first_real * twist_sine).astype(jnp.bfloat16)
    block_real, block_imag = (
        lax.all_to_all(spread_real, "ctx", split_axis=1, concat_axis=2, tiled=True),
        lax.all_to_all(spread_imag, "ctx", split_axis=1, concat_axis=2, tiled=True),
    )
    freq_real = contract("caj,jb->cab", block_real, cosine_full) + contract(
        "caj,jb->cab", block_imag, sine_full
    )
    freq_imag = contract("caj,jb->cab", block_imag, cosine_full) - contract(
        "caj,jb->cab", block_real, sine_full
    )
    resp_real = spectrum[0].astype(jnp.float32)
    resp_imag = spectrum[1].astype(jnp.float32)
    shaped_real = (freq_real * resp_real - freq_imag * resp_imag).astype(jnp.bfloat16)
    shaped_imag = (freq_real * resp_imag + freq_imag * resp_real).astype(jnp.bfloat16)
    inner_real = contract("cab,bj->caj", shaped_real, cosine_full) - contract(
        "cab,bj->caj", shaped_imag, sine_full
    )
    inner_imag = contract("cab,bj->caj", shaped_imag, cosine_full) + contract(
        "cab,bj->caj", shaped_real, sine_full
    )
    twist_cosine, twist_sine = twist_tables(local_ticks, positions, length_all)
    back_real = (inner_real * twist_cosine - inner_imag * twist_sine).astype(jnp.bfloat16)
    back_imag = (inner_imag * twist_cosine + inner_real * twist_sine).astype(jnp.bfloat16)
    summed = contract(
        "ia,caj->cij",
        cosine_half,
        lax.all_to_all(back_real, "ctx", split_axis=2, concat_axis=1, tiled=True),
    ) - contract(
        "ia,caj->cij",
        sine_half,
        lax.all_to_all(back_imag, "ctx", split_axis=2, concat_axis=1, tiled=True),
    )
    spatial = (summed * (1.0 / length_all)).astype(jnp.bfloat16)
    convolved = lax.all_to_all(spatial, "ctx", split_axis=1, concat_axis=2, tiled=True).reshape(
        channels, tokens
    )
    gated_rows = (
        q_feature.astype(jnp.float32)
        * (convolved.astype(jnp.float32) + skip_gain[:, None] * product.astype(jnp.float32))
    ).astype(jnp.bfloat16)
    tp_index = lax.axis_index("tp")
    my_weight = lax.dynamic_slice_in_dim(out_weight, tp_index * channels, channels, 0)
    return lax.psum_scatter(
        jnp.dot(my_weight.T, gated_rows, preferred_element_type=jnp.float32).astype(jnp.bfloat16),
        "tp",
        scatter_dimension=0,
        tiled=True,
    )


def cosine_sine(product, length):
    angles = (product % length).astype(np.float64) * (2.0 * np.pi / length)
    return np.cos(angles), np.sin(angles)


@functools.lru_cache(maxsize=None)
def constant_tables(block, members, rows_half, a_half):
    quarter = block // 4
    firsts, lasts, twists = [], [], []
    part = np.arange(members)
    for g in range(2):
        for s in range(2):
            a = (
                (g * members + part)[:, None] * 2 * a_half
                + s * a_half
                + np.arange(a_half)[None, :]
            ).reshape(-1)

            def rows(group, core):
                device = group * members + part
                i = device[:, None] * 2 * rows_half + core * rows_half
                return (i + np.arange(rows_half)[None, :]).reshape(-1)

            i_in = np.concatenate([rows(g, s), rows(g, 1 - s), rows(1 - g, s), rows(1 - g, 1 - s)])
            cosine, sine = cosine_sine(a[:, None] * i_in[None, :], block)
            firsts.append(np.concatenate([cosine, -sine], 0))
            i_out = np.concatenate([rows(0, 1 - s), rows(1, 1 - s), rows(0, s), rows(1, s)])
            cosine, sine = cosine_sine(i_out[:, None] * a[None, :], block)
            lasts.append(np.concatenate([cosine, -sine], 1))
            twists.append(np.stack(cosine_sine(a[:, None] * np.arange(block)[None, :], block * block)))
    inner, outer = [], []
    for rho in range(4):
        cosine, sine = cosine_sine(
            np.arange(quarter)[:, None] * (4 * np.arange(quarter) + rho)[None, :], block
        )
        inner.append(np.block([[cosine, -sine], [sine, cosine]]))
        outer.append(np.block([[cosine.T, sine.T], [-sine.T, cosine.T]]))
    order = np.zeros((block, block), np.float32)
    b = np.arange(block)
    order[b, (b % 4) * quarter + b // 4] = 1.0
    narrow = lambda x: np.asarray(x, np.float32).astype(ml_dtypes.bfloat16)
    return dict(
        first=narrow(np.stack(firsts)),
        last=narrow(np.stack(lasts)),
        twist=np.stack(twists).astype(np.float32),
        inner=narrow(np.stack(inner)),
        outer=narrow(np.stack(outer)),
        order=narrow(order),
    )


def rows_order(channels, rows):
    table = np.zeros((channels * rows, channels * rows), np.float32)
    half = rows // 2
    for i in range(rows):
        for c in range(channels):
            table[(i // half) * channels * half + c * half + i % half, i * channels + c] = 1.0
    return table.astype(ml_dtypes.bfloat16)


def rows_kernel(block, *refs):
    *ins, order_ref, out_ref = refs
    tokens = ins[0].shape[1]
    pieces = []
    for i in range(tokens // block):
        cut = slice(i * block, (i + 1) * block)
        piece = ins[0][:, cut].astype(F32)
        for other in ins[1:]:
            piece = piece * other[:, cut].astype(F32)
        pieces.append(piece)
    stacked = jnp.concatenate(pieces, axis=0).astype(BF16)
    ordered = jnp.dot(order_ref[...], stacked, preferred_element_type=F32)
    out_ref[...] = ordered.astype(BF16).reshape(out_ref.shape)


def as_rows(block, *arrays):
    channels, tokens = arrays[0].shape
    rows = tokens // block
    return pl.pallas_call(
        functools.partial(rows_kernel, block),
        out_shape=jax.ShapeDtypeStruct((2, channels, rows // 2, block), BF16),
        in_specs=[VMEM] * (len(arrays) + 1),
        out_specs=VMEM,
        compiler_params=pltpu.CompilerParams(vmem_limit_bytes=16 * MIB),
        cost_estimate=pl.CostEstimate(flops=40_000_000, bytes_accessed=MIB, transcendentals=0),
    )(*arrays, jnp.asarray(rows_order(channels, rows)))


def spectrum_kernel(in_ref, order_ref, out_ref):
    block = order_ref.shape[0]
    rows = in_ref[...].reshape(-1, block)
    moved = jnp.dot(rows, order_ref[...], preferred_element_type=F32)
    out_ref[...] = moved.astype(BF16).reshape(out_ref.shape)


def arrange_spectrum(spectrum, order):
    two, channels, a_here, block = spectrum.shape
    a_half = a_here // 2
    return pl.pallas_call(
        spectrum_kernel,
        grid=(2, channels),
        out_shape=jax.ShapeDtypeStruct((2, channels, two, a_half, block), BF16),
        in_specs=[
            pl.BlockSpec((two, 1, a_half, block), lambda h, c: (0, c, h, 0)),
            pl.BlockSpec((block, block), lambda h, c: (0, 0)),
        ],
        out_specs=pl.BlockSpec((1, 1, two, a_half, block), lambda h, c: (h, c, 0, 0, 0)),
        compiler_params=pltpu.CompilerParams(vmem_limit_bytes=16 * MIB),
        cost_estimate=pl.CostEstimate(
            flops=1_100_000_000, bytes_accessed=4 * MIB, transcendentals=0
        ),
    )(spectrum, order)


def transform_kernel(
    place_ref, xa, xb, za1, za2, zb1, zb2, first, twist, spec, inner, outer, last, send, keep
):
    block = xa.shape[-1]
    quarter = block // 4
    flat = lambda ref: ref[...].reshape(-1, block)
    signal = jnp.concatenate([flat(xa), flat(xb), flat(za1), flat(za2), flat(zb1), flat(zb2)], 0)
    a_rows = first.shape[1] // 2
    turned = []
    for q in range(4):
        cut = slice(q * quarter, (q + 1) * quarter)
        both = jnp.dot(first[0], signal[:, cut], preferred_element_type=F32)
        real, imag = both[:a_rows], both[a_rows:]
        cosine, sine = twist[0, 0, :, cut], twist[0, 1, :, cut]
        turned.append((real * cosine + imag * sine, imag * cosine - real * sine))
    (r0, i0), (r1, i1), (r2, i2), (r3, i3) = turned
    er, ei, dr, di = r0 + r2, i0 + i2, r0 - r2, i0 - i2
    fr, fi, hr, hi = r1 + r3, i1 + i3, r1 - r3, i1 - i3
    mixes = [(er + fr, ei + fi), (dr + hi, di - hr), (er - fr, ei - fi), (dr - hi, di + hr)]
    backs = []
    for rho in range(4):
        real, imag = mixes[rho]
        pair = jnp.concatenate([real.astype(BF16), imag.astype(BF16)], axis=1)
        freq = jnp.dot(pair, inner[rho], preferred_element_type=F32)
        zr, zi = freq[:, :quarter], freq[:, quarter:]
        cut = slice(rho * quarter, (rho + 1) * quarter)
        gr = spec[:, 0, :, cut].reshape(-1, quarter).astype(F32)
        gi = spec[:, 1, :, cut].reshape(-1, quarter).astype(F32)
        pair = jnp.concatenate(
            [(zr * gr - zi * gi).astype(BF16), (zr * gi + zi * gr).astype(BF16)], axis=1
        )
        out = jnp.dot(pair, outer[rho], preferred_element_type=F32)
        backs.append((out[:, :quarter], out[:, quarter:]))
    (r0, i0), (r1, i1), (r2, i2), (r3, i3) = backs
    er, ei, dr, di = r0 + r2, i0 + i2, r0 - r2, i0 - i2
    fr, fi, hr, hi = r1 + r3, i1 + i3, r1 - r3, i1 - i3
    mixes = [(er + fr, ei + fi), (dr - hi, di + hr), (er - fr, ei - fi), (dr + hi, di - hr)]
    scale = 1.0 / (block * block)
    half = last.shape[1] // 2
    for q in range(4):
        cut = slice(q * quarter, (q + 1) * quarter)
        real, imag = mixes[q]
        cosine, sine = twist[0, 0, :, cut], twist[0, 1, :, cut]
        pair = jnp.concatenate(
            [
                (real * cosine - imag * sine).astype(BF16),
                (imag * cosine + real * sine).astype(BF16),
            ],
            axis=0,
        )
        out = jnp.dot(last[0], pair, preferred_element_type=F32) * scale
        send[:, :, cut] = out[:half].astype(BF16).reshape(send.shape[0], send.shape[1], quarter)
        keep[:, :, cut] = out[half:].reshape(keep.shape[0], keep.shape[1], quarter)


def transform(place, pieces, spec, tables):
    members, rows_half, block = pieces[0].shape
    whole = lambda x: pl.BlockSpec(x.shape, lambda n, p: (0,) * x.ndim)
    picked = lambda x: pl.BlockSpec((1,) + x.shape[1:], lambda n, p: (p[0],) + (0,) * (x.ndim - 1))
    first, twist, last = tables["first"], tables["twist"], tables["last"]
    inner, outer = tables["inner"], tables["outer"]
    out = (2 * members, rows_half, block)
    return pl.pallas_call(
        transform_kernel,
        grid_spec=pltpu.PrefetchScalarGridSpec(
            num_scalar_prefetch=1,
            grid=(1,),
            in_specs=[whole(x) for x in pieces]
            + [picked(first), picked(twist), whole(spec), whole(inner), whole(outer), picked(last)],
            out_specs=[pl.BlockSpec(out, lambda n, p: (0, 0, 0))] * 2,
        ),
        out_shape=[jax.ShapeDtypeStruct(out, BF16), jax.ShapeDtypeStruct(out, F32)],
        compiler_params=pltpu.CompilerParams(vmem_limit_bytes=48 * MIB),
        cost_estimate=pl.CostEstimate(
            flops=2_200_000_000, bytes_accessed=12 * MIB, transcendentals=0
        ),
    )(place, *pieces, first, twist, spec, inner, outer, last)


def gate_kernel(conv, prod, gate, skip, weight, keep, send):
    _, channels, rows, block = conv.shape
    pieces = []
    for c in range(channels):
        total = conv[0, c].astype(F32) + conv[1, c].astype(F32)
        total = total + skip[c] * prod[c].astype(F32)
        pieces.append((gate[c].astype(F32) * total).astype(BF16))
    gated = jnp.concatenate(pieces, axis=0)
    mixed = jnp.dot(weight[...], gated, preferred_element_type=F32)
    outs = keep.shape[0]
    for r in range(rows):
        cut = slice(r * block, (r + 1) * block)
        keep[:, cut] = mixed[r * outs : (r + 1) * outs].astype(BF16)
        send[:, cut] = mixed[(rows + r) * outs : (rows + r + 1) * outs].astype(BF16)


def gate_and_project(conv, prod, gate, skip, weight, outs):
    _, channels, rows, block = conv.shape
    return pl.pallas_call(
        gate_kernel,
        out_shape=[jax.ShapeDtypeStruct((outs, rows * block), BF16)] * 2,
        in_specs=[VMEM, VMEM, VMEM, pl.BlockSpec(memory_space=pltpu.SMEM), VMEM],
        out_specs=[VMEM, VMEM],
        compiler_params=pltpu.CompilerParams(vmem_limit_bytes=16 * MIB),
        cost_estimate=pl.CostEstimate(
            flops=80_000_000, bytes_accessed=2 * MIB, transcendentals=0
        ),
    )(conv, prod, gate, skip, weight)


def local_channels(k_feature, v_feature, q_feature, spectrum, skip_gain, out_weight):
    channels, tokens = k_feature.shape
    block = spectrum.shape[3]
    ctx_count = lax.axis_size("ctx")
    members = ctx_count // 2
    rows_half = tokens // block // 2
    a_half = spectrum.shape[2] // 2
    outs = out_weight.shape[1] // 2
    ctx, tp = lax.axis_index("ctx"), lax.axis_index("tp")
    tables = {
        name: jnp.asarray(table)
        for name, table in constant_tables(block, members, rows_half, a_half).items()
    }
    halves = [list(range(members)), list(range(members, 2 * members))]
    spread = lambda x: lax.all_to_all(x, "ctx", 0, 0, axis_index_groups=halves, tiled=True)
    across = lambda x: lax.ppermute(
        x, "ctx", [(d, (d + members) % ctx_count) for d in range(ctx_count)]
    )
    swap = lambda x: lax.ppermute(x, "tp", [(0, 1), (1, 0)])
    regroup = lambda x: lax.all_to_all(x, "tp", 0, 0, tiled=True)

    product = regroup(as_rows(block, k_feature, v_feature)).reshape(members, rows_half, block)
    xa = spread(product)
    xb = swap(xa)
    cut = members // 2
    za1, za2 = across(xa[:cut]), across(xa[cut:])
    zb1, zb2 = swap(za1), swap(za2)
    gate = regroup(as_rows(block, q_feature)).reshape(members, rows_half, block)
    skip = regroup(jnp.broadcast_to(skip_gain[None], (2, channels))).reshape(-1)
    spec = regroup(arrange_spectrum(spectrum, tables["order"]))
    spec = spread(spec.reshape(members, 2, a_half, block))

    place = (ctx // members * 2 + tp).astype(jnp.int32).reshape(1)
    send, keep = transform(place, (xa, xb, za1, za2, zb1, zb2), spec, tables)
    total = (keep + swap(send).astype(F32)).astype(BF16)
    conv = lax.all_to_all(total, "ctx", 0, 0, tiled=True).reshape(2, members, rows_half, block)

    mine = lax.dynamic_slice_in_dim(out_weight, tp * outs, outs, 1)
    other = lax.dynamic_slice_in_dim(out_weight, (1 - tp) * outs, outs, 1)
    weight = jnp.stack([mine, other]).astype(F32)
    weight = jnp.einsum("hce,rs->hrecs", weight, jnp.eye(rows_half, dtype=F32))
    weight = weight.astype(BF16).reshape(2 * rows_half * outs, members * rows_half)
    kept, sent = gate_and_project(conv, product, gate, skip, weight, outs)
    came = swap(sent)
    low = jnp.where(tp == 0, kept, came)
    high = jnp.where(tp == 0, came, kept)
    return jnp.concatenate([low, high], axis=1)


def local(k_feature, v_feature, q_feature, spectrum, skip_gain, out_weight):
    channels, tokens = k_feature.shape
    block = spectrum.shape[3]
    ctx_count, tp_count = lax.axis_size("ctx"), lax.axis_size("tp")
    by_channels = (
        tp_count == 2
        and ctx_count == 2 * channels * tp_count
        and tokens * ctx_count * 2 == block * block
        and tokens % (32 * block) == 0
        and spectrum.shape[2] % 32 == 0
        and block % 512 == 0
        and out_weight.shape[1] % 16 == 0
    )
    plan = local_channels if by_channels else local_general
    return plan(k_feature, v_feature, q_feature, spectrum, skip_gain, out_weight)


def solution(mesh):
    placed = (
        P("tp", "ctx"),
        P("tp", "ctx"),
        P("tp", "ctx"),
        P(None, "tp", "ctx", None),
        P("tp"),
        P(),
    )
    return jax.shard_map(
        local, mesh=mesh, in_specs=placed, out_specs=P("tp", "ctx"), check_vma=False
    )
```

```python
import functools
import math

import numpy as np
import ml_dtypes
import jax
import jax.numpy as jnp
from jax import lax
from jax.experimental import pallas as pl
from jax.experimental.pallas import tpu as pltpu
from jax.sharding import PartitionSpec as P

F32 = jnp.float32
BF16 = jnp.bfloat16
VMEM = pl.BlockSpec(memory_space=pltpu.VMEM)
SMEM = pl.BlockSpec(memory_space=pltpu.SMEM)
ANY = pl.BlockSpec(memory_space=pltpu.HBM)
MIB = 1 << 20
SMALL = pl.CostEstimate(flops=1, bytes_accessed=1, transcendentals=0)


def fourier_tables(length_all):
    positions = jnp.arange(length_all, dtype=jnp.int32)
    phase_index = positions[:, None] * positions[None, :] % length_all
    angles = phase_index.astype(jnp.float32) * (2.0 * math.pi / length_all)
    return (jnp.cos(angles).astype(jnp.bfloat16), jnp.sin(angles).astype(jnp.bfloat16))


def twist_tables(left_index, right_index, length_all):
    phase_index = left_index[:, None] * right_index[None, :] % length_all
    angles = phase_index.astype(jnp.float32) * (2.0 * math.pi / length_all)
    return (jnp.cos(angles), jnp.sin(angles))


def contract(form, left, right):
    return jnp.einsum(form, left, right, preferred_element_type=jnp.float32)


def local_general(k_feature, v_feature, q_feature, spectrum, skip_gain, out_weight):
    channels, tokens = k_feature.shape
    block_order = spectrum.shape[3]
    length_all = block_order * block_order
    ctx_count = lax.axis_size("ctx")
    slab_width = block_order // ctx_count
    rows_here = tokens // block_order
    ctx_index = lax.axis_index("ctx")
    product = (k_feature.astype(jnp.float32) * v_feature.astype(jnp.float32)).astype(jnp.bfloat16)
    cosine_full, sine_full = fourier_tables(block_order)
    cosine_half = cosine_full[: block_order // 2]
    sine_half = sine_full[: block_order // 2]
    positions = jnp.arange(block_order, dtype=jnp.int32)
    local_ticks = ctx_index * slab_width + jnp.arange(slab_width, dtype=jnp.int32)
    grid_rows = lax.all_to_all(
        product.reshape(channels, rows_here, block_order),
        "ctx",
        split_axis=2,
        concat_axis=1,
        tiled=True,
    )
    first_real = contract("cij,ia->caj", grid_rows, cosine_half)
    first_imag = -contract("cij,ia->caj", grid_rows, sine_half)
    twist_cosine, twist_sine = twist_tables(positions, local_ticks, length_all)
    spread_real = (first_real * twist_cosine + first_imag * twist_sine).astype(jnp.bfloat16)
    spread_imag = (first_imag * twist_cosine - first_real * twist_sine).astype(jnp.bfloat16)
    block_real, block_imag = (
        lax.all_to_all(spread_real, "ctx", split_axis=1, concat_axis=2, tiled=True),
        lax.all_to_all(spread_imag, "ctx", split_axis=1, concat_axis=2, tiled=True),
    )
    freq_real = contract("caj,jb->cab", block_real, cosine_full) + contract(
        "caj,jb->cab", block_imag, sine_full
    )
    freq_imag = contract("caj,jb->cab", block_imag, cosine_full) - contract(
        "caj,jb->cab", block_real, sine_full
    )
    resp_real = spectrum[0].astype(jnp.float32)
    resp_imag = spectrum[1].astype(jnp.float32)
    shaped_real = (freq_real * resp_real - freq_imag * resp_imag).astype(jnp.bfloat16)
    shaped_imag = (freq_real * resp_imag + freq_imag * resp_real).astype(jnp.bfloat16)
    inner_real = contract("cab,bj->caj", shaped_real, cosine_full) - contract(
        "cab,bj->caj", shaped_imag, sine_full
    )
    inner_imag = contract("cab,bj->caj", shaped_imag, cosine_full) + contract(
        "cab,bj->caj", shaped_real, sine_full
    )
    twist_cosine, twist_sine = twist_tables(local_ticks, positions, length_all)
    back_real = (inner_real * twist_cosine - inner_imag * twist_sine).astype(jnp.bfloat16)
    back_imag = (inner_imag * twist_cosine + inner_real * twist_sine).astype(jnp.bfloat16)
    summed = contract(
        "ia,caj->cij",
        cosine_half,
        lax.all_to_all(back_real, "ctx", split_axis=2, concat_axis=1, tiled=True),
    ) - contract(
        "ia,caj->cij",
        sine_half,
        lax.all_to_all(back_imag, "ctx", split_axis=2, concat_axis=1, tiled=True),
    )
    spatial = (summed * (1.0 / length_all)).astype(jnp.bfloat16)
    convolved = lax.all_to_all(spatial, "ctx", split_axis=1, concat_axis=2, tiled=True).reshape(
        channels, tokens
    )
    gated_rows = (
        q_feature.astype(jnp.float32)
        * (convolved.astype(jnp.float32) + skip_gain[:, None] * product.astype(jnp.float32))
    ).astype(jnp.bfloat16)
    tp_index = lax.axis_index("tp")
    my_weight = lax.dynamic_slice_in_dim(out_weight, tp_index * channels, channels, 0)
    return lax.psum_scatter(
        jnp.dot(my_weight.T, gated_rows, preferred_element_type=jnp.float32).astype(jnp.bfloat16),
        "tp",
        scatter_dimension=0,
        tiled=True,
    )


def cosine_sine(product, length):
    angles = (product % length).astype(np.float64) * (2.0 * np.pi / length)
    return np.cos(angles), np.sin(angles)


@functools.lru_cache(maxsize=None)
def constant_tables(block, members, rows_half, a_half):
    quarter = block // 4
    firsts, lasts, coarses, fines = [], [], [], []
    part = np.arange(members)
    for g in range(2):
        for s in range(2):
            a = (
                (g * members + part)[:, None] * 2 * a_half
                + s * a_half
                + np.arange(a_half)[None, :]
            ).reshape(-1)

            def rows(group, core):
                device = group * members + part
                i = device[:, None] * 2 * rows_half + core * rows_half
                return (i + np.arange(rows_half)[None, :]).reshape(-1)

            i_in = np.concatenate([rows(g, s), rows(g, 1 - s), rows(1 - g, s), rows(1 - g, 1 - s)])
            cosine, sine = cosine_sine(a[:, None] * i_in[None, :], block)
            firsts.append(np.concatenate([cosine, -sine], 0))
            i_out = np.concatenate([rows(0, 1 - s), rows(1, 1 - s), rows(0, s), rows(1, s)])
            cosine, sine = cosine_sine(i_out[:, None] * a[None, :], block)
            lasts.append(np.concatenate([cosine, -sine], 1))
            coarse = 128 * (np.arange(128) % (block // 128))
            coarses.append(np.stack(cosine_sine(a[:, None] * coarse[None, :], block * block)))
            fines.append(np.stack(cosine_sine(a[:, None] * np.arange(128)[None, :], block * block)))
    inner = []
    for rho in range(4):
        cosine, sine = cosine_sine(
            np.arange(quarter)[:, None] * (4 * np.arange(quarter) + rho)[None, :], block
        )
        inner.append(np.stack([cosine, sine, cosine.T, sine.T]))
    order = np.zeros((quarter, quarter), np.float32)
    b = np.arange(quarter)
    order[b, (b % 4) * (quarter // 4) + b // 4] = 1.0
    narrow = lambda x: np.asarray(x, np.float32).astype(ml_dtypes.bfloat16)
    return dict(
        first=narrow(np.stack(firsts)),
        last=narrow(np.stack(lasts)),
        turns=np.stack([coarses, fines], 1).astype(np.float32),
        inner=narrow(np.stack(inner)),
        order=narrow(order),
    )


def product_kernel(block, count, core_ref, *refs):
    ins, outs, scratch, sem = refs[:count], refs[count:-1 - count], refs[-1 - count : -1], refs[-1]
    copies = [pltpu.make_async_copy(ins[n], scratch[n], sem.at[n]) for n in range(count)]
    for copy in copies:
        copy.start()
    rows_copy = None
    if len(outs) == 4:
        spectrum, own, send, other_rows = outs
        a_half = other_rows.shape[2]
        at = pl.ds(pl.multiple_of((1 - core_ref[0]) * a_half, a_half), a_half)
        rows_copy = pltpu.make_async_copy(spectrum.at[:, :, at, :], other_rows, sem.at[count])
        rows_copy.start()
    else:
        own, send = outs
    core = core_ref[0]
    channels, tokens = ins[0].shape
    place = 0 if own.shape[0] == channels else channels * core
    rows = tokens // block
    half = rows // 2
    to = lax.broadcasted_iota(jnp.int32, (channels * rows, channels * rows), 0)
    at = lax.broadcasted_iota(jnp.int32, (channels * rows, channels * rows), 1)
    side = jnp.bitwise_xor(to // (channels * half), core)
    source = (side * half + to % half) * channels + (to // half) % channels
    order = jnp.where(at == source, 1.0, 0.0).astype(BF16)
    for copy in copies:
        copy.wait()
    pieces = []
    for i in range(rows):
        cut = slice(i * block, (i + 1) * block)
        piece = scratch[0][:, cut].astype(F32)
        for other in scratch[1:]:
            piece = piece * other[:, cut].astype(F32)
        pieces.append(piece)
    stacked = jnp.concatenate(pieces, axis=0).astype(BF16)
    ordered = jnp.dot(order, stacked, preferred_element_type=F32).astype(BF16)
    ordered = ordered.reshape(2, channels, half, block)
    own[pl.ds(place, channels)] = ordered[0]
    send[...] = ordered[1]
    if rows_copy is not None:
        rows_copy.wait()


def as_rows(core, block, *arrays, spectrum=None):
    channels, tokens = arrays[0].shape
    half = tokens // block // 2
    room, extra, shapes = 1, [], []
    if spectrum is not None:
        two, _, a_here, _ = spectrum.shape
        room, extra = 2, [spectrum]
        shapes = [jax.ShapeDtypeStruct((two, channels, a_here // 2, block), BF16)]
    return pl.pallas_call(
        functools.partial(product_kernel, block, len(arrays)),
        out_shape=[
            jax.ShapeDtypeStruct((room * channels, half, block), BF16),
            jax.ShapeDtypeStruct((channels, half, block), BF16),
        ]
        + shapes,
        in_specs=[SMEM] + [ANY] * len(arrays + tuple(extra)),
        out_specs=[VMEM] * (2 + len(shapes)),
        scratch_shapes=[pltpu.VMEM((channels, tokens), BF16)] * len(arrays)
        + [pltpu.SemaphoreType.DMA((len(arrays) + 1,))],
        cost_estimate=SMALL,
    )(core, *arrays, *extra)


def spectrum_kernel(core_ref, in_ref, came_ref, order_ref, *refs):
    moved, rows, came, order, sem = refs
    core = core_ref[0]
    two, channels, a_half, block = rows.shape
    at = pl.ds(pl.multiple_of(core * a_half, a_half), a_half)
    copies = [
        pltpu.make_async_copy(order_ref, order, sem.at[0]),
        pltpu.make_async_copy(in_ref.at[:, :, at, :], rows, sem.at[1]),
        pltpu.make_async_copy(came_ref, came, sem.at[2]),
    ]
    for copy in copies:
        copy.start()
    copies[0].wait()
    quarter = block // 4
    step = quarter // 4
    for side, ref in ((core, rows), (1 - core, came)):
        copies[1 if ref is rows else 2].wait()
        flat = jnp.concatenate([ref[n, c] for c in range(channels) for n in range(two)], 0)
        parts = [
            jnp.dot(flat[:, q * quarter : (q + 1) * quarter], order[...], preferred_element_type=F32)
            for q in range(4)
        ]
        for rho in range(4):
            columns = [part[:, rho * step : (rho + 1) * step] for part in parts]
            columns = jnp.concatenate(columns, axis=1).astype(BF16)
            moved[pl.ds(channels * side, channels), :, :, rho * quarter : (rho + 1) * quarter] = (
                columns.reshape(channels, two, a_half, quarter)
            )


def arrange_spectrum(core, spectrum, came, order):
    two, channels, a_half, block = came.shape
    return pl.pallas_call(
        spectrum_kernel,
        out_shape=jax.ShapeDtypeStruct((2 * channels, two, a_half, block), BF16),
        in_specs=[SMEM, ANY, ANY, ANY],
        out_specs=VMEM,
        scratch_shapes=[
            pltpu.VMEM(came.shape, BF16),
            pltpu.VMEM(came.shape, BF16),
            pltpu.VMEM(order.shape, BF16),
            pltpu.SemaphoreType.DMA((3,)),
        ],
        cost_estimate=SMALL,
    )(core, spectrum, came, order)


def weight_kernel(rows, core_ref, weight, out):
    channels, outs = weight.shape
    half = outs // 2
    core = core_ref[0]
    shape = out.shape
    to = lax.broadcasted_iota(jnp.int32, (shape[0], outs), 0)
    at = lax.broadcasted_iota(jnp.int32, (shape[0], outs), 1)
    column = jnp.bitwise_xor(to // (rows * half), core) * half + to % half
    pick = jnp.where(at == column, 1.0, 0.0).astype(BF16)
    turned = lax.dot_general(
        pick, weight[...], (((1,), (1,)), ((), ())), preferred_element_type=F32
    ).astype(BF16)
    to = lax.broadcasted_iota(jnp.int32, (channels, shape[1]), 0)
    at = lax.broadcasted_iota(jnp.int32, (channels, shape[1]), 1)
    channel = (at // rows + core * (channels // 2)) % channels
    widen = jnp.where(channel == to, 1.0, 0.0).astype(BF16)
    wide = jnp.dot(turned, widen, preferred_element_type=F32)
    to = lax.broadcasted_iota(jnp.int32, shape, 0)
    at = lax.broadcasted_iota(jnp.int32, shape, 1)
    out[...] = jnp.where(at % rows == (to // half) % rows, wide, 0.0).astype(BF16)


def projection(core, weight, rows):
    channels, outs = weight.shape
    return pl.pallas_call(
        functools.partial(weight_kernel, rows),
        out_shape=jax.ShapeDtypeStruct((rows * outs, rows * channels), BF16),
        in_specs=[SMEM, VMEM],
        out_specs=VMEM,
        compiler_params=pltpu.CompilerParams(vmem_limit_bytes=4 * MIB),
    )(core, weight)


def butterflies(values, sign):
    (r0, i0), (r1, i1), (r2, i2), (r3, i3) = values
    er, ei, dr, di = r0 + r2, i0 + i2, r0 - r2, i0 - i2
    fr, fi, hr, hi = r1 + r3, i1 + i3, r1 - r3, i1 - i3
    plus, minus = (dr - hi, di + hr), (dr + hi, di - hr)
    if sign < 0:
        plus, minus = minus, plus
    return [(er + fr, ei + fi), plus, (er - fr, ei - fi), minus]


def turn(values, cosine, sine):
    real, imag = values
    rows = real.shape[0]
    both = jnp.concatenate([real.astype(BF16), imag.astype(BF16)], axis=0)
    with_cosine = jnp.dot(both, cosine, preferred_element_type=F32)
    with_sine = jnp.dot(both, sine, preferred_element_type=F32)
    return with_cosine[:rows], with_cosine[rows:], with_sine[:rows], with_sine[rows:]


def transform_kernel(place_ref, *refs):
    ins, (send, keep, signal, spec, *tables, twist, sem) = refs[:9], refs[-10:]
    first, turns, inner, last = tables
    pieces, spec_in, (first_in, turns_in, inner_in, last_in) = ins[:4], ins[4], ins[5:9]
    place = place_ref[0]
    count = pieces[0].shape[0]
    moves = [(first_in.at[place], first)]
    moves += [(ref, signal.at[pl.ds(n * count, count)]) for n, ref in enumerate(pieces)]
    moves += [(turns_in.at[place], turns), (inner_in, inner), (spec_in, spec)]
    moves += [(last_in.at[place], last)]
    copies = [pltpu.make_async_copy(*move, sem.at[n]) for n, move in enumerate(moves)]
    for copy in copies:
        copy.start()
    for copy in copies[:6]:
        copy.wait()
    block = signal.shape[-1]
    quarter = block // 4
    lines = signal[...].reshape(-1, block)
    a_rows = first.shape[0] // 2
    turned = []
    for q in range(4):
        cut = slice(q * quarter, (q + 1) * quarter)
        both = jnp.dot(first[...], lines[:, cut], preferred_element_type=F32)
        for h in range(q * quarter // 128, (q + 1) * quarter // 128):
            lanes = slice(128 * h, 128 * (h + 1))
            uc, us = turns[0, 0, :, h : h + 1], turns[0, 1, :, h : h + 1]
            vc, vs = turns[1, 0], turns[1, 1]
            twist[0, :, lanes] = uc * vc - us * vs
            twist[1, :, lanes] = us * vc + uc * vs
        real, imag = both[:a_rows], both[a_rows:]
        cosine, sine = twist[0, :, cut], twist[1, :, cut]
        turned.append((real * cosine + imag * sine, imag * cosine - real * sine))
    mixes = butterflies(turned, -1)
    for copy in copies[6:-1]:
        copy.wait()
    backs = []
    for rho in range(4):
        rc, ic, rs, si = turn(mixes[rho], inner[rho, 0], inner[rho, 1])
        zr, zi = rc + si, ic - rs
        cut = slice(rho * quarter, (rho + 1) * quarter)
        gr = spec[:, 0, :, cut].reshape(-1, quarter).astype(F32)
        gi = spec[:, 1, :, cut].reshape(-1, quarter).astype(F32)
        shaped = (zr * gr - zi * gi, zr * gi + zi * gr)
        rc, ic, rs, si = turn(shaped, inner[rho, 2], inner[rho, 3])
        backs.append((rc - si, ic + rs))
    mixes = butterflies(backs, 1)
    scale = 1.0 / (block * block)
    half = last.shape[0] // 2
    copies[-1].wait()
    for q, (real, imag) in enumerate(mixes):
        cut = slice(q * quarter, (q + 1) * quarter)
        cosine, sine = twist[0, :, cut], twist[1, :, cut]
        pair = jnp.concatenate(
            [
                (real * cosine - imag * sine).astype(BF16),
                (imag * cosine + real * sine).astype(BF16),
            ],
            axis=0,
        )
        out = jnp.dot(last[...], pair, preferred_element_type=F32) * scale
        send[:, :, cut] = out[:half].astype(BF16).reshape(send.shape[0], send.shape[1], quarter)
        keep[:, :, cut] = out[half:].reshape(keep.shape[0], keep.shape[1], quarter)


def transform(place, pieces, spec, tables):
    members, rows_half, block = pieces[0].shape
    held = [tables[n] for n in ("first", "turns", "inner", "last")]
    first, turns, inner, last = held
    out = (2 * members, rows_half, block)
    operands = [*pieces, spec, *held]
    return pl.pallas_call(
        transform_kernel,
        in_specs=[SMEM] + [ANY] * len(operands),
        out_specs=[VMEM, VMEM],
        out_shape=[jax.ShapeDtypeStruct(out, BF16), jax.ShapeDtypeStruct(out, F32)],
        scratch_shapes=[
            pltpu.VMEM((4 * members, rows_half, block), BF16),
            pltpu.VMEM(spec.shape, BF16),
            pltpu.VMEM(first.shape[1:], BF16),
            pltpu.VMEM(turns.shape[1:], F32),
            pltpu.VMEM(inner.shape, BF16),
            pltpu.VMEM(last.shape[1:], BF16),
            pltpu.VMEM((2, turns.shape[3], block), F32),
            pltpu.SemaphoreType.DMA((9,)),
        ],
        compiler_params=pltpu.CompilerParams(vmem_limit_bytes=60 * MIB),
        cost_estimate=SMALL,
    )(place, *operands)


def gate_kernel(core_ref, conv, prod, gate, gate_other, skip, skip_other, weight, keep, send):
    _, channels, rows, block = conv.shape
    core = core_ref[0]
    here = channels // 2
    pieces = []
    for side, (values, gains) in enumerate(((gate, skip), (gate_other, skip_other))):
        for n in range(here):
            c = jnp.bitwise_xor(core, side) * here + n
            total = conv[0, c].astype(F32) + conv[1, c].astype(F32)
            total = total + gains[n] * prod[c].astype(F32)
            pieces.append((values[n].astype(F32) * total).astype(BF16))
    gated = jnp.concatenate(pieces, axis=0)
    mixed = jnp.dot(weight[...], gated, preferred_element_type=F32)
    outs = keep.shape[0]
    for r in range(rows):
        cut = slice(r * block, (r + 1) * block)
        keep[:, cut] = mixed[r * outs : (r + 1) * outs].astype(BF16)
        send[:, cut] = mixed[(rows + r) * outs : (rows + r + 1) * outs].astype(BF16)


def gate_and_project(core, conv, prod, gate, gate_other, skip, skip_other, weight):
    _, channels, rows, block = conv.shape
    outs = weight.shape[0] // (2 * rows)
    return pl.pallas_call(
        gate_kernel,
        out_shape=[jax.ShapeDtypeStruct((outs, rows * block), BF16)] * 2,
        in_specs=[SMEM, VMEM, VMEM, VMEM, VMEM, SMEM, SMEM, VMEM],
        out_specs=[VMEM, VMEM],
        compiler_params=pltpu.CompilerParams(vmem_limit_bytes=16 * MIB),
        cost_estimate=SMALL,
    )(core, conv, prod, gate, gate_other, skip, skip_other, weight)


def local_channels(k_feature, v_feature, q_feature, spectrum, skip_gain, out_weight):
    channels, tokens = k_feature.shape
    block = spectrum.shape[3]
    ctx_count = lax.axis_size("ctx")
    members = ctx_count // 2
    rows_half = tokens // block // 2
    a_half = spectrum.shape[2] // 2
    ctx, tp = lax.axis_index("ctx"), lax.axis_index("tp")
    core = tp.astype(jnp.int32).reshape(1)
    member = (ctx % members).astype(jnp.int32).reshape(1)
    place = (ctx // members * 2 + tp).astype(jnp.int32).reshape(1)
    tables = {
        name: jnp.asarray(table)
        for name, table in constant_tables(block, members, rows_half, a_half).items()
    }
    halves = [list(range(members)), list(range(members, 2 * members))]
    spread = lambda x: lax.all_to_all(x, "ctx", 0, 0, axis_index_groups=halves, tiled=True)
    across = lambda x: lax.ppermute(
        x, "ctx", [(d, (d + members) % ctx_count) for d in range(ctx_count)]
    )
    swap = lambda x: lax.ppermute(x, "tp", [(0, 1), (1, 0)])

    def joined(own, sent):
        start = ((1 - tp) * channels,) + (0,) * (own.ndim - 1)
        return lax.dynamic_update_slice(own, swap(sent), start)

    own, sent, other_rows = as_rows(core, block, k_feature, v_feature, spectrum=spectrum)
    sent, q_feature = lax.optimization_barrier((sent, q_feature))
    product = joined(own, sent)
    gate, gate_sent = as_rows(core, block, q_feature)
    product, spectrum, other_rows, gate, gate_sent, skip_gain, out_weight = (
        lax.optimization_barrier(
            (product, spectrum, other_rows, gate, gate_sent, skip_gain, out_weight)
        )
    )
    came_rows = swap(other_rows)
    gate_other = swap(gate_sent)
    skip_other = swap(skip_gain)
    xa = spread(product)
    spec = arrange_spectrum(core, spectrum, came_rows, tables["order"])
    weight = projection(core, out_weight, rows_half)
    xa, spec, gate_other, skip_other, weight = lax.optimization_barrier(
        (xa, spec, gate_other, skip_other, weight)
    )
    xb = swap(xa)
    za = across(xa)
    spec = spread(spec)
    zb = swap(za)


    send, keep = transform(place, (xa, xb, za, zb), spec, tables)
    total = (keep + swap(send).astype(F32)).astype(BF16)
    conv = lax.all_to_all(total, "ctx", 0, 0, tiled=True).reshape(2, members, rows_half, block)
    kept, sent = gate_and_project(
        core, conv, product, gate, gate_other, skip_gain, skip_other, weight
    )
    came = swap(sent)
    low = jnp.where(tp == 0, kept, came)
    high = jnp.where(tp == 0, came, kept)
    return jnp.concatenate([low, high], axis=1)


def local(k_feature, v_feature, q_feature, spectrum, skip_gain, out_weight):
    channels, tokens = k_feature.shape
    block = spectrum.shape[3]
    ctx_count, tp_count = lax.axis_size("ctx"), lax.axis_size("tp")
    by_channels = (
        tp_count == 2
        and ctx_count == 2 * channels * tp_count
        and tokens * ctx_count * 2 == block * block
        and tokens % (32 * block) == 0
        and spectrum.shape[2] % 32 == 0
        and block % 512 == 0
        and out_weight.shape[1] % 16 == 0
    )
    plan = local_channels if by_channels else local_general
    return plan(k_feature, v_feature, q_feature, spectrum, skip_gain, out_weight)


def solution(mesh):
    placed = (
        P("tp", "ctx"),
        P("tp", "ctx"),
        P("tp", "ctx"),
        P(None, "tp", "ctx", None),
        P("tp"),
        P(),
    )
    return jax.shard_map(
        local, mesh=mesh, in_specs=placed, out_specs=P("tp", "ctx"), check_vma=False
    )
```

```python
import functools
import math

import numpy as np
import ml_dtypes
import jax
import jax.numpy as jnp
from jax import lax
from jax.experimental import pallas as pl
from jax.experimental.pallas import tpu as pltpu
from jax.sharding import PartitionSpec as P

F32 = jnp.float32
BF16 = jnp.bfloat16
VMEM = pl.BlockSpec(memory_space=pltpu.VMEM)
SMEM = pl.BlockSpec(memory_space=pltpu.SMEM)
ANY = pl.BlockSpec(memory_space=pltpu.HBM)
ANYWHERE = pl.BlockSpec(memory_space=pl.ANY)
MIB = 1 << 20
SMALL = pl.CostEstimate(flops=1, bytes_accessed=1, transcendentals=0)


def fourier_tables(length_all):
    positions = jnp.arange(length_all, dtype=jnp.int32)
    phase_index = positions[:, None] * positions[None, :] % length_all
    angles = phase_index.astype(jnp.float32) * (2.0 * math.pi / length_all)
    return (jnp.cos(angles).astype(jnp.bfloat16), jnp.sin(angles).astype(jnp.bfloat16))


def twist_tables(left_index, right_index, length_all):
    phase_index = left_index[:, None] * right_index[None, :] % length_all
    angles = phase_index.astype(jnp.float32) * (2.0 * math.pi / length_all)
    return (jnp.cos(angles), jnp.sin(angles))


def contract(form, left, right):
    return jnp.einsum(form, left, right, preferred_element_type=jnp.float32)


def local_general(k_feature, v_feature, q_feature, spectrum, skip_gain, out_weight):
    channels, tokens = k_feature.shape
    block_order = spectrum.shape[3]
    length_all = block_order * block_order
    ctx_count = lax.axis_size("ctx")
    slab_width = block_order // ctx_count
    rows_here = tokens // block_order
    ctx_index = lax.axis_index("ctx")
    product = (k_feature.astype(jnp.float32) * v_feature.astype(jnp.float32)).astype(jnp.bfloat16)
    cosine_full, sine_full = fourier_tables(block_order)
    cosine_half = cosine_full[: block_order // 2]
    sine_half = sine_full[: block_order // 2]
    positions = jnp.arange(block_order, dtype=jnp.int32)
    local_ticks = ctx_index * slab_width + jnp.arange(slab_width, dtype=jnp.int32)
    grid_rows = lax.all_to_all(
        product.reshape(channels, rows_here, block_order),
        "ctx",
        split_axis=2,
        concat_axis=1,
        tiled=True,
    )
    first_real = contract("cij,ia->caj", grid_rows, cosine_half)
    first_imag = -contract("cij,ia->caj", grid_rows, sine_half)
    twist_cosine, twist_sine = twist_tables(positions, local_ticks, length_all)
    spread_real = (first_real * twist_cosine + first_imag * twist_sine).astype(jnp.bfloat16)
    spread_imag = (first_imag * twist_cosine - first_real * twist_sine).astype(jnp.bfloat16)
    block_real, block_imag = (
        lax.all_to_all(spread_real, "ctx", split_axis=1, concat_axis=2, tiled=True),
        lax.all_to_all(spread_imag, "ctx", split_axis=1, concat_axis=2, tiled=True),
    )
    freq_real = contract("caj,jb->cab", block_real, cosine_full) + contract(
        "caj,jb->cab", block_imag, sine_full
    )
    freq_imag = contract("caj,jb->cab", block_imag, cosine_full) - contract(
        "caj,jb->cab", block_real, sine_full
    )
    resp_real = spectrum[0].astype(jnp.float32)
    resp_imag = spectrum[1].astype(jnp.float32)
    shaped_real = (freq_real * resp_real - freq_imag * resp_imag).astype(jnp.bfloat16)
    shaped_imag = (freq_real * resp_imag + freq_imag * resp_real).astype(jnp.bfloat16)
    inner_real = contract("cab,bj->caj", shaped_real, cosine_full) - contract(
        "cab,bj->caj", shaped_imag, sine_full
    )
    inner_imag = contract("cab,bj->caj", shaped_imag, cosine_full) + contract(
        "cab,bj->caj", shaped_real, sine_full
    )
    twist_cosine, twist_sine = twist_tables(local_ticks, positions, length_all)
    back_real = (inner_real * twist_cosine - inner_imag * twist_sine).astype(jnp.bfloat16)
    back_imag = (inner_imag * twist_cosine + inner_real * twist_sine).astype(jnp.bfloat16)
    summed = contract(
        "ia,caj->cij",
        cosine_half,
        lax.all_to_all(back_real, "ctx", split_axis=2, concat_axis=1, tiled=True),
    ) - contract(
        "ia,caj->cij",
        sine_half,
        lax.all_to_all(back_imag, "ctx", split_axis=2, concat_axis=1, tiled=True),
    )
    spatial = (summed * (1.0 / length_all)).astype(jnp.bfloat16)
    convolved = lax.all_to_all(spatial, "ctx", split_axis=1, concat_axis=2, tiled=True).reshape(
        channels, tokens
    )
    gated_rows = (
        q_feature.astype(jnp.float32)
        * (convolved.astype(jnp.float32) + skip_gain[:, None] * product.astype(jnp.float32))
    ).astype(jnp.bfloat16)
    tp_index = lax.axis_index("tp")
    my_weight = lax.dynamic_slice_in_dim(out_weight, tp_index * channels, channels, 0)
    return lax.psum_scatter(
        jnp.dot(my_weight.T, gated_rows, preferred_element_type=jnp.float32).astype(jnp.bfloat16),
        "tp",
        scatter_dimension=0,
        tiled=True,
    )


def cosine_sine(product, length):
    angles = (product % length).astype(np.float64) * (2.0 * np.pi / length)
    return np.cos(angles), np.sin(angles)


@functools.lru_cache(maxsize=None)
def constant_tables(block, members, rows_half, a_half):
    quarter = block // 4
    firsts, lasts, coarses, fines = [], [], [], []
    part = np.arange(members)
    for g in range(2):
        for s in range(2):
            a = (
                (g * members + part)[:, None] * 2 * a_half
                + s * a_half
                + np.arange(a_half)[None, :]
            ).reshape(-1)

            def rows(group, core):
                device = group * members + part
                i = device[:, None] * 2 * rows_half + core * rows_half
                return (i + np.arange(rows_half)[None, :]).reshape(-1)

            i_in = np.concatenate([rows(g, s), rows(g, 1 - s), rows(1 - g, s), rows(1 - g, 1 - s)])
            cosine, sine = cosine_sine(a[:, None] * i_in[None, :], block)
            firsts.append(np.concatenate([cosine, -sine], 0))
            i_out = np.concatenate([rows(0, 1 - s), rows(1, 1 - s), rows(0, s), rows(1, s)])
            cosine, sine = cosine_sine(i_out[:, None] * a[None, :], block)
            lasts.append(np.concatenate([cosine, -sine], 1))
            coarse = 128 * (np.arange(128) % (block // 128))
            coarses.append(np.stack(cosine_sine(a[:, None] * coarse[None, :], block * block)))
            fines.append(np.stack(cosine_sine(a[:, None] * np.arange(128)[None, :], block * block)))
    inner = []
    for rho in range(4):
        cosine, sine = cosine_sine(
            np.arange(quarter)[:, None] * (4 * np.arange(quarter) + rho)[None, :], block
        )
        inner.append(np.stack([cosine, sine, cosine.T, sine.T]))
    order = np.zeros((quarter, quarter), np.float32)
    b = np.arange(quarter)
    order[b, (b % 4) * (quarter // 4) + b // 4] = 1.0
    narrow = lambda x: np.asarray(x, np.float32).astype(ml_dtypes.bfloat16)
    rest = np.stack([coarses, fines], 1).astype(np.float32)
    turns = []
    for _ in range(3):
        turns.append(narrow(rest))
        rest = rest - turns[-1].astype(np.float32)
    turns = np.stack(turns + [np.zeros_like(turns[0])], 1).transpose(0, 2, 4, 1, 3, 5)
    turns = turns.reshape(4, 2 * turns.shape[2], 2, 2 * quarter).transpose(0, 2, 1, 3)
    square = (-1, 2 * quarter, 2 * quarter)
    entries = [np.stack(firsts), np.stack(lasts), np.stack(inner).reshape(square)]
    return dict(
        transform=np.concatenate([narrow(x) for x in entries] + [turns.reshape(square)]),
        order=narrow(order),
    )


def product_kernel(block, count, core_ref, *refs):
    ins, outs, scratch, sem = refs[:count], refs[count:-1 - count], refs[-1 - count : -1], refs[-1]
    copies = [pltpu.make_async_copy(ins[n], scratch[n], sem.at[n]) for n in range(count)]
    for copy in copies:
        copy.start()
    rows_copy = None
    if len(outs) == 4:
        spectrum, own, send, other_rows = outs
        a_half = other_rows.shape[2]
        at = pl.ds(pl.multiple_of((1 - core_ref[0]) * a_half, a_half), a_half)
        rows_copy = pltpu.make_async_copy(spectrum.at[:, :, at, :], other_rows, sem.at[count])
        rows_copy.start()
    else:
        own, send = outs
    core = core_ref[0]
    channels, tokens = ins[0].shape
    place = 0 if own.shape[0] == channels else channels * core
    rows = tokens // block
    half = rows // 2
    to = lax.broadcasted_iota(jnp.int32, (channels * rows, channels * rows), 0)
    at = lax.broadcasted_iota(jnp.int32, (channels * rows, channels * rows), 1)
    side = jnp.bitwise_xor(to // (channels * half), core)
    source = (side * half + to % half) * channels + (to // half) % channels
    order = jnp.where(at == source, 1.0, 0.0).astype(BF16)
    for copy in copies:
        copy.wait()
    pieces = []
    for i in range(rows):
        cut = slice(i * block, (i + 1) * block)
        piece = scratch[0][:, cut].astype(F32)
        for other in scratch[1:]:
            piece = piece * other[:, cut].astype(F32)
        pieces.append(piece)
    stacked = jnp.concatenate(pieces, axis=0).astype(BF16)
    ordered = jnp.dot(order, stacked, preferred_element_type=F32).astype(BF16)
    ordered = ordered.reshape(2, channels, half, block)
    own[pl.ds(place, channels)] = ordered[0]
    send[...] = ordered[1]
    if rows_copy is not None:
        rows_copy.wait()


def as_rows(core, block, *arrays, spectrum=None):
    channels, tokens = arrays[0].shape
    half = tokens // block // 2
    room, extra, shapes = 1, [], []
    if spectrum is not None:
        two, _, a_here, _ = spectrum.shape
        room, extra = 2, [spectrum]
        shapes = [jax.ShapeDtypeStruct((two, channels, a_here // 2, block), BF16)]
    return pl.pallas_call(
        functools.partial(product_kernel, block, len(arrays)),
        out_shape=[
            jax.ShapeDtypeStruct((room * channels, half, block), BF16),
            jax.ShapeDtypeStruct((channels, half, block), BF16),
        ]
        + shapes,
        in_specs=[SMEM] + [ANY] * len(arrays + tuple(extra)),
        out_specs=[VMEM] * (2 + len(shapes)),
        scratch_shapes=[pltpu.VMEM((channels, tokens), BF16)] * len(arrays)
        + [pltpu.SemaphoreType.DMA((len(arrays) + 1,))],
        cost_estimate=SMALL,
    )(core, *arrays, *extra)


def spectrum_kernel(core_ref, in_ref, came_ref, order_ref, *refs):
    moved, rows, came, order, sem = refs
    core = core_ref[0]
    two, channels, a_half, block = rows.shape
    at = pl.ds(pl.multiple_of(core * a_half, a_half), a_half)
    copies = [
        pltpu.make_async_copy(order_ref, order, sem.at[0]),
        pltpu.make_async_copy(in_ref.at[:, :, at, :], rows, sem.at[1]),
        pltpu.make_async_copy(came_ref, came, sem.at[2]),
    ]
    for copy in copies:
        copy.start()
    copies[0].wait()
    quarter = block // 4
    step = quarter // 4
    for side, ref in ((core, rows), (1 - core, came)):
        copies[1 if ref is rows else 2].wait()
        flat = jnp.concatenate([ref[n, c] for c in range(channels) for n in range(two)], 0)
        parts = [
            jnp.dot(flat[:, q * quarter : (q + 1) * quarter], order[...], preferred_element_type=F32)
            for q in range(4)
        ]
        for rho in range(4):
            columns = [part[:, rho * step : (rho + 1) * step] for part in parts]
            columns = jnp.concatenate(columns, axis=1).astype(BF16)
            moved[pl.ds(channels * side, channels), :, :, rho * quarter : (rho + 1) * quarter] = (
                columns.reshape(channels, two, a_half, quarter)
            )


def arrange_spectrum(core, spectrum, came, order):
    two, channels, a_half, block = came.shape
    return pl.pallas_call(
        spectrum_kernel,
        out_shape=jax.ShapeDtypeStruct((2 * channels, two, a_half, block), BF16),
        in_specs=[SMEM, ANY, ANY, ANY],
        out_specs=VMEM,
        scratch_shapes=[
            pltpu.VMEM(came.shape, BF16),
            pltpu.VMEM(came.shape, BF16),
            pltpu.VMEM(order.shape, BF16),
            pltpu.SemaphoreType.DMA((3,)),
        ],
        cost_estimate=SMALL,
    )(core, spectrum, came, order)


def weight_kernel(rows, core_ref, weight, out):
    channels, outs = weight.shape
    half = outs // 2
    core = core_ref[0]
    shape = out.shape
    to = lax.broadcasted_iota(jnp.int32, (shape[0], outs), 0)
    at = lax.broadcasted_iota(jnp.int32, (shape[0], outs), 1)
    column = jnp.bitwise_xor(to // (rows * half), core) * half + to % half
    pick = jnp.where(at == column, 1.0, 0.0).astype(BF16)
    turned = lax.dot_general(
        pick, weight[...], (((1,), (1,)), ((), ())), preferred_element_type=F32
    ).astype(BF16)
    to = lax.broadcasted_iota(jnp.int32, (channels, shape[1]), 0)
    at = lax.broadcasted_iota(jnp.int32, (channels, shape[1]), 1)
    channel = (at // rows + core * (channels // 2)) % channels
    widen = jnp.where(channel == to, 1.0, 0.0).astype(BF16)
    wide = jnp.dot(turned, widen, preferred_element_type=F32)
    to = lax.broadcasted_iota(jnp.int32, shape, 0)
    at = lax.broadcasted_iota(jnp.int32, shape, 1)
    out[...] = jnp.where(at % rows == (to // half) % rows, wide, 0.0).astype(BF16)


def projection(core, weight, rows):
    channels, outs = weight.shape
    return pl.pallas_call(
        functools.partial(weight_kernel, rows),
        out_shape=jax.ShapeDtypeStruct((rows * outs, rows * channels), BF16),
        in_specs=[SMEM, VMEM],
        out_specs=VMEM,
        compiler_params=pltpu.CompilerParams(vmem_limit_bytes=4 * MIB),
    )(core, weight)


def butterflies(values, sign):
    (r0, i0), (r1, i1), (r2, i2), (r3, i3) = values
    er, ei, dr, di = r0 + r2, i0 + i2, r0 - r2, i0 - i2
    fr, fi, hr, hi = r1 + r3, i1 + i3, r1 - r3, i1 - i3
    plus, minus = (dr - hi, di + hr), (dr + hi, di - hr)
    if sign < 0:
        plus, minus = minus, plus
    return [(er + fr, ei + fi), plus, (er - fr, ei - fi), minus]


def turn(values, cosine, sine):
    real, imag = values
    rows = real.shape[0]
    both = jnp.concatenate([real.astype(BF16), imag.astype(BF16)], axis=0)
    with_cosine = jnp.dot(both, cosine, preferred_element_type=F32)
    with_sine = jnp.dot(both, sine, preferred_element_type=F32)
    return with_cosine[:rows], with_cosine[rows:], with_sine[:rows], with_sine[rows:]


def full_turns(turns, rows):
    def whole(kind, which):
        cut = slice(kind * rows, (kind + 1) * rows)
        part = lambda n: turns[n // 2, cut, pl.ds((2 * (n % 2) + which) * 128, 128)].astype(F32)
        return part(0) + part(1) + part(2)

    return (whole(0, 0), whole(0, 1)), (whole(1, 0), whole(1, 1))


def pair_of(inner, rho, way):
    quarter = inner.shape[-1] // 2
    four = inner[rho].reshape(4, quarter, quarter)
    return four[2 * way], four[2 * way + 1]


def transform_kernel(place_ref, *refs):
    ins, (send, keep, signal, spec, first, last, inner, turns, twist, sem) = refs[:-10], refs[-10:]
    *pieces, spec_in, table = ins
    place = place_ref[0]
    count = pieces[0].shape[0]
    size = turns.shape[0]
    moves = [(table.at[place], first)]
    moves += [(ref, signal.at[pl.ds(n * count, count)]) for n, ref in enumerate(pieces)]
    moves += [(table.at[pl.ds(12 + size * place, size)], turns)]
    moves += [(table.at[pl.ds(8, 4)], inner), (spec_in, spec), (table.at[4 + place], last)]
    copies = [pltpu.make_async_copy(*move, sem.at[n]) for n, move in enumerate(moves)]
    for copy in copies:
        copy.start()
    for copy in copies[:6]:
        copy.wait()
    block = signal.shape[-1]
    quarter = block // 4
    lines = signal[...].reshape(-1, block)
    a_rows = first.shape[0] // 2
    coarse, fine = full_turns(turns, a_rows)
    turned = []
    for q in range(4):
        cut = slice(q * quarter, (q + 1) * quarter)
        both = jnp.dot(first[...], lines[:, cut], preferred_element_type=F32)
        for h in range(q * quarter // 128, (q + 1) * quarter // 128):
            lanes = slice(128 * h, 128 * (h + 1))
            uc, us = coarse[0][:, h : h + 1], coarse[1][:, h : h + 1]
            twist[0, :, lanes] = uc * fine[0] - us * fine[1]
            twist[1, :, lanes] = us * fine[0] + uc * fine[1]
        real, imag = both[:a_rows], both[a_rows:]
        cosine, sine = twist[0, :, cut], twist[1, :, cut]
        turned.append((real * cosine + imag * sine, imag * cosine - real * sine))
    mixes = butterflies(turned, -1)
    for copy in copies[6:-1]:
        copy.wait()
    backs = []
    for rho in range(4):
        rc, ic, rs, si = turn(mixes[rho], *pair_of(inner, rho, 0))
        zr, zi = rc + si, ic - rs
        cut = slice(rho * quarter, (rho + 1) * quarter)
        gr = spec[:, 0, :, cut].reshape(-1, quarter).astype(F32)
        gi = spec[:, 1, :, cut].reshape(-1, quarter).astype(F32)
        shaped = (zr * gr - zi * gi, zr * gi + zi * gr)
        rc, ic, rs, si = turn(shaped, *pair_of(inner, rho, 1))
        backs.append((rc - si, ic + rs))
    mixes = butterflies(backs, 1)
    scale = 1.0 / (block * block)
    half = last.shape[0] // 2
    copies[-1].wait()
    for q, (real, imag) in enumerate(mixes):
        cut = slice(q * quarter, (q + 1) * quarter)
        cosine, sine = twist[0, :, cut], twist[1, :, cut]
        pair = jnp.concatenate(
            [
                (real * cosine - imag * sine).astype(BF16),
                (imag * cosine + real * sine).astype(BF16),
            ],
            axis=0,
        )
        out = jnp.dot(last[...], pair, preferred_element_type=F32) * scale
        send[:, :, cut] = out[:half].astype(BF16).reshape(send.shape[0], send.shape[1], quarter)
        keep[:, :, cut] = out[half:].astype(BF16).reshape(keep.shape[0], keep.shape[1], quarter)


def transform(place, pieces, spec, table):
    members, rows_half, block = pieces[0].shape
    a_rows = spec.shape[0] * spec.shape[2]
    out = (2 * members, rows_half, block)
    square = table.shape[1:]
    return pl.pallas_call(
        transform_kernel,
        in_specs=[SMEM] + [ANYWHERE] * (len(pieces) + 1) + [ANY],
        out_specs=[VMEM, VMEM],
        out_shape=[jax.ShapeDtypeStruct(out, BF16)] * 2,
        scratch_shapes=[
            pltpu.VMEM((4 * members, rows_half, block), BF16),
            pltpu.VMEM(spec.shape, BF16),
            pltpu.VMEM(square, BF16),
            pltpu.VMEM(square, BF16),
            pltpu.VMEM((4,) + square, BF16),
            pltpu.VMEM(((table.shape[0] - 12) // 4,) + square, BF16),
            pltpu.VMEM((2, a_rows, block), F32),
            pltpu.SemaphoreType.DMA((len(pieces) + 5,)),
        ],
        compiler_params=pltpu.CompilerParams(vmem_limit_bytes=48 * MIB),
        cost_estimate=SMALL,
    )(place, *pieces, spec, table)


def gate_kernel(core_ref, conv, prod, gate, gate_other, skip, skip_other, weight, keep, send):
    _, channels, rows, block = conv.shape
    core = core_ref[0]
    here = channels // 2
    pieces = []
    for side, (values, gains) in enumerate(((gate, skip), (gate_other, skip_other))):
        for n in range(here):
            c = jnp.bitwise_xor(core, side) * here + n
            total = conv[0, c].astype(F32) + conv[1, c].astype(F32)
            total = total + gains[n] * prod[c].astype(F32)
            pieces.append((values[n].astype(F32) * total).astype(BF16))
    gated = jnp.concatenate(pieces, axis=0)
    mixed = jnp.dot(weight[...], gated, preferred_element_type=F32)
    outs = keep.shape[0]
    for r in range(rows):
        cut = slice(r * block, (r + 1) * block)
        keep[:, cut] = mixed[r * outs : (r + 1) * outs].astype(BF16)
        send[:, cut] = mixed[(rows + r) * outs : (rows + r + 1) * outs].astype(BF16)


def gate_and_project(core, conv, prod, gate, gate_other, skip, skip_other, weight):
    _, channels, rows, block = conv.shape
    outs = weight.shape[0] // (2 * rows)
    return pl.pallas_call(
        gate_kernel,
        out_shape=[jax.ShapeDtypeStruct((outs, rows * block), BF16)] * 2,
        in_specs=[SMEM, VMEM, VMEM, VMEM, VMEM, SMEM, SMEM, VMEM],
        out_specs=[VMEM, VMEM],
        compiler_params=pltpu.CompilerParams(vmem_limit_bytes=16 * MIB),
        cost_estimate=SMALL,
    )(core, conv, prod, gate, gate_other, skip, skip_other, weight)


def local_channels(k_feature, v_feature, q_feature, spectrum, skip_gain, out_weight):
    channels, tokens = k_feature.shape
    block = spectrum.shape[3]
    ctx_count = lax.axis_size("ctx")
    members = ctx_count // 2
    rows_half = tokens // block // 2
    a_half = spectrum.shape[2] // 2
    ctx, tp = lax.axis_index("ctx"), lax.axis_index("tp")
    core = tp.astype(jnp.int32).reshape(1)
    member = (ctx % members).astype(jnp.int32).reshape(1)
    place = (ctx // members * 2 + tp).astype(jnp.int32).reshape(1)
    tables = {
        name: jnp.asarray(table)
        for name, table in constant_tables(block, members, rows_half, a_half).items()
    }
    halves = [list(range(members)), list(range(members, 2 * members))]
    spread = lambda x: lax.all_to_all(x, "ctx", 0, 0, axis_index_groups=halves, tiled=True)
    across = lambda x: lax.ppermute(
        x, "ctx", [(d, (d + members) % ctx_count) for d in range(ctx_count)]
    )
    swap = lambda x: lax.ppermute(x, "tp", [(0, 1), (1, 0)])

    def joined(own, sent):
        start = ((1 - tp) * channels,) + (0,) * (own.ndim - 1)
        return lax.dynamic_update_slice(own, swap(sent), start)

    own, sent, other_rows = as_rows(core, block, k_feature, v_feature, spectrum=spectrum)
    sent, q_feature = lax.optimization_barrier((sent, q_feature))
    product = joined(own, sent)
    gate, gate_sent = as_rows(core, block, q_feature)
    product, spectrum, other_rows, gate, gate_sent, skip_gain, out_weight = (
        lax.optimization_barrier(
            (product, spectrum, other_rows, gate, gate_sent, skip_gain, out_weight)
        )
    )
    came_rows = swap(other_rows)
    gate_other = swap(gate_sent)
    skip_other = swap(skip_gain)
    xa = spread(product)
    spec = arrange_spectrum(core, spectrum, came_rows, tables["order"])
    weight = projection(core, out_weight, rows_half)
    xa, spec, gate_other, skip_other, weight = lax.optimization_barrier(
        (xa, spec, gate_other, skip_other, weight)
    )
    xb = swap(xa)
    za = across(xa)
    spec = spread(spec)
    zb = swap(za)


    send, keep = transform(place, (xa, xb, za, zb), spec, tables["transform"])
    total = (keep.astype(F32) + swap(send).astype(F32)).astype(BF16)
    conv = lax.all_to_all(total, "ctx", 0, 0, tiled=True).reshape(2, members, rows_half, block)
    kept, sent = gate_and_project(
        core, conv, product, gate, gate_other, skip_gain, skip_other, weight
    )
    came = swap(sent)
    low = jnp.where(tp == 0, kept, came)
    high = jnp.where(tp == 0, came, kept)
    return jnp.concatenate([low, high], axis=1)


def local(k_feature, v_feature, q_feature, spectrum, skip_gain, out_weight):
    channels, tokens = k_feature.shape
    block = spectrum.shape[3]
    ctx_count, tp_count = lax.axis_size("ctx"), lax.axis_size("tp")
    by_channels = (
        tp_count == 2
        and ctx_count == 2 * channels * tp_count
        and tokens * ctx_count * 2 == block * block
        and tokens % (32 * block) == 0
        and spectrum.shape[2] % 32 == 0
        and block % 512 == 0
        and out_weight.shape[1] % 16 == 0
    )
    plan = local_channels if by_channels else local_general
    return plan(k_feature, v_feature, q_feature, spectrum, skip_gain, out_weight)


def solution(mesh):
    placed = (
        P("tp", "ctx"),
        P("tp", "ctx"),
        P("tp", "ctx"),
        P(None, "tp", "ctx", None),
        P("tp"),
        P(),
    )
    return jax.shard_map(
        local, mesh=mesh, in_specs=placed, out_specs=P("tp", "ctx"), check_vma=False
    )
```

```python
import functools
import math

import numpy as np
import ml_dtypes
import jax
import jax.numpy as jnp
from jax import lax
from jax.experimental import pallas as pl
from jax.experimental.pallas import tpu as pltpu
from jax.sharding import PartitionSpec as P

F32 = jnp.float32
BF16 = jnp.bfloat16
VMEM = pl.BlockSpec(memory_space=pltpu.VMEM)
SMEM = pl.BlockSpec(memory_space=pltpu.SMEM)
ANY = pl.BlockSpec(memory_space=pltpu.HBM)
ANYWHERE = pl.BlockSpec(memory_space=pl.ANY)
MIB = 1 << 20
SMALL = pl.CostEstimate(flops=1, bytes_accessed=1, transcendentals=0)


def fourier_tables(length_all):
    positions = jnp.arange(length_all, dtype=jnp.int32)
    phase_index = positions[:, None] * positions[None, :] % length_all
    angles = phase_index.astype(jnp.float32) * (2.0 * math.pi / length_all)
    return (jnp.cos(angles).astype(jnp.bfloat16), jnp.sin(angles).astype(jnp.bfloat16))


def twist_tables(left_index, right_index, length_all):
    phase_index = left_index[:, None] * right_index[None, :] % length_all
    angles = phase_index.astype(jnp.float32) * (2.0 * math.pi / length_all)
    return (jnp.cos(angles), jnp.sin(angles))


def contract(form, left, right):
    return jnp.einsum(form, left, right, preferred_element_type=jnp.float32)


def local_general(k_feature, v_feature, q_feature, spectrum, skip_gain, out_weight):
    channels, tokens = k_feature.shape
    block_order = spectrum.shape[3]
    length_all = block_order * block_order
    ctx_count = lax.axis_size("ctx")
    slab_width = block_order // ctx_count
    rows_here = tokens // block_order
    ctx_index = lax.axis_index("ctx")
    product = (k_feature.astype(jnp.float32) * v_feature.astype(jnp.float32)).astype(jnp.bfloat16)
    cosine_full, sine_full = fourier_tables(block_order)
    cosine_half = cosine_full[: block_order // 2]
    sine_half = sine_full[: block_order // 2]
    positions = jnp.arange(block_order, dtype=jnp.int32)
    local_ticks = ctx_index * slab_width + jnp.arange(slab_width, dtype=jnp.int32)
    grid_rows = lax.all_to_all(
        product.reshape(channels, rows_here, block_order),
        "ctx",
        split_axis=2,
        concat_axis=1,
        tiled=True,
    )
    first_real = contract("cij,ia->caj", grid_rows, cosine_half)
    first_imag = -contract("cij,ia->caj", grid_rows, sine_half)
    twist_cosine, twist_sine = twist_tables(positions, local_ticks, length_all)
    spread_real = (first_real * twist_cosine + first_imag * twist_sine).astype(jnp.bfloat16)
    spread_imag = (first_imag * twist_cosine - first_real * twist_sine).astype(jnp.bfloat16)
    block_real, block_imag = (
        lax.all_to_all(spread_real, "ctx", split_axis=1, concat_axis=2, tiled=True),
        lax.all_to_all(spread_imag, "ctx", split_axis=1, concat_axis=2, tiled=True),
    )
    freq_real = contract("caj,jb->cab", block_real, cosine_full) + contract(
        "caj,jb->cab", block_imag, sine_full
    )
    freq_imag = contract("caj,jb->cab", block_imag, cosine_full) - contract(
        "caj,jb->cab", block_real, sine_full
    )
    resp_real = spectrum[0].astype(jnp.float32)
    resp_imag = spectrum[1].astype(jnp.float32)
    shaped_real = (freq_real * resp_real - freq_imag * resp_imag).astype(jnp.bfloat16)
    shaped_imag = (freq_real * resp_imag + freq_imag * resp_real).astype(jnp.bfloat16)
    inner_real = contract("cab,bj->caj", shaped_real, cosine_full) - contract(
        "cab,bj->caj", shaped_imag, sine_full
    )
    inner_imag = contract("cab,bj->caj", shaped_imag, cosine_full) + contract(
        "cab,bj->caj", shaped_real, sine_full
    )
    twist_cosine, twist_sine = twist_tables(local_ticks, positions, length_all)
    back_real = (inner_real * twist_cosine - inner_imag * twist_sine).astype(jnp.bfloat16)
    back_imag = (inner_imag * twist_cosine + inner_real * twist_sine).astype(jnp.bfloat16)
    summed = contract(
        "ia,caj->cij",
        cosine_half,
        lax.all_to_all(back_real, "ctx", split_axis=2, concat_axis=1, tiled=True),
    ) - contract(
        "ia,caj->cij",
        sine_half,
        lax.all_to_all(back_imag, "ctx", split_axis=2, concat_axis=1, tiled=True),
    )
    spatial = (summed * (1.0 / length_all)).astype(jnp.bfloat16)
    convolved = lax.all_to_all(spatial, "ctx", split_axis=1, concat_axis=2, tiled=True).reshape(
        channels, tokens
    )
    gated_rows = (
        q_feature.astype(jnp.float32)
        * (convolved.astype(jnp.float32) + skip_gain[:, None] * product.astype(jnp.float32))
    ).astype(jnp.bfloat16)
    tp_index = lax.axis_index("tp")
    my_weight = lax.dynamic_slice_in_dim(out_weight, tp_index * channels, channels, 0)
    return lax.psum_scatter(
        jnp.dot(my_weight.T, gated_rows, preferred_element_type=jnp.float32).astype(jnp.bfloat16),
        "tp",
        scatter_dimension=0,
        tiled=True,
    )


def cosine_sine(product, length):
    angles = (product % length).astype(np.float64) * (2.0 * np.pi / length)
    return np.cos(angles), np.sin(angles)


@functools.lru_cache(maxsize=None)
def constant_tables(block, members, rows_half, a_half):
    quarter = block // 4
    firsts, lasts, coarses, fines = [], [], [], []
    part = np.arange(members)
    for g in range(2):
        for s in range(2):
            a = (
                (g * members + part)[:, None] * 2 * a_half
                + s * a_half
                + np.arange(a_half)[None, :]
            ).reshape(-1)

            def rows(group, core):
                device = group * members + part
                i = device[:, None] * 2 * rows_half + core * rows_half
                return (i + np.arange(rows_half)[None, :]).reshape(-1)

            i_in = np.concatenate([rows(g, s), rows(g, 1 - s), rows(1 - g, s), rows(1 - g, 1 - s)])
            cosine, sine = cosine_sine(a[:, None] * i_in[None, :], block)
            firsts.append(np.concatenate([cosine, -sine], 0))
            i_out = np.concatenate([rows(0, 1 - s), rows(1, 1 - s), rows(0, s), rows(1, s)])
            cosine, sine = cosine_sine(i_out[:, None] * a[None, :], block)
            lasts.append(np.concatenate([cosine, -sine], 1))
            coarse = 128 * (np.arange(128) % (block // 128))
            coarses.append(np.stack(cosine_sine(a[:, None] * coarse[None, :], block * block)))
            fines.append(np.stack(cosine_sine(a[:, None] * np.arange(128)[None, :], block * block)))
    inner = []
    for rho in range(4):
        cosine, sine = cosine_sine(
            np.arange(quarter)[:, None] * (4 * np.arange(quarter) + rho)[None, :], block
        )
        inner.append(np.stack([cosine, sine, cosine.T, sine.T]))
    order = np.zeros((quarter, quarter), np.float32)
    b = np.arange(quarter)
    order[b, (b % 4) * (quarter // 4) + b // 4] = 1.0
    narrow = lambda x: np.asarray(x, np.float32).astype(ml_dtypes.bfloat16)
    rest = np.stack([coarses, fines], 1).astype(np.float32)
    turns = []
    for _ in range(3):
        turns.append(narrow(rest))
        rest = rest - turns[-1].astype(np.float32)
    turns = np.stack(turns + [np.zeros_like(turns[0])], 1).transpose(0, 2, 4, 1, 3, 5)
    turns = turns.reshape(4, 2 * turns.shape[2], 2, 2 * quarter).transpose(0, 2, 1, 3)
    square = (-1, 2 * quarter, 2 * quarter)
    entries = [np.stack(firsts), np.stack(lasts), np.stack(inner).reshape(square)]
    return dict(
        transform=np.concatenate([narrow(x) for x in entries] + [turns.reshape(square)]),
        order=narrow(order),
    )


def product_kernel(block, count, core_ref, *refs):
    ins, outs, scratch, sem = refs[:count], refs[count:-1 - count], refs[-1 - count : -1], refs[-1]
    copies = [pltpu.make_async_copy(ins[n], scratch[n], sem.at[n]) for n in range(count)]
    for copy in copies:
        copy.start()
    rows_copy = None
    if len(outs) == 4:
        spectrum, own, send, other_rows = outs
        a_half = other_rows.shape[2]
        at = pl.ds(pl.multiple_of((1 - core_ref[0]) * a_half, a_half), a_half)
        rows_copy = pltpu.make_async_copy(spectrum.at[:, :, at, :], other_rows, sem.at[count])
        rows_copy.start()
    else:
        own, send = outs
    core = core_ref[0]
    channels, tokens = ins[0].shape
    place = 0 if own.shape[0] == channels else channels * core
    rows = tokens // block
    half = rows // 2
    to = lax.broadcasted_iota(jnp.int32, (channels * rows, channels * rows), 0)
    at = lax.broadcasted_iota(jnp.int32, (channels * rows, channels * rows), 1)
    side = jnp.bitwise_xor(to // (channels * half), core)
    source = (side * half + to % half) * channels + (to // half) % channels
    order = jnp.where(at == source, 1.0, 0.0).astype(BF16)
    for copy in copies:
        copy.wait()
    pieces = []
    for i in range(rows):
        cut = slice(i * block, (i + 1) * block)
        piece = scratch[0][:, cut].astype(F32)
        for other in scratch[1:]:
            piece = piece * other[:, cut].astype(F32)
        pieces.append(piece)
    stacked = jnp.concatenate(pieces, axis=0).astype(BF16)
    ordered = jnp.dot(order, stacked, preferred_element_type=F32).astype(BF16)
    ordered = ordered.reshape(2, channels, half, block)
    own[pl.ds(place, channels)] = ordered[0]
    send[...] = ordered[1]
    if rows_copy is not None:
        rows_copy.wait()


def as_rows(core, block, *arrays, spectrum=None):
    channels, tokens = arrays[0].shape
    half = tokens // block // 2
    room, extra, shapes = 1, [], []
    if spectrum is not None:
        two, _, a_here, _ = spectrum.shape
        room, extra = 2, [spectrum]
        shapes = [jax.ShapeDtypeStruct((two, channels, a_here // 2, block), BF16)]
    return pl.pallas_call(
        functools.partial(product_kernel, block, len(arrays)),
        out_shape=[
            jax.ShapeDtypeStruct((room * channels, half, block), BF16),
            jax.ShapeDtypeStruct((channels, half, block), BF16),
        ]
        + shapes,
        in_specs=[SMEM] + [ANY] * len(arrays + tuple(extra)),
        out_specs=[VMEM] * (2 + len(shapes)),
        scratch_shapes=[pltpu.VMEM((channels, tokens), BF16)] * len(arrays)
        + [pltpu.SemaphoreType.DMA((len(arrays) + 1,))],
        cost_estimate=SMALL,
    )(core, *arrays, *extra)


def spectrum_kernel(core_ref, in_ref, came_ref, order_ref, *refs):
    moved, rows, came, order, sem = refs
    core = core_ref[0]
    two, channels, a_half, block = rows.shape
    at = pl.ds(pl.multiple_of(core * a_half, a_half), a_half)
    copies = [
        pltpu.make_async_copy(order_ref, order, sem.at[0]),
        pltpu.make_async_copy(in_ref.at[:, :, at, :], rows, sem.at[1]),
        pltpu.make_async_copy(came_ref, came, sem.at[2]),
    ]
    for copy in copies:
        copy.start()
    copies[0].wait()
    quarter = block // 4
    step = quarter // 4
    for side, ref in ((core, rows), (1 - core, came)):
        copies[1 if ref is rows else 2].wait()
        flat = jnp.concatenate([ref[n, c] for c in range(channels) for n in range(two)], 0)
        parts = [
            jnp.dot(flat[:, q * quarter : (q + 1) * quarter], order[...], preferred_element_type=F32)
            for q in range(4)
        ]
        for rho in range(4):
            columns = [part[:, rho * step : (rho + 1) * step] for part in parts]
            columns = jnp.concatenate(columns, axis=1).astype(BF16)
            moved[pl.ds(channels * side, channels), :, :, rho * quarter : (rho + 1) * quarter] = (
                columns.reshape(channels, two, a_half, quarter)
            )


def arrange_spectrum(core, spectrum, came, order):
    two, channels, a_half, block = came.shape
    return pl.pallas_call(
        spectrum_kernel,
        out_shape=jax.ShapeDtypeStruct((2 * channels, two, a_half, block), BF16),
        in_specs=[SMEM, ANY, ANY, ANY],
        out_specs=VMEM,
        scratch_shapes=[
            pltpu.VMEM(came.shape, BF16),
            pltpu.VMEM(came.shape, BF16),
            pltpu.VMEM(order.shape, BF16),
            pltpu.SemaphoreType.DMA((3,)),
        ],
        cost_estimate=SMALL,
    )(core, spectrum, came, order)


def weight_kernel(rows, core_ref, weight, out):
    channels, outs = weight.shape
    half = outs // 2
    core = core_ref[0]
    shape = out.shape
    to = lax.broadcasted_iota(jnp.int32, (shape[0], outs), 0)
    at = lax.broadcasted_iota(jnp.int32, (shape[0], outs), 1)
    column = jnp.bitwise_xor(to // (rows * half), core) * half + to % half
    pick = jnp.where(at == column, 1.0, 0.0).astype(BF16)
    turned = lax.dot_general(
        pick, weight[...], (((1,), (1,)), ((), ())), preferred_element_type=F32
    ).astype(BF16)
    to = lax.broadcasted_iota(jnp.int32, (channels, shape[1]), 0)
    at = lax.broadcasted_iota(jnp.int32, (channels, shape[1]), 1)
    channel = (at // rows + core * (channels // 2)) % channels
    widen = jnp.where(channel == to, 1.0, 0.0).astype(BF16)
    wide = jnp.dot(turned, widen, preferred_element_type=F32)
    to = lax.broadcasted_iota(jnp.int32, shape, 0)
    at = lax.broadcasted_iota(jnp.int32, shape, 1)
    out[...] = jnp.where(at % rows == (to // half) % rows, wide, 0.0).astype(BF16)


def projection(core, weight, rows):
    channels, outs = weight.shape
    return pl.pallas_call(
        functools.partial(weight_kernel, rows),
        out_shape=jax.ShapeDtypeStruct((rows * outs, rows * channels), BF16),
        in_specs=[SMEM, VMEM],
        out_specs=VMEM,
        compiler_params=pltpu.CompilerParams(vmem_limit_bytes=4 * MIB),
    )(core, weight)


def butterflies(values, sign):
    (r0, i0), (r1, i1), (r2, i2), (r3, i3) = values
    er, ei, dr, di = r0 + r2, i0 + i2, r0 - r2, i0 - i2
    fr, fi, hr, hi = r1 + r3, i1 + i3, r1 - r3, i1 - i3
    plus, minus = (dr - hi, di + hr), (dr + hi, di - hr)
    if sign < 0:
        plus, minus = minus, plus
    return [(er + fr, ei + fi), plus, (er - fr, ei - fi), minus]


def turn(values, cosine, sine):
    real, imag = values
    rows = real.shape[0]
    both = jnp.concatenate([real.astype(BF16), imag.astype(BF16)], axis=0)
    with_cosine = jnp.dot(both, cosine, preferred_element_type=F32)
    with_sine = jnp.dot(both, sine, preferred_element_type=F32)
    return with_cosine[:rows], with_cosine[rows:], with_sine[:rows], with_sine[rows:]


def full_turns(turns, rows):
    def whole(kind, which):
        cut = slice(kind * rows, (kind + 1) * rows)
        part = lambda n: turns[n // 2, cut, pl.ds((2 * (n % 2) + which) * 128, 128)].astype(F32)
        return part(0) + part(1) + part(2)

    return (whole(0, 0), whole(0, 1)), (whole(1, 0), whole(1, 1))


def pair_of(inner, rho, way):
    quarter = inner.shape[-1] // 2
    four = inner[rho].reshape(4, quarter, quarter)
    return four[2 * way], four[2 * way + 1]


def transform_kernel(place_ref, *refs):
    ins, (send, keep, signal, spec, first, last, inner, turns, twist, sem) = refs[:-10], refs[-10:]
    *pieces, spec_in, table = ins
    place = place_ref[0]
    count = pieces[0].shape[0]
    size = turns.shape[0]
    moves = [(table.at[place], first)]
    moves += [(ref, signal.at[pl.ds(n * count, count)]) for n, ref in enumerate(pieces)]
    moves += [(table.at[pl.ds(12 + size * place, size)], turns)]
    moves += [(table.at[pl.ds(8, 4)], inner), (spec_in, spec), (table.at[4 + place], last)]
    copies = [pltpu.make_async_copy(*move, sem.at[n]) for n, move in enumerate(moves)]
    for copy in copies:
        copy.start()
    for copy in copies[:6]:
        copy.wait()
    block = signal.shape[-1]
    quarter = block // 4
    lines = signal[...].reshape(-1, block)
    a_rows = first.shape[0] // 2
    coarse, fine = full_turns(turns, a_rows)
    turned = []
    for q in range(4):
        cut = slice(q * quarter, (q + 1) * quarter)
        both = jnp.dot(first[...], lines[:, cut], preferred_element_type=F32)
        for h in range(q * quarter // 128, (q + 1) * quarter // 128):
            lanes = slice(128 * h, 128 * (h + 1))
            uc, us = coarse[0][:, h : h + 1], coarse[1][:, h : h + 1]
            twist[0, :, lanes] = uc * fine[0] - us * fine[1]
            twist[1, :, lanes] = us * fine[0] + uc * fine[1]
        real, imag = both[:a_rows], both[a_rows:]
        cosine, sine = twist[0, :, cut], twist[1, :, cut]
        turned.append((real * cosine + imag * sine, imag * cosine - real * sine))
    mixes = butterflies(turned, -1)
    for copy in copies[6:-1]:
        copy.wait()
    backs = []
    for rho in range(4):
        rc, ic, rs, si = turn(mixes[rho], *pair_of(inner, rho, 0))
        zr, zi = rc + si, ic - rs
        cut = slice(rho * quarter, (rho + 1) * quarter)
        gr = spec[:, 0, :, cut].reshape(-1, quarter).astype(F32)
        gi = spec[:, 1, :, cut].reshape(-1, quarter).astype(F32)
        shaped = (zr * gr - zi * gi, zr * gi + zi * gr)
        rc, ic, rs, si = turn(shaped, *pair_of(inner, rho, 1))
        backs.append((rc - si, ic + rs))
    mixes = butterflies(backs, 1)
    scale = 1.0 / (block * block)
    half = last.shape[0] // 2
    copies[-1].wait()
    for q, (real, imag) in enumerate(mixes):
        cut = slice(q * quarter, (q + 1) * quarter)
        cosine, sine = twist[0, :, cut], twist[1, :, cut]
        pair = jnp.concatenate(
            [
                (real * cosine - imag * sine).astype(BF16),
                (imag * cosine + real * sine).astype(BF16),
            ],
            axis=0,
        )
        out = jnp.dot(last[...], pair, preferred_element_type=F32) * scale
        send[:, :, cut] = out[:half].astype(BF16).reshape(send.shape[0], send.shape[1], quarter)
        keep[:, :, cut] = out[half:].astype(BF16).reshape(keep.shape[0], keep.shape[1], quarter)


def transform(place, pieces, spec, table):
    members, rows_half, block = pieces[0].shape
    a_rows = spec.shape[0] * spec.shape[2]
    out = (2 * members, rows_half, block)
    square = table.shape[1:]
    return pl.pallas_call(
        transform_kernel,
        in_specs=[SMEM] + [ANYWHERE] * (len(pieces) + 1) + [ANY],
        out_specs=[VMEM, VMEM],
        out_shape=[jax.ShapeDtypeStruct(out, BF16)] * 2,
        scratch_shapes=[
            pltpu.VMEM((4 * members, rows_half, block), BF16),
            pltpu.VMEM(spec.shape, BF16),
            pltpu.VMEM(square, BF16),
            pltpu.VMEM(square, BF16),
            pltpu.VMEM((4,) + square, BF16),
            pltpu.VMEM(((table.shape[0] - 12) // 4,) + square, BF16),
            pltpu.VMEM((2, a_rows, block), F32),
            pltpu.SemaphoreType.DMA((len(pieces) + 5,)),
        ],
        compiler_params=pltpu.CompilerParams(vmem_limit_bytes=48 * MIB),
        cost_estimate=SMALL,
    )(place, *pieces, spec, table)


def gate_kernel(core_ref, conv, prod, gate, gate_other, skip, skip_other, weight, keep, send):
    _, channels, rows, block = conv.shape
    core = core_ref[0]
    here = channels // 2
    pieces = []
    for side, (values, gains) in enumerate(((gate, skip), (gate_other, skip_other))):
        for n in range(here):
            c = jnp.bitwise_xor(core, side) * here + n
            total = conv[0, c].astype(F32) + conv[1, c].astype(F32)
            total = total + gains[n] * prod[c].astype(F32)
            pieces.append((values[n].astype(F32) * total).astype(BF16))
    gated = jnp.concatenate(pieces, axis=0)
    mixed = jnp.dot(weight[...], gated, preferred_element_type=F32)
    outs = keep.shape[0]
    for r in range(rows):
        cut = slice(r * block, (r + 1) * block)
        keep[:, cut] = mixed[r * outs : (r + 1) * outs].astype(BF16)
        send[:, cut] = mixed[(rows + r) * outs : (rows + r + 1) * outs].astype(BF16)


def gate_and_project(core, conv, prod, gate, gate_other, skip, skip_other, weight):
    _, channels, rows, block = conv.shape
    outs = weight.shape[0] // (2 * rows)
    return pl.pallas_call(
        gate_kernel,
        out_shape=[jax.ShapeDtypeStruct((outs, rows * block), BF16)] * 2,
        in_specs=[SMEM, VMEM, VMEM, VMEM, VMEM, SMEM, SMEM, VMEM],
        out_specs=[VMEM, VMEM],
        compiler_params=pltpu.CompilerParams(vmem_limit_bytes=16 * MIB),
        cost_estimate=SMALL,
    )(core, conv, prod, gate, gate_other, skip, skip_other, weight)


def local_channels(k_feature, v_feature, q_feature, spectrum, skip_gain, out_weight):
    channels, tokens = k_feature.shape
    block = spectrum.shape[3]
    ctx_count = lax.axis_size("ctx")
    members = ctx_count // 2
    rows_half = tokens // block // 2
    a_half = spectrum.shape[2] // 2
    ctx, tp = lax.axis_index("ctx"), lax.axis_index("tp")
    core = tp.astype(jnp.int32).reshape(1)
    member = (ctx % members).astype(jnp.int32).reshape(1)
    place = (ctx // members * 2 + tp).astype(jnp.int32).reshape(1)
    tables = {
        name: jnp.asarray(table)
        for name, table in constant_tables(block, members, rows_half, a_half).items()
    }
    halves = [list(range(members)), list(range(members, 2 * members))]
    spread = lambda x: lax.all_to_all(x, "ctx", 0, 0, axis_index_groups=halves, tiled=True)
    across = lambda x: lax.ppermute(
        x, "ctx", [(d, (d + members) % ctx_count) for d in range(ctx_count)]
    )
    swap = lambda x: lax.ppermute(x, "tp", [(0, 1), (1, 0)])

    def joined(own, sent):
        start = ((1 - tp) * channels,) + (0,) * (own.ndim - 1)
        return lax.dynamic_update_slice(own, swap(sent), start)

    own, sent, other_rows = as_rows(core, block, k_feature, v_feature, spectrum=spectrum)
    product = joined(own, sent)
    product, spectrum, other_rows = lax.optimization_barrier((product, spectrum, other_rows))
    xa = spread(product)
    spec = arrange_spectrum(core, spectrum, swap(other_rows), tables["order"])
    xa, spec, q_feature, skip_gain, out_weight = lax.optimization_barrier(
        (xa, spec, q_feature, skip_gain, out_weight)
    )
    xb = swap(xa)
    za = across(xa)
    spec = spread(spec)
    gate, gate_sent = as_rows(core, block, q_feature)
    gate_other = swap(gate_sent)
    skip_other = swap(skip_gain)
    weight = projection(core, out_weight, rows_half)
    za, gate, gate_other, skip_other, weight = lax.optimization_barrier(
        (za, gate, gate_other, skip_other, weight)
    )
    zb = swap(za)

    send, keep = transform(place, (xa, xb, za, zb), spec, tables["transform"])
    total = (keep.astype(F32) + swap(send).astype(F32)).astype(BF16)
    conv = lax.all_to_all(total, "ctx", 0, 0, tiled=True).reshape(2, members, rows_half, block)
    kept, sent = gate_and_project(
        core, conv, product, gate, gate_other, skip_gain, skip_other, weight
    )
    came = swap(sent)
    low = jnp.where(tp == 0, kept, came)
    high = jnp.where(tp == 0, came, kept)
    return jnp.concatenate([low, high], axis=1)


def local(k_feature, v_feature, q_feature, spectrum, skip_gain, out_weight):
    channels, tokens = k_feature.shape
    block = spectrum.shape[3]
    ctx_count, tp_count = lax.axis_size("ctx"), lax.axis_size("tp")
    by_channels = (
        tp_count == 2
        and ctx_count == 2 * channels * tp_count
        and tokens * ctx_count * 2 == block * block
        and tokens % (32 * block) == 0
        and spectrum.shape[2] % 32 == 0
        and block % 512 == 0
        and out_weight.shape[1] % 16 == 0
    )
    plan = local_channels if by_channels else local_general
    return plan(k_feature, v_feature, q_feature, spectrum, skip_gain, out_weight)


def solution(mesh):
    placed = (
        P("tp", "ctx"),
        P("tp", "ctx"),
        P("tp", "ctx"),
        P(None, "tp", "ctx", None),
        P("tp"),
        P(),
    )
    return jax.shard_map(
        local, mesh=mesh, in_specs=placed, out_specs=P("tp", "ctx"), check_vma=False
    )
```

```python
import functools
import math

import numpy as np
import ml_dtypes
import jax
import jax.numpy as jnp
from jax import lax
from jax.experimental import pallas as pl
from jax.experimental.pallas import tpu as pltpu
from jax.sharding import PartitionSpec as P

F32 = jnp.float32
BF16 = jnp.bfloat16
VMEM = pl.BlockSpec(memory_space=pltpu.VMEM)
SMEM = pl.BlockSpec(memory_space=pltpu.SMEM)
ANY = pl.BlockSpec(memory_space=pltpu.HBM)
ANYWHERE = pl.BlockSpec(memory_space=pl.ANY)
MIB = 1 << 20
SMALL = pl.CostEstimate(flops=1, bytes_accessed=1, transcendentals=0)


def fourier_tables(length_all):
    positions = jnp.arange(length_all, dtype=jnp.int32)
    phase_index = positions[:, None] * positions[None, :] % length_all
    angles = phase_index.astype(jnp.float32) * (2.0 * math.pi / length_all)
    return (jnp.cos(angles).astype(jnp.bfloat16), jnp.sin(angles).astype(jnp.bfloat16))


def twist_tables(left_index, right_index, length_all):
    phase_index = left_index[:, None] * right_index[None, :] % length_all
    angles = phase_index.astype(jnp.float32) * (2.0 * math.pi / length_all)
    return (jnp.cos(angles), jnp.sin(angles))


def contract(form, left, right):
    return jnp.einsum(form, left, right, preferred_element_type=jnp.float32)


def local_general(k_feature, v_feature, q_feature, spectrum, skip_gain, out_weight):
    channels, tokens = k_feature.shape
    block_order = spectrum.shape[3]
    length_all = block_order * block_order
    ctx_count = lax.axis_size("ctx")
    slab_width = block_order // ctx_count
    rows_here = tokens // block_order
    ctx_index = lax.axis_index("ctx")
    product = (k_feature.astype(jnp.float32) * v_feature.astype(jnp.float32)).astype(jnp.bfloat16)
    cosine_full, sine_full = fourier_tables(block_order)
    cosine_half = cosine_full[: block_order // 2]
    sine_half = sine_full[: block_order // 2]
    positions = jnp.arange(block_order, dtype=jnp.int32)
    local_ticks = ctx_index * slab_width + jnp.arange(slab_width, dtype=jnp.int32)
    grid_rows = lax.all_to_all(
        product.reshape(channels, rows_here, block_order),
        "ctx",
        split_axis=2,
        concat_axis=1,
        tiled=True,
    )
    first_real = contract("cij,ia->caj", grid_rows, cosine_half)
    first_imag = -contract("cij,ia->caj", grid_rows, sine_half)
    twist_cosine, twist_sine = twist_tables(positions, local_ticks, length_all)
    spread_real = (first_real * twist_cosine + first_imag * twist_sine).astype(jnp.bfloat16)
    spread_imag = (first_imag * twist_cosine - first_real * twist_sine).astype(jnp.bfloat16)
    block_real, block_imag = (
        lax.all_to_all(spread_real, "ctx", split_axis=1, concat_axis=2, tiled=True),
        lax.all_to_all(spread_imag, "ctx", split_axis=1, concat_axis=2, tiled=True),
    )
    freq_real = contract("caj,jb->cab", block_real, cosine_full) + contract(
        "caj,jb->cab", block_imag, sine_full
    )
    freq_imag = contract("caj,jb->cab", block_imag, cosine_full) - contract(
        "caj,jb->cab", block_real, sine_full
    )
    resp_real = spectrum[0].astype(jnp.float32)
    resp_imag = spectrum[1].astype(jnp.float32)
    shaped_real = (freq_real * resp_real - freq_imag * resp_imag).astype(jnp.bfloat16)
    shaped_imag = (freq_real * resp_imag + freq_imag * resp_real).astype(jnp.bfloat16)
    inner_real = contract("cab,bj->caj", shaped_real, cosine_full) - contract(
        "cab,bj->caj", shaped_imag, sine_full
    )
    inner_imag = contract("cab,bj->caj", shaped_imag, cosine_full) + contract(
        "cab,bj->caj", shaped_real, sine_full
    )
    twist_cosine, twist_sine = twist_tables(local_ticks, positions, length_all)
    back_real = (inner_real * twist_cosine - inner_imag * twist_sine).astype(jnp.bfloat16)
    back_imag = (inner_imag * twist_cosine + inner_real * twist_sine).astype(jnp.bfloat16)
    summed = contract(
        "ia,caj->cij",
        cosine_half,
        lax.all_to_all(back_real, "ctx", split_axis=2, concat_axis=1, tiled=True),
    ) - contract(
        "ia,caj->cij",
        sine_half,
        lax.all_to_all(back_imag, "ctx", split_axis=2, concat_axis=1, tiled=True),
    )
    spatial = (summed * (1.0 / length_all)).astype(jnp.bfloat16)
    convolved = lax.all_to_all(spatial, "ctx", split_axis=1, concat_axis=2, tiled=True).reshape(
        channels, tokens
    )
    gated_rows = (
        q_feature.astype(jnp.float32)
        * (convolved.astype(jnp.float32) + skip_gain[:, None] * product.astype(jnp.float32))
    ).astype(jnp.bfloat16)
    tp_index = lax.axis_index("tp")
    my_weight = lax.dynamic_slice_in_dim(out_weight, tp_index * channels, channels, 0)
    return lax.psum_scatter(
        jnp.dot(my_weight.T, gated_rows, preferred_element_type=jnp.float32).astype(jnp.bfloat16),
        "tp",
        scatter_dimension=0,
        tiled=True,
    )


def cosine_sine(product, length):
    angles = (product % length).astype(np.float64) * (2.0 * np.pi / length)
    return np.cos(angles), np.sin(angles)


def last_order(members):
    size = members // 2
    return [quarter * size + n for n in range(size) for quarter in (2, 0, 3, 1)]


@functools.lru_cache(maxsize=None)
def constant_tables(block, members, rows_half, a_half):
    quarter = block // 4
    firsts, lasts, coarses, fines = [], [], [], []
    part = np.arange(members)
    for g in range(2):
        for s in range(2):
            a = (
                (g * members + part)[:, None] * 2 * a_half
                + s * a_half
                + np.arange(a_half)[None, :]
            ).reshape(-1)

            def rows(group, core):
                device = group * members + part
                i = device[:, None] * 2 * rows_half + core * rows_half
                return (i + np.arange(rows_half)[None, :]).reshape(-1)

            i_in = np.concatenate([rows(g, s), rows(g, 1 - s), rows(1 - g, s), rows(1 - g, 1 - s)])
            cosine, sine = cosine_sine(a[:, None] * i_in[None, :], block)
            firsts.append(np.concatenate([cosine, -sine], 0))
            place = last_order(members)

            def by_place(core):
                i = np.concatenate([rows(0, core), rows(1, core)])
                return i.reshape(2 * members, -1)[place].reshape(-1)

            i_out = np.concatenate([by_place(1 - s), by_place(s)])
            cosine, sine = cosine_sine(i_out[:, None] * a[None, :], block)
            lasts.append(np.concatenate([cosine, -sine], 1))
            coarse = 128 * (np.arange(128) % (block // 128))
            coarses.append(np.stack(cosine_sine(a[:, None] * coarse[None, :], block * block)))
            fines.append(np.stack(cosine_sine(a[:, None] * np.arange(128)[None, :], block * block)))
    inner = []
    for rho in range(4):
        cosine, sine = cosine_sine(
            np.arange(quarter)[:, None] * (4 * np.arange(quarter) + rho)[None, :], block
        )
        inner.append(np.stack([cosine, sine, cosine.T, sine.T]))
    order = np.zeros((quarter, quarter), np.float32)
    b = np.arange(quarter)
    order[b, (b % 4) * (quarter // 4) + b // 4] = 1.0
    narrow = lambda x: np.asarray(x, np.float32).astype(ml_dtypes.bfloat16)
    rest = np.stack([coarses, fines], 1).astype(np.float32)
    turns = []
    for _ in range(3):
        turns.append(narrow(rest))
        rest = rest - turns[-1].astype(np.float32)
    turns = np.stack(turns + [np.zeros_like(turns[0])], 1).transpose(0, 2, 4, 1, 3, 5)
    turns = turns.reshape(4, 2 * turns.shape[2], 2, 2 * quarter).transpose(0, 2, 1, 3)
    square = (-1, 2 * quarter, 2 * quarter)
    entries = [np.stack(firsts), np.stack(lasts), np.stack(inner).reshape(square)]
    return dict(
        transform=np.concatenate([narrow(x) for x in entries] + [turns.reshape(square)]),
        order=narrow(order),
    )


def product_kernel(block, count, core_ref, *refs):
    ins, outs, scratch, sem = refs[:count], refs[count:-1 - count], refs[-1 - count : -1], refs[-1]
    copies = [pltpu.make_async_copy(ins[n], scratch[n], sem.at[n]) for n in range(count)]
    for copy in copies:
        copy.start()
    rows_copy = None
    if len(outs) == 4:
        spectrum, own, send, other_rows = outs
        a_half = other_rows.shape[2]
        at = pl.ds(pl.multiple_of((1 - core_ref[0]) * a_half, a_half), a_half)
        rows_copy = pltpu.make_async_copy(spectrum.at[:, :, at, :], other_rows, sem.at[count])
        rows_copy.start()
    else:
        own, send = outs
    core = core_ref[0]
    channels, tokens = ins[0].shape
    place = 0 if own.shape[0] == channels else channels * core
    rows = tokens // block
    half = rows // 2
    to = lax.broadcasted_iota(jnp.int32, (channels * rows, channels * rows), 0)
    at = lax.broadcasted_iota(jnp.int32, (channels * rows, channels * rows), 1)
    side = jnp.bitwise_xor(to // (channels * half), core)
    source = (side * half + to % half) * channels + (to // half) % channels
    order = jnp.where(at == source, 1.0, 0.0).astype(BF16)
    for copy in copies:
        copy.wait()
    pieces = []
    for i in range(rows):
        cut = slice(i * block, (i + 1) * block)
        piece = scratch[0][:, cut].astype(F32)
        for other in scratch[1:]:
            piece = piece * other[:, cut].astype(F32)
        pieces.append(piece)
    stacked = jnp.concatenate(pieces, axis=0).astype(BF16)
    ordered = jnp.dot(order, stacked, preferred_element_type=F32).astype(BF16)
    ordered = ordered.reshape(2, channels, half, block)
    own[pl.ds(place, channels)] = ordered[0]
    send[...] = ordered[1]
    if rows_copy is not None:
        rows_copy.wait()


def as_rows(core, block, *arrays, spectrum=None):
    channels, tokens = arrays[0].shape
    half = tokens // block // 2
    room, extra, shapes = 1, [], []
    if spectrum is not None:
        two, _, a_here, _ = spectrum.shape
        room, extra = 2, [spectrum]
        shapes = [jax.ShapeDtypeStruct((two, channels, a_here // 2, block), BF16)]
    return pl.pallas_call(
        functools.partial(product_kernel, block, len(arrays)),
        out_shape=[
            jax.ShapeDtypeStruct((room * channels, half, block), BF16),
            jax.ShapeDtypeStruct((channels, half, block), BF16),
        ]
        + shapes,
        in_specs=[SMEM] + [ANY] * len(arrays + tuple(extra)),
        out_specs=[VMEM] * (2 + len(shapes)),
        scratch_shapes=[pltpu.VMEM((channels, tokens), BF16)] * len(arrays)
        + [pltpu.SemaphoreType.DMA((len(arrays) + 1,))],
        cost_estimate=SMALL,
    )(core, *arrays, *extra)


def spectrum_kernel(core_ref, in_ref, came_ref, order_ref, *refs):
    moved, rows, came, order, sem = refs
    core = core_ref[0]
    two, channels, a_half, block = rows.shape
    at = pl.ds(pl.multiple_of(core * a_half, a_half), a_half)
    copies = [
        pltpu.make_async_copy(order_ref, order, sem.at[0]),
        pltpu.make_async_copy(in_ref.at[:, :, at, :], rows, sem.at[1]),
        pltpu.make_async_copy(came_ref, came, sem.at[2]),
    ]
    for copy in copies:
        copy.start()
    copies[0].wait()
    quarter = block // 4
    step = quarter // 4
    for side, ref in ((core, rows), (1 - core, came)):
        copies[1 if ref is rows else 2].wait()
        flat = jnp.concatenate([ref[n, c] for c in range(channels) for n in range(two)], 0)
        parts = [
            jnp.dot(flat[:, q * quarter : (q + 1) * quarter], order[...], preferred_element_type=F32)
            for q in range(4)
        ]
        for rho in range(4):
            columns = [part[:, rho * step : (rho + 1) * step] for part in parts]
            columns = jnp.concatenate(columns, axis=1).astype(BF16)
            moved[pl.ds(channels * side, channels), :, :, rho * quarter : (rho + 1) * quarter] = (
                columns.reshape(channels, two, a_half, quarter)
            )


def arrange_spectrum(core, spectrum, came, order):
    two, channels, a_half, block = came.shape
    return pl.pallas_call(
        spectrum_kernel,
        out_shape=jax.ShapeDtypeStruct((2 * channels, two, a_half, block), BF16),
        in_specs=[SMEM, ANY, ANY, ANY],
        out_specs=VMEM,
        scratch_shapes=[
            pltpu.VMEM(came.shape, BF16),
            pltpu.VMEM(came.shape, BF16),
            pltpu.VMEM(order.shape, BF16),
            pltpu.SemaphoreType.DMA((3,)),
        ],
        cost_estimate=SMALL,
    )(core, spectrum, came, order)


def weight_kernel(rows, core_ref, weight, out):
    channels, outs = weight.shape
    half = outs // 2
    core = core_ref[0]
    shape = out.shape
    to = lax.broadcasted_iota(jnp.int32, (shape[0], outs), 0)
    at = lax.broadcasted_iota(jnp.int32, (shape[0], outs), 1)
    column = jnp.bitwise_xor(to // (rows * half), core) * half + to % half
    pick = jnp.where(at == column, 1.0, 0.0).astype(BF16)
    turned = lax.dot_general(
        pick, weight[...], (((1,), (1,)), ((), ())), preferred_element_type=F32
    ).astype(BF16)
    to = lax.broadcasted_iota(jnp.int32, (channels, shape[1]), 0)
    at = lax.broadcasted_iota(jnp.int32, (channels, shape[1]), 1)
    channel = (at // rows + core * (channels // 2)) % channels
    widen = jnp.where(channel == to, 1.0, 0.0).astype(BF16)
    wide = jnp.dot(turned, widen, preferred_element_type=F32)
    to = lax.broadcasted_iota(jnp.int32, shape, 0)
    at = lax.broadcasted_iota(jnp.int32, shape, 1)
    out[...] = jnp.where(at % rows == (to // half) % rows, wide, 0.0).astype(BF16)


def projection(core, weight, rows):
    channels, outs = weight.shape
    return pl.pallas_call(
        functools.partial(weight_kernel, rows),
        out_shape=jax.ShapeDtypeStruct((rows * outs, rows * channels), BF16),
        in_specs=[SMEM, VMEM],
        out_specs=VMEM,
        compiler_params=pltpu.CompilerParams(vmem_limit_bytes=4 * MIB),
    )(core, weight)


def butterflies(values, sign):
    (r0, i0), (r1, i1), (r2, i2), (r3, i3) = values
    er, ei, dr, di = r0 + r2, i0 + i2, r0 - r2, i0 - i2
    fr, fi, hr, hi = r1 + r3, i1 + i3, r1 - r3, i1 - i3
    plus, minus = (dr - hi, di + hr), (dr + hi, di - hr)
    if sign < 0:
        plus, minus = minus, plus
    return [(er + fr, ei + fi), plus, (er - fr, ei - fi), minus]


def turn(values, cosine, sine):
    real, imag = values
    rows = real.shape[0]
    both = jnp.concatenate([real.astype(BF16), imag.astype(BF16)], axis=0)
    with_cosine = jnp.dot(both, cosine, preferred_element_type=F32)
    with_sine = jnp.dot(both, sine, preferred_element_type=F32)
    return with_cosine[:rows], with_cosine[rows:], with_sine[:rows], with_sine[rows:]


def full_turns(turns, rows):
    def whole(kind, which):
        cut = slice(kind * rows, (kind + 1) * rows)
        part = lambda n: turns[n // 2, cut, pl.ds((2 * (n % 2) + which) * 128, 128)].astype(F32)
        return part(0) + part(1) + part(2)

    return (whole(0, 0), whole(0, 1)), (whole(1, 0), whole(1, 1))


def pair_of(inner, rho, way):
    quarter = inner.shape[-1] // 2
    four = inner[rho].reshape(4, quarter, quarter)
    return four[2 * way], four[2 * way + 1]


def transform_kernel(place_ref, *refs):
    ins, (send, keep, signal, spec, first, last, inner, turns, twist, sem) = refs[:-10], refs[-10:]
    *pieces, spec_in, table = ins
    place = place_ref[0]
    count = pieces[0].shape[0]
    size = turns.shape[0]
    moves = [(table.at[place], first)]
    moves += [(ref, signal.at[pl.ds(n * count, count)]) for n, ref in enumerate(pieces)]
    moves += [(table.at[pl.ds(12 + size * place, size)], turns)]
    moves += [(table.at[pl.ds(8, 4)], inner), (spec_in, spec), (table.at[4 + place], last)]
    copies = [pltpu.make_async_copy(*move, sem.at[n]) for n, move in enumerate(moves)]
    for copy in copies:
        copy.start()
    for copy in copies[:6]:
        copy.wait()
    block = signal.shape[-1]
    quarter = block // 4
    lines = signal[...].reshape(-1, block)
    a_rows = first.shape[0] // 2
    coarse, fine = full_turns(turns, a_rows)
    turned = []
    for q in range(4):
        cut = slice(q * quarter, (q + 1) * quarter)
        both = jnp.dot(first[...], lines[:, cut], preferred_element_type=F32)
        for h in range(q * quarter // 128, (q + 1) * quarter // 128):
            lanes = slice(128 * h, 128 * (h + 1))
            uc, us = coarse[0][:, h : h + 1], coarse[1][:, h : h + 1]
            twist[0, :, lanes] = uc * fine[0] - us * fine[1]
            twist[1, :, lanes] = us * fine[0] + uc * fine[1]
        real, imag = both[:a_rows], both[a_rows:]
        cosine, sine = twist[0, :, cut], twist[1, :, cut]
        turned.append((real * cosine + imag * sine, imag * cosine - real * sine))
    mixes = butterflies(turned, -1)
    for copy in copies[6:-1]:
        copy.wait()
    backs = []
    for rho in range(4):
        rc, ic, rs, si = turn(mixes[rho], *pair_of(inner, rho, 0))
        zr, zi = rc + si, ic - rs
        cut = slice(rho * quarter, (rho + 1) * quarter)
        gr = spec[:, 0, :, cut].reshape(-1, quarter).astype(F32)
        gi = spec[:, 1, :, cut].reshape(-1, quarter).astype(F32)
        shaped = (zr * gr - zi * gi, zr * gi + zi * gr)
        rc, ic, rs, si = turn(shaped, *pair_of(inner, rho, 1))
        backs.append((rc - si, ic + rs))
    mixes = butterflies(backs, 1)
    scale = 1.0 / (block * block)
    half = last.shape[0] // 2
    copies[-1].wait()
    for q, (real, imag) in enumerate(mixes):
        cut = slice(q * quarter, (q + 1) * quarter)
        cosine, sine = twist[0, :, cut], twist[1, :, cut]
        pair = jnp.concatenate(
            [
                (real * cosine - imag * sine).astype(BF16),
                (imag * cosine + real * sine).astype(BF16),
            ],
            axis=0,
        )
        out = jnp.dot(last[...], pair, preferred_element_type=F32) * scale
        send[:, :, cut] = out[:half].astype(BF16).reshape(send.shape[0], send.shape[1], quarter)
        keep[:, :, cut] = out[half:].astype(BF16).reshape(keep.shape[0], keep.shape[1], quarter)


def transform(place, pieces, spec, table):
    members, rows_half, block = pieces[0].shape
    a_rows = spec.shape[0] * spec.shape[2]
    out = (2 * members, rows_half, block)
    square = table.shape[1:]
    return pl.pallas_call(
        transform_kernel,
        in_specs=[SMEM] + [ANYWHERE] * (len(pieces) + 1) + [ANY],
        out_specs=[VMEM, VMEM],
        out_shape=[jax.ShapeDtypeStruct(out, BF16)] * 2,
        scratch_shapes=[
            pltpu.VMEM((4 * members, rows_half, block), BF16),
            pltpu.VMEM(spec.shape, BF16),
            pltpu.VMEM(square, BF16),
            pltpu.VMEM(square, BF16),
            pltpu.VMEM((4,) + square, BF16),
            pltpu.VMEM(((table.shape[0] - 12) // 4,) + square, BF16),
            pltpu.VMEM((2, a_rows, block), F32),
            pltpu.SemaphoreType.DMA((len(pieces) + 5,)),
        ],
        compiler_params=pltpu.CompilerParams(vmem_limit_bytes=48 * MIB),
        cost_estimate=SMALL,
    )(place, *pieces, spec, table)


def gate_kernel(core_ref, conv, prod, gate, gate_other, skip, skip_other, weight, keep, send):
    here, _, rows, block = conv.shape
    core = core_ref[0]
    pieces = []
    for side, (values, gains) in enumerate(((gate, skip), (gate_other, skip_other))):
        for n in range(here):
            high = jnp.bitwise_xor(core, side)
            total = conv[n, 2 * high].astype(F32) + conv[n, 2 * high + 1].astype(F32)
            total = total + gains[n] * prod[high * here + n].astype(F32)
            pieces.append((values[n].astype(F32) * total).astype(BF16))
    gated = jnp.concatenate(pieces, axis=0)
    mixed = jnp.dot(weight[...], gated, preferred_element_type=F32)
    outs = keep.shape[0]
    for r in range(rows):
        cut = slice(r * block, (r + 1) * block)
        keep[:, cut] = mixed[r * outs : (r + 1) * outs].astype(BF16)
        send[:, cut] = mixed[(rows + r) * outs : (rows + r + 1) * outs].astype(BF16)


def gate_and_project(core, conv, prod, gate, gate_other, skip, skip_other, weight):
    _, _, rows, block = conv.shape
    outs = weight.shape[0] // (2 * rows)
    return pl.pallas_call(
        gate_kernel,
        out_shape=[jax.ShapeDtypeStruct((outs, rows * block), BF16)] * 2,
        in_specs=[SMEM, VMEM, VMEM, VMEM, VMEM, SMEM, SMEM, VMEM],
        out_specs=[VMEM, VMEM],
        compiler_params=pltpu.CompilerParams(vmem_limit_bytes=16 * MIB),
        cost_estimate=SMALL,
    )(core, conv, prod, gate, gate_other, skip, skip_other, weight)


def local_channels(k_feature, v_feature, q_feature, spectrum, skip_gain, out_weight):
    channels, tokens = k_feature.shape
    block = spectrum.shape[3]
    ctx_count = lax.axis_size("ctx")
    members = ctx_count // 2
    rows_half = tokens // block // 2
    a_half = spectrum.shape[2] // 2
    ctx, tp = lax.axis_index("ctx"), lax.axis_index("tp")
    core = tp.astype(jnp.int32).reshape(1)
    member = (ctx % members).astype(jnp.int32).reshape(1)
    place = (ctx // members * 2 + tp).astype(jnp.int32).reshape(1)
    tables = {
        name: jnp.asarray(table)
        for name, table in constant_tables(block, members, rows_half, a_half).items()
    }
    halves = [list(range(members)), list(range(members, 2 * members))]
    spread = lambda x: lax.all_to_all(x, "ctx", 0, 0, axis_index_groups=halves, tiled=True)
    across = lambda x: lax.ppermute(
        x, "ctx", [(d, (d + members) % ctx_count) for d in range(ctx_count)]
    )
    swap = lambda x: lax.ppermute(x, "tp", [(0, 1), (1, 0)])

    def joined(own, sent):
        start = ((1 - tp) * channels,) + (0,) * (own.ndim - 1)
        return lax.dynamic_update_slice(own, swap(sent), start)

    own, sent, other_rows = as_rows(core, block, k_feature, v_feature, spectrum=spectrum)
    product = joined(own, sent)
    product, spectrum, other_rows = lax.optimization_barrier((product, spectrum, other_rows))
    xa = spread(product)
    spec = arrange_spectrum(core, spectrum, swap(other_rows), tables["order"])
    xa, spec, q_feature, skip_gain, out_weight = lax.optimization_barrier(
        (xa, spec, q_feature, skip_gain, out_weight)
    )
    xb = swap(xa)
    za = across(xa)
    spec = spread(spec)
    gate, gate_sent = as_rows(core, block, q_feature)
    gate_other = swap(gate_sent)
    skip_other = swap(skip_gain)
    weight = projection(core, out_weight, rows_half)
    za, gate, gate_other, skip_other, weight = lax.optimization_barrier(
        (za, gate, gate_other, skip_other, weight)
    )
    zb = swap(za)

    send, keep = transform(place, (xa, xb, za, zb), spec, tables["transform"])
    total = (keep.astype(F32) + swap(send).astype(F32)).astype(BF16)
    conv = lax.all_to_all(
        total, "ctx", 0, 0, axis_index_groups=[last_order(members)], tiled=True
    ).reshape(channels, 4, rows_half, block)
    kept, sent = gate_and_project(
        core, conv, product, gate, gate_other, skip_gain, skip_other, weight
    )
    came = swap(sent)
    low = jnp.where(tp == 0, kept, came)
    high = jnp.where(tp == 0, came, kept)
    return jnp.concatenate([low, high], axis=1)


def local(k_feature, v_feature, q_feature, spectrum, skip_gain, out_weight):
    channels, tokens = k_feature.shape
    block = spectrum.shape[3]
    ctx_count, tp_count = lax.axis_size("ctx"), lax.axis_size("tp")
    by_channels = (
        tp_count == 2
        and ctx_count == 2 * channels * tp_count
        and tokens * ctx_count * 2 == block * block
        and tokens % (32 * block) == 0
        and spectrum.shape[2] % 32 == 0
        and block % 512 == 0
        and out_weight.shape[1] % 16 == 0
    )
    plan = local_channels if by_channels else local_general
    return plan(k_feature, v_feature, q_feature, spectrum, skip_gain, out_weight)


def solution(mesh):
    placed = (
        P("tp", "ctx"),
        P("tp", "ctx"),
        P("tp", "ctx"),
        P(None, "tp", "ctx", None),
        P("tp"),
        P(),
    )
    return jax.shard_map(
        local, mesh=mesh, in_specs=placed, out_specs=P("tp", "ctx"), check_vma=False
    )
```

```python
import functools
import math

import numpy as np
import ml_dtypes
import jax
import jax.numpy as jnp
from jax import lax
from jax.experimental import pallas as pl
from jax.experimental.pallas import tpu as pltpu
from jax.sharding import PartitionSpec as P

F32 = jnp.float32
BF16 = jnp.bfloat16
VMEM = pl.BlockSpec(memory_space=pltpu.VMEM)
SMEM = pl.BlockSpec(memory_space=pltpu.SMEM)
ANY = pl.BlockSpec(memory_space=pltpu.HBM)
ANYWHERE = pl.BlockSpec(memory_space=pl.ANY)
MIB = 1 << 20
SMALL = pl.CostEstimate(flops=1, bytes_accessed=1, transcendentals=0)


def fourier_tables(length_all):
    positions = jnp.arange(length_all, dtype=jnp.int32)
    phase_index = positions[:, None] * positions[None, :] % length_all
    angles = phase_index.astype(jnp.float32) * (2.0 * math.pi / length_all)
    return (jnp.cos(angles).astype(jnp.bfloat16), jnp.sin(angles).astype(jnp.bfloat16))


def twist_tables(left_index, right_index, length_all):
    phase_index = left_index[:, None] * right_index[None, :] % length_all
    angles = phase_index.astype(jnp.float32) * (2.0 * math.pi / length_all)
    return (jnp.cos(angles), jnp.sin(angles))


def contract(form, left, right):
    return jnp.einsum(form, left, right, preferred_element_type=jnp.float32)


def local_general(k_feature, v_feature, q_feature, spectrum, skip_gain, out_weight):
    channels, tokens = k_feature.shape
    block_order = spectrum.shape[3]
    length_all = block_order * block_order
    ctx_count = lax.axis_size("ctx")
    slab_width = block_order // ctx_count
    rows_here = tokens // block_order
    ctx_index = lax.axis_index("ctx")
    product = (k_feature.astype(jnp.float32) * v_feature.astype(jnp.float32)).astype(jnp.bfloat16)
    cosine_full, sine_full = fourier_tables(block_order)
    cosine_half = cosine_full[: block_order // 2]
    sine_half = sine_full[: block_order // 2]
    positions = jnp.arange(block_order, dtype=jnp.int32)
    local_ticks = ctx_index * slab_width + jnp.arange(slab_width, dtype=jnp.int32)
    grid_rows = lax.all_to_all(
        product.reshape(channels, rows_here, block_order),
        "ctx",
        split_axis=2,
        concat_axis=1,
        tiled=True,
    )
    first_real = contract("cij,ia->caj", grid_rows, cosine_half)
    first_imag = -contract("cij,ia->caj", grid_rows, sine_half)
    twist_cosine, twist_sine = twist_tables(positions, local_ticks, length_all)
    spread_real = (first_real * twist_cosine + first_imag * twist_sine).astype(jnp.bfloat16)
    spread_imag = (first_imag * twist_cosine - first_real * twist_sine).astype(jnp.bfloat16)
    block_real, block_imag = (
        lax.all_to_all(spread_real, "ctx", split_axis=1, concat_axis=2, tiled=True),
        lax.all_to_all(spread_imag, "ctx", split_axis=1, concat_axis=2, tiled=True),
    )
    freq_real = contract("caj,jb->cab", block_real, cosine_full) + contract(
        "caj,jb->cab", block_imag, sine_full
    )
    freq_imag = contract("caj,jb->cab", block_imag, cosine_full) - contract(
        "caj,jb->cab", block_real, sine_full
    )
    resp_real = spectrum[0].astype(jnp.float32)
    resp_imag = spectrum[1].astype(jnp.float32)
    shaped_real = (freq_real * resp_real - freq_imag * resp_imag).astype(jnp.bfloat16)
    shaped_imag = (freq_real * resp_imag + freq_imag * resp_real).astype(jnp.bfloat16)
    inner_real = contract("cab,bj->caj", shaped_real, cosine_full) - contract(
        "cab,bj->caj", shaped_imag, sine_full
    )
    inner_imag = contract("cab,bj->caj", shaped_imag, cosine_full) + contract(
        "cab,bj->caj", shaped_real, sine_full
    )
    twist_cosine, twist_sine = twist_tables(local_ticks, positions, length_all)
    back_real = (inner_real * twist_cosine - inner_imag * twist_sine).astype(jnp.bfloat16)
    back_imag = (inner_imag * twist_cosine + inner_real * twist_sine).astype(jnp.bfloat16)
    summed = contract(
        "ia,caj->cij",
        cosine_half,
        lax.all_to_all(back_real, "ctx", split_axis=2, concat_axis=1, tiled=True),
    ) - contract(
        "ia,caj->cij",
        sine_half,
        lax.all_to_all(back_imag, "ctx", split_axis=2, concat_axis=1, tiled=True),
    )
    spatial = (summed * (1.0 / length_all)).astype(jnp.bfloat16)
    convolved = lax.all_to_all(spatial, "ctx", split_axis=1, concat_axis=2, tiled=True).reshape(
        channels, tokens
    )
    gated_rows = (
        q_feature.astype(jnp.float32)
        * (convolved.astype(jnp.float32) + skip_gain[:, None] * product.astype(jnp.float32))
    ).astype(jnp.bfloat16)
    tp_index = lax.axis_index("tp")
    my_weight = lax.dynamic_slice_in_dim(out_weight, tp_index * channels, channels, 0)
    return lax.psum_scatter(
        jnp.dot(my_weight.T, gated_rows, preferred_element_type=jnp.float32).astype(jnp.bfloat16),
        "tp",
        scatter_dimension=0,
        tiled=True,
    )


def cosine_sine(product, length):
    angles = (product % length).astype(np.float64) * (2.0 * np.pi / length)
    return np.cos(angles), np.sin(angles)


def last_order(members):
    size = members // 2
    turns = lambda n: (2 * size + n, size - 1 - n, 3 * size + n, 2 * size - 1 - n)
    return [device for n in range(size) for device in turns(n)]


@functools.lru_cache(maxsize=None)
def constant_tables(block, members, rows_half, a_half):
    quarter = block // 4
    firsts, lasts, coarses, fines = [], [], [], []
    part = np.arange(members)
    for g in range(2):
        for s in range(2):
            a = (
                (g * members + part)[:, None] * 2 * a_half
                + s * a_half
                + np.arange(a_half)[None, :]
            ).reshape(-1)

            def rows(group, core):
                device = group * members + part
                i = device[:, None] * 2 * rows_half + core * rows_half
                return (i + np.arange(rows_half)[None, :]).reshape(-1)

            i_in = np.concatenate([rows(g, s), rows(g, 1 - s), rows(1 - g, s), rows(1 - g, 1 - s)])
            cosine, sine = cosine_sine(a[:, None] * i_in[None, :], block)
            firsts.append(np.concatenate([cosine, -sine], 0))
            place = last_order(members)

            def by_place(core):
                i = np.concatenate([rows(0, core), rows(1, core)])
                return i.reshape(2 * members, -1)[place].reshape(-1)

            i_out = np.concatenate([by_place(1 - s), by_place(s)])
            cosine, sine = cosine_sine(i_out[:, None] * a[None, :], block)
            lasts.append(np.concatenate([cosine, -sine], 1))
            coarse = 128 * (np.arange(128) % (block // 128))
            coarses.append(np.stack(cosine_sine(a[:, None] * coarse[None, :], block * block)))
            fines.append(np.stack(cosine_sine(a[:, None] * np.arange(128)[None, :], block * block)))
    inner = []
    for rho in range(4):
        cosine, sine = cosine_sine(
            np.arange(quarter)[:, None] * (4 * np.arange(quarter) + rho)[None, :], block
        )
        inner.append(np.stack([cosine, sine, cosine.T, sine.T]))
    order = np.zeros((quarter, quarter), np.float32)
    b = np.arange(quarter)
    order[b, (b % 4) * (quarter // 4) + b // 4] = 1.0
    narrow = lambda x: np.asarray(x, np.float32).astype(ml_dtypes.bfloat16)
    rest = np.stack([coarses, fines], 1).astype(np.float32)
    turns = []
    for _ in range(3):
        turns.append(narrow(rest))
        rest = rest - turns[-1].astype(np.float32)
    turns = np.stack(turns + [np.zeros_like(turns[0])], 1).transpose(0, 2, 4, 1, 3, 5)
    turns = turns.reshape(4, 2 * turns.shape[2], 2, 2 * quarter).transpose(0, 2, 1, 3)
    square = (-1, 2 * quarter, 2 * quarter)
    entries = [np.stack(firsts), np.stack(lasts), np.stack(inner).reshape(square)]
    return dict(
        transform=np.concatenate([narrow(x) for x in entries] + [turns.reshape(square)]),
        order=narrow(order),
    )


def product_kernel(block, count, core_ref, *refs):
    ins, outs, scratch, sem = refs[:count], refs[count:-1 - count], refs[-1 - count : -1], refs[-1]
    copies = [pltpu.make_async_copy(ins[n], scratch[n], sem.at[n]) for n in range(count)]
    for copy in copies:
        copy.start()
    rows_copy = None
    if len(outs) == 4:
        spectrum, own, send, other_rows = outs
        a_half = other_rows.shape[2]
        at = pl.ds(pl.multiple_of((1 - core_ref[0]) * a_half, a_half), a_half)
        rows_copy = pltpu.make_async_copy(spectrum.at[:, :, at, :], other_rows, sem.at[count])
        rows_copy.start()
    else:
        own, send = outs
    core = core_ref[0]
    channels, tokens = ins[0].shape
    place = 0 if own.shape[0] == channels else channels * core
    rows = tokens // block
    half = rows // 2
    to = lax.broadcasted_iota(jnp.int32, (channels * rows, channels * rows), 0)
    at = lax.broadcasted_iota(jnp.int32, (channels * rows, channels * rows), 1)
    side = jnp.bitwise_xor(to // (channels * half), core)
    source = (side * half + to % half) * channels + (to // half) % channels
    order = jnp.where(at == source, 1.0, 0.0).astype(BF16)
    for copy in copies:
        copy.wait()
    pieces = []
    for i in range(rows):
        cut = slice(i * block, (i + 1) * block)
        piece = scratch[0][:, cut].astype(F32)
        for other in scratch[1:]:
            piece = piece * other[:, cut].astype(F32)
        pieces.append(piece)
    stacked = jnp.concatenate(pieces, axis=0).astype(BF16)
    ordered = jnp.dot(order, stacked, preferred_element_type=F32).astype(BF16)
    ordered = ordered.reshape(2, channels, half, block)
    own[pl.ds(place, channels)] = ordered[0]
    send[...] = ordered[1]
    if rows_copy is not None:
        rows_copy.wait()


def as_rows(core, block, *arrays, spectrum=None):
    channels, tokens = arrays[0].shape
    half = tokens // block // 2
    room, extra, shapes = 1, [], []
    if spectrum is not None:
        two, _, a_here, _ = spectrum.shape
        room, extra = 2, [spectrum]
        shapes = [jax.ShapeDtypeStruct((two, channels, a_here // 2, block), BF16)]
    return pl.pallas_call(
        functools.partial(product_kernel, block, len(arrays)),
        out_shape=[
            jax.ShapeDtypeStruct((room * channels, half, block), BF16),
            jax.ShapeDtypeStruct((channels, half, block), BF16),
        ]
        + shapes,
        in_specs=[SMEM] + [ANY] * len(arrays + tuple(extra)),
        out_specs=[VMEM] * (2 + len(shapes)),
        scratch_shapes=[pltpu.VMEM((channels, tokens), BF16)] * len(arrays)
        + [pltpu.SemaphoreType.DMA((len(arrays) + 1,))],
        cost_estimate=SMALL,
    )(core, *arrays, *extra)


def spectrum_kernel(core_ref, in_ref, came_ref, order_ref, *refs):
    moved, rows, came, order, sem = refs
    core = core_ref[0]
    two, channels, a_half, block = rows.shape
    at = pl.ds(pl.multiple_of(core * a_half, a_half), a_half)
    copies = [
        pltpu.make_async_copy(order_ref, order, sem.at[0]),
        pltpu.make_async_copy(in_ref.at[:, :, at, :], rows, sem.at[1]),
        pltpu.make_async_copy(came_ref, came, sem.at[2]),
    ]
    for copy in copies:
        copy.start()
    copies[0].wait()
    quarter = block // 4
    step = quarter // 4
    for side, ref in ((core, rows), (1 - core, came)):
        copies[1 if ref is rows else 2].wait()
        flat = jnp.concatenate([ref[n, c] for c in range(channels) for n in range(two)], 0)
        parts = [
            jnp.dot(flat[:, q * quarter : (q + 1) * quarter], order[...], preferred_element_type=F32)
            for q in range(4)
        ]
        for rho in range(4):
            columns = [part[:, rho * step : (rho + 1) * step] for part in parts]
            columns = jnp.concatenate(columns, axis=1).astype(BF16)
            moved[pl.ds(channels * side, channels), :, :, rho * quarter : (rho + 1) * quarter] = (
                columns.reshape(channels, two, a_half, quarter)
            )


def arrange_spectrum(core, spectrum, came, order):
    two, channels, a_half, block = came.shape
    return pl.pallas_call(
        spectrum_kernel,
        out_shape=jax.ShapeDtypeStruct((2 * channels, two, a_half, block), BF16),
        in_specs=[SMEM, ANY, ANY, ANY],
        out_specs=VMEM,
        scratch_shapes=[
            pltpu.VMEM(came.shape, BF16),
            pltpu.VMEM(came.shape, BF16),
            pltpu.VMEM(order.shape, BF16),
            pltpu.SemaphoreType.DMA((3,)),
        ],
        cost_estimate=SMALL,
    )(core, spectrum, came, order)


def weight_kernel(rows, core_ref, weight, out):
    channels, outs = weight.shape
    half = outs // 2
    core = core_ref[0]
    shape = out.shape
    to = lax.broadcasted_iota(jnp.int32, (shape[0], outs), 0)
    at = lax.broadcasted_iota(jnp.int32, (shape[0], outs), 1)
    column = jnp.bitwise_xor(to // (rows * half), core) * half + to % half
    pick = jnp.where(at == column, 1.0, 0.0).astype(BF16)
    turned = lax.dot_general(
        pick, weight[...], (((1,), (1,)), ((), ())), preferred_element_type=F32
    ).astype(BF16)
    to = lax.broadcasted_iota(jnp.int32, (channels, shape[1]), 0)
    at = lax.broadcasted_iota(jnp.int32, (channels, shape[1]), 1)
    channel = (at // rows + core * (channels // 2)) % channels
    widen = jnp.where(channel == to, 1.0, 0.0).astype(BF16)
    wide = jnp.dot(turned, widen, preferred_element_type=F32)
    to = lax.broadcasted_iota(jnp.int32, shape, 0)
    at = lax.broadcasted_iota(jnp.int32, shape, 1)
    out[...] = jnp.where(at % rows == (to // half) % rows, wide, 0.0).astype(BF16)


def projection(core, weight, rows):
    channels, outs = weight.shape
    return pl.pallas_call(
        functools.partial(weight_kernel, rows),
        out_shape=jax.ShapeDtypeStruct((rows * outs, rows * channels), BF16),
        in_specs=[SMEM, VMEM],
        out_specs=VMEM,
        compiler_params=pltpu.CompilerParams(vmem_limit_bytes=4 * MIB),
    )(core, weight)


def butterflies(values, sign):
    (r0, i0), (r1, i1), (r2, i2), (r3, i3) = values
    er, ei, dr, di = r0 + r2, i0 + i2, r0 - r2, i0 - i2
    fr, fi, hr, hi = r1 + r3, i1 + i3, r1 - r3, i1 - i3
    plus, minus = (dr - hi, di + hr), (dr + hi, di - hr)
    if sign < 0:
        plus, minus = minus, plus
    return [(er + fr, ei + fi), plus, (er - fr, ei - fi), minus]


def turn(values, cosine, sine):
    real, imag = values
    rows = real.shape[0]
    both = jnp.concatenate([real.astype(BF16), imag.astype(BF16)], axis=0)
    with_cosine = jnp.dot(both, cosine, preferred_element_type=F32)
    with_sine = jnp.dot(both, sine, preferred_element_type=F32)
    return with_cosine[:rows], with_cosine[rows:], with_sine[:rows], with_sine[rows:]


def full_turns(turns, rows):
    def whole(kind, which):
        cut = slice(kind * rows, (kind + 1) * rows)
        part = lambda n: turns[n // 2, cut, pl.ds((2 * (n % 2) + which) * 128, 128)].astype(F32)
        return part(0) + part(1) + part(2)

    return (whole(0, 0), whole(0, 1)), (whole(1, 0), whole(1, 1))


def pair_of(inner, rho, way):
    quarter = inner.shape[-1] // 2
    four = inner[rho].reshape(4, quarter, quarter)
    return four[2 * way], four[2 * way + 1]


def transform_kernel(place_ref, *refs):
    ins, (send, keep, signal, spec, first, last, inner, turns, twist, sem) = refs[:-10], refs[-10:]
    *pieces, spec_in, table = ins
    place = place_ref[0]
    count = pieces[0].shape[0]
    size = turns.shape[0]
    moves = [(table.at[place], first)]
    moves += [(ref, signal.at[pl.ds(n * count, count)]) for n, ref in enumerate(pieces)]
    moves += [(table.at[pl.ds(12 + size * place, size)], turns)]
    moves += [(table.at[pl.ds(8, 4)], inner), (spec_in, spec), (table.at[4 + place], last)]
    copies = [pltpu.make_async_copy(*move, sem.at[n]) for n, move in enumerate(moves)]
    for copy in copies:
        copy.start()
    for copy in copies[:6]:
        copy.wait()
    block = signal.shape[-1]
    quarter = block // 4
    lines = signal[...].reshape(-1, block)
    a_rows = first.shape[0] // 2
    coarse, fine = full_turns(turns, a_rows)
    turned = []
    for q in range(4):
        cut = slice(q * quarter, (q + 1) * quarter)
        both = jnp.dot(first[...], lines[:, cut], preferred_element_type=F32)
        for h in range(q * quarter // 128, (q + 1) * quarter // 128):
            lanes = slice(128 * h, 128 * (h + 1))
            uc, us = coarse[0][:, h : h + 1], coarse[1][:, h : h + 1]
            twist[0, :, lanes] = uc * fine[0] - us * fine[1]
            twist[1, :, lanes] = us * fine[0] + uc * fine[1]
        real, imag = both[:a_rows], both[a_rows:]
        cosine, sine = twist[0, :, cut], twist[1, :, cut]
        turned.append((real * cosine + imag * sine, imag * cosine - real * sine))
    mixes = butterflies(turned, -1)
    for copy in copies[6:-1]:
        copy.wait()
    backs = []
    for rho in range(4):
        rc, ic, rs, si = turn(mixes[rho], *pair_of(inner, rho, 0))
        zr, zi = rc + si, ic - rs
        cut = slice(rho * quarter, (rho + 1) * quarter)
        gr = spec[:, 0, :, cut].reshape(-1, quarter).astype(F32)
        gi = spec[:, 1, :, cut].reshape(-1, quarter).astype(F32)
        shaped = (zr * gr - zi * gi, zr * gi + zi * gr)
        rc, ic, rs, si = turn(shaped, *pair_of(inner, rho, 1))
        backs.append((rc - si, ic + rs))
    mixes = butterflies(backs, 1)
    scale = 1.0 / (block * block)
    half = last.shape[0] // 2
    copies[-1].wait()
    for q, (real, imag) in enumerate(mixes):
        cut = slice(q * quarter, (q + 1) * quarter)
        cosine, sine = twist[0, :, cut], twist[1, :, cut]
        pair = jnp.concatenate(
            [
                (real * cosine - imag * sine).astype(BF16),
                (imag * cosine + real * sine).astype(BF16),
            ],
            axis=0,
        )
        out = jnp.dot(last[...], pair, preferred_element_type=F32) * scale
        send[:, :, cut] = out[:half].astype(BF16).reshape(send.shape[0], send.shape[1], quarter)
        keep[:, :, cut] = out[half:].astype(BF16).reshape(keep.shape[0], keep.shape[1], quarter)


def transform(place, pieces, spec, table):
    members, rows_half, block = pieces[0].shape
    a_rows = spec.shape[0] * spec.shape[2]
    out = (2 * members, rows_half, block)
    square = table.shape[1:]
    return pl.pallas_call(
        transform_kernel,
        in_specs=[SMEM] + [ANYWHERE] * (len(pieces) + 1) + [ANY],
        out_specs=[VMEM, VMEM],
        out_shape=[jax.ShapeDtypeStruct(out, BF16)] * 2,
        scratch_shapes=[
            pltpu.VMEM((4 * members, rows_half, block), BF16),
            pltpu.VMEM(spec.shape, BF16),
            pltpu.VMEM(square, BF16),
            pltpu.VMEM(square, BF16),
            pltpu.VMEM((4,) + square, BF16),
            pltpu.VMEM(((table.shape[0] - 12) // 4,) + square, BF16),
            pltpu.VMEM((2, a_rows, block), F32),
            pltpu.SemaphoreType.DMA((len(pieces) + 5,)),
        ],
        compiler_params=pltpu.CompilerParams(vmem_limit_bytes=48 * MIB),
        cost_estimate=SMALL,
    )(place, *pieces, spec, table)


def gate_kernel(core_ref, conv, prod, gate, gate_other, skip, skip_other, weight, keep, send):
    here, _, rows, block = conv.shape
    core = core_ref[0]
    pieces = []
    for side, (values, gains) in enumerate(((gate, skip), (gate_other, skip_other))):
        for n in range(here):
            high = jnp.bitwise_xor(core, side)
            total = conv[n, 2 * high].astype(F32) + conv[here - 1 - n, 2 * high + 1].astype(F32)
            total = total + gains[n] * prod[high * here + n].astype(F32)
            pieces.append((values[n].astype(F32) * total).astype(BF16))
    gated = jnp.concatenate(pieces, axis=0)
    mixed = jnp.dot(weight[...], gated, preferred_element_type=F32)
    outs = keep.shape[0]
    for r in range(rows):
        cut = slice(r * block, (r + 1) * block)
        keep[:, cut] = mixed[r * outs : (r + 1) * outs].astype(BF16)
        send[:, cut] = mixed[(rows + r) * outs : (rows + r + 1) * outs].astype(BF16)


def gate_and_project(core, conv, prod, gate, gate_other, skip, skip_other, weight):
    _, _, rows, block = conv.shape
    outs = weight.shape[0] // (2 * rows)
    return pl.pallas_call(
        gate_kernel,
        out_shape=[jax.ShapeDtypeStruct((outs, rows * block), BF16)] * 2,
        in_specs=[SMEM, VMEM, VMEM, VMEM, VMEM, SMEM, SMEM, VMEM],
        out_specs=[VMEM, VMEM],
        compiler_params=pltpu.CompilerParams(vmem_limit_bytes=16 * MIB),
        cost_estimate=SMALL,
    )(core, conv, prod, gate, gate_other, skip, skip_other, weight)


def local_channels(k_feature, v_feature, q_feature, spectrum, skip_gain, out_weight):
    channels, tokens = k_feature.shape
    block = spectrum.shape[3]
    ctx_count = lax.axis_size("ctx")
    members = ctx_count // 2
    rows_half = tokens // block // 2
    a_half = spectrum.shape[2] // 2
    ctx, tp = lax.axis_index("ctx"), lax.axis_index("tp")
    core = tp.astype(jnp.int32).reshape(1)
    member = (ctx % members).astype(jnp.int32).reshape(1)
    place = (ctx // members * 2 + tp).astype(jnp.int32).reshape(1)
    tables = {
        name: jnp.asarray(table)
        for name, table in constant_tables(block, members, rows_half, a_half).items()
    }
    halves = [list(range(members)), list(range(members, 2 * members))]
    spread = lambda x: lax.all_to_all(x, "ctx", 0, 0, axis_index_groups=halves, tiled=True)
    across = lambda x: lax.ppermute(
        x, "ctx", [(d, (d + members) % ctx_count) for d in range(ctx_count)]
    )
    swap = lambda x: lax.ppermute(x, "tp", [(0, 1), (1, 0)])

    def joined(own, sent):
        start = ((1 - tp) * channels,) + (0,) * (own.ndim - 1)
        return lax.dynamic_update_slice(own, swap(sent), start)

    own, sent, other_rows = as_rows(core, block, k_feature, v_feature, spectrum=spectrum)
    product = joined(own, sent)
    product, spectrum, other_rows = lax.optimization_barrier((product, spectrum, other_rows))
    xa = spread(product)
    spec = arrange_spectrum(core, spectrum, swap(other_rows), tables["order"])
    xa, spec, q_feature, skip_gain, out_weight = lax.optimization_barrier(
        (xa, spec, q_feature, skip_gain, out_weight)
    )
    xb = swap(xa)
    za = across(xa)
    spec = spread(spec)
    gate, gate_sent = as_rows(core, block, q_feature)
    gate_other = swap(gate_sent)
    skip_other = swap(skip_gain)
    weight = projection(core, out_weight, rows_half)
    za, gate, gate_other, skip_other, weight = lax.optimization_barrier(
        (za, gate, gate_other, skip_other, weight)
    )
    zb = swap(za)

    send, keep = transform(place, (xa, xb, za, zb), spec, tables["transform"])
    total = (keep.astype(F32) + swap(send).astype(F32)).astype(BF16)
    conv = lax.all_to_all(
        total, "ctx", 0, 0, axis_index_groups=[last_order(members)], tiled=True
    ).reshape(channels, 4, rows_half, block)
    kept, sent = gate_and_project(
        core, conv, product, gate, gate_other, skip_gain, skip_other, weight
    )
    came = swap(sent)
    low = jnp.where(tp == 0, kept, came)
    high = jnp.where(tp == 0, came, kept)
    return jnp.concatenate([low, high], axis=1)


def local(k_feature, v_feature, q_feature, spectrum, skip_gain, out_weight):
    channels, tokens = k_feature.shape
    block = spectrum.shape[3]
    ctx_count, tp_count = lax.axis_size("ctx"), lax.axis_size("tp")
    by_channels = (
        tp_count == 2
        and ctx_count == 2 * channels * tp_count
        and tokens * ctx_count * 2 == block * block
        and tokens % (32 * block) == 0
        and spectrum.shape[2] % 32 == 0
        and block % 512 == 0
        and out_weight.shape[1] % 16 == 0
    )
    plan = local_channels if by_channels else local_general
    return plan(k_feature, v_feature, q_feature, spectrum, skip_gain, out_weight)


def solution(mesh):
    placed = (
        P("tp", "ctx"),
        P("tp", "ctx"),
        P("tp", "ctx"),
        P(None, "tp", "ctx", None),
        P("tp"),
        P(),
    )
    return jax.shard_map(
        local, mesh=mesh, in_specs=placed, out_specs=P("tp", "ctx"), check_vma=False
    )
```

```python
import functools
import math

import numpy as np
import ml_dtypes
import jax
import jax.numpy as jnp
from jax import lax
from jax.experimental import pallas as pl
from jax.experimental.pallas import tpu as pltpu
from jax.sharding import PartitionSpec as P

F32 = jnp.float32
BF16 = jnp.bfloat16
VMEM = pl.BlockSpec(memory_space=pltpu.VMEM)
SMEM = pl.BlockSpec(memory_space=pltpu.SMEM)
ANY = pl.BlockSpec(memory_space=pltpu.HBM)
ANYWHERE = pl.BlockSpec(memory_space=pl.ANY)
MIB = 1 << 20
SMALL = pl.CostEstimate(flops=1, bytes_accessed=1, transcendentals=0)


def fourier_tables(length_all):
    positions = jnp.arange(length_all, dtype=jnp.int32)
    phase_index = positions[:, None] * positions[None, :] % length_all
    angles = phase_index.astype(jnp.float32) * (2.0 * math.pi / length_all)
    return (jnp.cos(angles).astype(jnp.bfloat16), jnp.sin(angles).astype(jnp.bfloat16))


def twist_tables(left_index, right_index, length_all):
    phase_index = left_index[:, None] * right_index[None, :] % length_all
    angles = phase_index.astype(jnp.float32) * (2.0 * math.pi / length_all)
    return (jnp.cos(angles), jnp.sin(angles))


def contract(form, left, right):
    return jnp.einsum(form, left, right, preferred_element_type=jnp.float32)


def local_general(k_feature, v_feature, q_feature, spectrum, skip_gain, out_weight):
    channels, tokens = k_feature.shape
    block_order = spectrum.shape[3]
    length_all = block_order * block_order
    ctx_count = lax.axis_size("ctx")
    slab_width = block_order // ctx_count
    rows_here = tokens // block_order
    ctx_index = lax.axis_index("ctx")
    product = (k_feature.astype(jnp.float32) * v_feature.astype(jnp.float32)).astype(jnp.bfloat16)
    cosine_full, sine_full = fourier_tables(block_order)
    cosine_half = cosine_full[: block_order // 2]
    sine_half = sine_full[: block_order // 2]
    positions = jnp.arange(block_order, dtype=jnp.int32)
    local_ticks = ctx_index * slab_width + jnp.arange(slab_width, dtype=jnp.int32)
    grid_rows = lax.all_to_all(
        product.reshape(channels, rows_here, block_order),
        "ctx",
        split_axis=2,
        concat_axis=1,
        tiled=True,
    )
    first_real = contract("cij,ia->caj", grid_rows, cosine_half)
    first_imag = -contract("cij,ia->caj", grid_rows, sine_half)
    twist_cosine, twist_sine = twist_tables(positions, local_ticks, length_all)
    spread_real = (first_real * twist_cosine + first_imag * twist_sine).astype(jnp.bfloat16)
    spread_imag = (first_imag * twist_cosine - first_real * twist_sine).astype(jnp.bfloat16)
    block_real, block_imag = (
        lax.all_to_all(spread_real, "ctx", split_axis=1, concat_axis=2, tiled=True),
        lax.all_to_all(spread_imag, "ctx", split_axis=1, concat_axis=2, tiled=True),
    )
    freq_real = contract("caj,jb->cab", block_real, cosine_full) + contract(
        "caj,jb->cab", block_imag, sine_full
    )
    freq_imag = contract("caj,jb->cab", block_imag, cosine_full) - contract(
        "caj,jb->cab", block_real, sine_full
    )
    resp_real = spectrum[0].astype(jnp.float32)
    resp_imag = spectrum[1].astype(jnp.float32)
    shaped_real = (freq_real * resp_real - freq_imag * resp_imag).astype(jnp.bfloat16)
    shaped_imag = (freq_real * resp_imag + freq_imag * resp_real).astype(jnp.bfloat16)
    inner_real = contract("cab,bj->caj", shaped_real, cosine_full) - contract(
        "cab,bj->caj", shaped_imag, sine_full
    )
    inner_imag = contract("cab,bj->caj", shaped_imag, cosine_full) + contract(
        "cab,bj->caj", shaped_real, sine_full
    )
    twist_cosine, twist_sine = twist_tables(local_ticks, positions, length_all)
    back_real = (inner_real * twist_cosine - inner_imag * twist_sine).astype(jnp.bfloat16)
    back_imag = (inner_imag * twist_cosine + inner_real * twist_sine).astype(jnp.bfloat16)
    summed = contract(
        "ia,caj->cij",
        cosine_half,
        lax.all_to_all(back_real, "ctx", split_axis=2, concat_axis=1, tiled=True),
    ) - contract(
        "ia,caj->cij",
        sine_half,
        lax.all_to_all(back_imag, "ctx", split_axis=2, concat_axis=1, tiled=True),
    )
    spatial = (summed * (1.0 / length_all)).astype(jnp.bfloat16)
    convolved = lax.all_to_all(spatial, "ctx", split_axis=1, concat_axis=2, tiled=True).reshape(
        channels, tokens
    )
    gated_rows = (
        q_feature.astype(jnp.float32)
        * (convolved.astype(jnp.float32) + skip_gain[:, None] * product.astype(jnp.float32))
    ).astype(jnp.bfloat16)
    tp_index = lax.axis_index("tp")
    my_weight = lax.dynamic_slice_in_dim(out_weight, tp_index * channels, channels, 0)
    return lax.psum_scatter(
        jnp.dot(my_weight.T, gated_rows, preferred_element_type=jnp.float32).astype(jnp.bfloat16),
        "tp",
        scatter_dimension=0,
        tiled=True,
    )


def cosine_sine(product, length):
    angles = (product % length).astype(np.float64) * (2.0 * np.pi / length)
    return np.cos(angles), np.sin(angles)


def last_order(members):
    size = members // 2
    turns = lambda n: (2 * size + n, size - 1 - n, 3 * size + n, 2 * size - 1 - n)
    return [device for n in range(size) for device in turns(n)]


@functools.lru_cache(maxsize=None)
def constant_tables(block, members, rows_half, a_half):
    quarter = block // 4
    firsts, lasts, coarses, fines = [], [], [], []
    part = np.arange(members)
    for g in range(2):
        for s in range(2):
            a = (
                (g * members + part)[:, None] * 2 * a_half
                + s * a_half
                + np.arange(a_half)[None, :]
            ).reshape(-1)

            def rows(group, core):
                device = group * members + part
                i = device[:, None] * 2 * rows_half + core * rows_half
                return (i + np.arange(rows_half)[None, :]).reshape(-1)

            i_in = np.concatenate([rows(g, s), rows(g, 1 - s), rows(1 - g, s), rows(1 - g, 1 - s)])
            cosine, sine = cosine_sine(a[:, None] * i_in[None, :], block)
            firsts.append(np.concatenate([cosine, -sine], 0))
            place = last_order(members)

            def by_place(core):
                i = np.concatenate([rows(0, core), rows(1, core)])
                return i.reshape(2 * members, -1)[place].reshape(-1)

            i_out = np.concatenate([by_place(1 - s), by_place(s)])
            cosine, sine = cosine_sine(i_out[:, None] * a[None, :], block)
            lasts.append(np.concatenate([cosine, -sine], 1))
            coarse = 128 * (np.arange(128) % (block // 128))
            coarses.append(np.stack(cosine_sine(a[:, None] * coarse[None, :], block * block)))
            fines.append(np.stack(cosine_sine(a[:, None] * np.arange(128)[None, :], block * block)))
    inner = []
    for rho in range(4):
        cosine, sine = cosine_sine(
            np.arange(quarter)[:, None] * (4 * np.arange(quarter) + rho)[None, :], block
        )
        inner.append(np.stack([cosine, sine, cosine.T, sine.T]))
    order = np.zeros((quarter, quarter), np.float32)
    b = np.arange(quarter)
    order[b, (b % 4) * (quarter // 4) + b // 4] = 1.0
    narrow = lambda x: np.asarray(x, np.float32).astype(ml_dtypes.bfloat16)
    rest = np.stack([coarses, fines], 1).astype(np.float32)
    turns = []
    for _ in range(3):
        turns.append(narrow(rest))
        rest = rest - turns[-1].astype(np.float32)
    turns = np.stack(turns + [np.zeros_like(turns[0])], 1).transpose(0, 2, 4, 1, 3, 5)
    turns = turns.reshape(4, 2 * turns.shape[2], 2, 2 * quarter).transpose(0, 2, 1, 3)
    square = (-1, 2 * quarter, 2 * quarter)
    entries = [np.stack(firsts), np.stack(lasts), np.stack(inner).reshape(square)]
    return dict(
        transform=np.concatenate([narrow(x) for x in entries] + [turns.reshape(square)]),
        order=narrow(order),
    )


def product_kernel(block, count, core_ref, *refs):
    ins, outs, scratch, sem = refs[:count], refs[count:-1 - count], refs[-1 - count : -1], refs[-1]
    copies = [pltpu.make_async_copy(ins[n], scratch[n], sem.at[n]) for n in range(count)]
    for copy in copies:
        copy.start()
    rows_copy = None
    if len(outs) == 4:
        spectrum, own, send, other_rows = outs
        a_half = other_rows.shape[2]
        at = pl.ds(pl.multiple_of((1 - core_ref[0]) * a_half, a_half), a_half)
        rows_copy = pltpu.make_async_copy(spectrum.at[:, :, at, :], other_rows, sem.at[count])
        rows_copy.start()
    else:
        own, send = outs
    core = core_ref[0]
    channels, tokens = ins[0].shape
    place = 0 if own.shape[0] == channels else channels * core
    rows = tokens // block
    half = rows // 2
    to = lax.broadcasted_iota(jnp.int32, (channels * rows, channels * rows), 0)
    at = lax.broadcasted_iota(jnp.int32, (channels * rows, channels * rows), 1)
    side = jnp.bitwise_xor(to // (channels * half), core)
    source = (side * half + to % half) * channels + (to // half) % channels
    order = jnp.where(at == source, 1.0, 0.0).astype(BF16)
    for copy in copies:
        copy.wait()
    pieces = []
    for i in range(rows):
        cut = slice(i * block, (i + 1) * block)
        piece = scratch[0][:, cut].astype(F32)
        for other in scratch[1:]:
            piece = piece * other[:, cut].astype(F32)
        pieces.append(piece)
    stacked = jnp.concatenate(pieces, axis=0).astype(BF16)
    ordered = jnp.dot(order, stacked, preferred_element_type=F32).astype(BF16)
    ordered = ordered.reshape(2, channels, half, block)
    own[pl.ds(place, channels)] = ordered[0]
    send[...] = ordered[1]
    if rows_copy is not None:
        rows_copy.wait()


def as_rows(core, block, *arrays, spectrum=None):
    channels, tokens = arrays[0].shape
    half = tokens // block // 2
    room, extra, shapes = 1, [], []
    if spectrum is not None:
        two, _, a_here, _ = spectrum.shape
        room, extra = 2, [spectrum]
        shapes = [jax.ShapeDtypeStruct((two, channels, a_here // 2, block), BF16)]
    return pl.pallas_call(
        functools.partial(product_kernel, block, len(arrays)),
        out_shape=[
            jax.ShapeDtypeStruct((room * channels, half, block), BF16),
            jax.ShapeDtypeStruct((channels, half, block), BF16),
        ]
        + shapes,
        in_specs=[SMEM] + [ANY] * len(arrays + tuple(extra)),
        out_specs=[VMEM] * (2 + len(shapes)),
        scratch_shapes=[pltpu.VMEM((channels, tokens), BF16)] * len(arrays)
        + [pltpu.SemaphoreType.DMA((len(arrays) + 1,))],
        cost_estimate=SMALL,
    )(core, *arrays, *extra)


def spectrum_kernel(core_ref, in_ref, came_ref, order_ref, *refs):
    moved, rows, came, order, sem = refs
    core = core_ref[0]
    two, channels, a_half, block = rows.shape
    at = pl.ds(pl.multiple_of(core * a_half, a_half), a_half)
    copies = [
        pltpu.make_async_copy(order_ref, order, sem.at[0]),
        pltpu.make_async_copy(in_ref.at[:, :, at, :], rows, sem.at[1]),
        pltpu.make_async_copy(came_ref, came, sem.at[2]),
    ]
    for copy in copies:
        copy.start()
    copies[0].wait()
    quarter = block // 4
    step = quarter // 4
    for side, ref in ((core, rows), (1 - core, came)):
        copies[1 if ref is rows else 2].wait()
        flat = jnp.concatenate([ref[n, c] for c in range(channels) for n in range(two)], 0)
        parts = [
            jnp.dot(flat[:, q * quarter : (q + 1) * quarter], order[...], preferred_element_type=F32)
            for q in range(4)
        ]
        for rho in range(4):
            columns = [part[:, rho * step : (rho + 1) * step] for part in parts]
            columns = jnp.concatenate(columns, axis=1).astype(BF16)
            moved[pl.ds(channels * side, channels), :, :, rho * quarter : (rho + 1) * quarter] = (
                columns.reshape(channels, two, a_half, quarter)
            )


def arrange_spectrum(core, spectrum, came, order):
    two, channels, a_half, block = came.shape
    return pl.pallas_call(
        spectrum_kernel,
        out_shape=jax.ShapeDtypeStruct((2 * channels, two, a_half, block), BF16),
        in_specs=[SMEM, ANY, ANY, ANY],
        out_specs=VMEM,
        scratch_shapes=[
            pltpu.VMEM(came.shape, BF16),
            pltpu.VMEM(came.shape, BF16),
            pltpu.VMEM(order.shape, BF16),
            pltpu.SemaphoreType.DMA((3,)),
        ],
        cost_estimate=SMALL,
    )(core, spectrum, came, order)


def weight_kernel(rows, core_ref, weight, out):
    channels, outs = weight.shape
    half = outs // 2
    core = core_ref[0]
    shape = out.shape
    to = lax.broadcasted_iota(jnp.int32, (shape[0], outs), 0)
    at = lax.broadcasted_iota(jnp.int32, (shape[0], outs), 1)
    column = jnp.bitwise_xor(to // (rows * half), core) * half + to % half
    pick = jnp.where(at == column, 1.0, 0.0).astype(BF16)
    turned = lax.dot_general(
        pick, weight[...], (((1,), (1,)), ((), ())), preferred_element_type=F32
    ).astype(BF16)
    to = lax.broadcasted_iota(jnp.int32, (channels, shape[1]), 0)
    at = lax.broadcasted_iota(jnp.int32, (channels, shape[1]), 1)
    channel = (at // rows + core * (channels // 2)) % channels
    widen = jnp.where(channel == to, 1.0, 0.0).astype(BF16)
    wide = jnp.dot(turned, widen, preferred_element_type=F32)
    to = lax.broadcasted_iota(jnp.int32, shape, 0)
    at = lax.broadcasted_iota(jnp.int32, shape, 1)
    out[...] = jnp.where(at % rows == (to // half) % rows, wide, 0.0).astype(BF16)


def projection(core, weight, rows):
    channels, outs = weight.shape
    return pl.pallas_call(
        functools.partial(weight_kernel, rows),
        out_shape=jax.ShapeDtypeStruct((rows * outs, rows * channels), BF16),
        in_specs=[SMEM, VMEM],
        out_specs=VMEM,
        compiler_params=pltpu.CompilerParams(vmem_limit_bytes=4 * MIB),
    )(core, weight)


def butterflies(values, sign):
    (r0, i0), (r1, i1), (r2, i2), (r3, i3) = values
    er, ei, dr, di = r0 + r2, i0 + i2, r0 - r2, i0 - i2
    fr, fi, hr, hi = r1 + r3, i1 + i3, r1 - r3, i1 - i3
    plus, minus = (dr - hi, di + hr), (dr + hi, di - hr)
    if sign < 0:
        plus, minus = minus, plus
    return [(er + fr, ei + fi), plus, (er - fr, ei - fi), minus]


def turn(values, cosine, sine):
    real, imag = values
    rows = real.shape[0]
    both = jnp.concatenate([real.astype(BF16), imag.astype(BF16)], axis=0)
    with_cosine = jnp.dot(both, cosine, preferred_element_type=F32)
    with_sine = jnp.dot(both, sine, preferred_element_type=F32)
    return with_cosine[:rows], with_cosine[rows:], with_sine[:rows], with_sine[rows:]


def full_turns(turns, rows):
    def whole(kind, which):
        cut = slice(kind * rows, (kind + 1) * rows)
        part = lambda n: turns[n // 2, cut, pl.ds((2 * (n % 2) + which) * 128, 128)].astype(F32)
        return part(0) + part(1) + part(2)

    return (whole(0, 0), whole(0, 1)), (whole(1, 0), whole(1, 1))


def pair_of(inner, rho, way):
    quarter = inner.shape[-1] // 2
    four = inner[rho].reshape(4, quarter, quarter)
    return four[2 * way], four[2 * way + 1]


def transform_kernel(place_ref, *refs):
    ins, (send, keep, signal, spec, first, last, inner, turns, twist, sem) = refs[:-10], refs[-10:]
    *pieces, spec_in, table = ins
    place = place_ref[0]
    count = pieces[0].shape[0]
    size = turns.shape[0]
    moves = [(table.at[place], first)]
    moves += [(ref, signal.at[pl.ds(n * count, count)]) for n, ref in enumerate(pieces)]
    moves += [(table.at[pl.ds(12 + size * place, size)], turns)]
    moves += [(table.at[pl.ds(8, 4)], inner), (spec_in, spec), (table.at[4 + place], last)]
    copies = [pltpu.make_async_copy(*move, sem.at[n]) for n, move in enumerate(moves)]
    for copy in copies:
        copy.start()
    for copy in copies[:6]:
        copy.wait()
    block = signal.shape[-1]
    quarter = block // 4
    lines = signal[...].reshape(-1, block)
    a_rows = first.shape[0] // 2
    coarse, fine = full_turns(turns, a_rows)
    turned = []
    for q in range(4):
        cut = slice(q * quarter, (q + 1) * quarter)
        both = jnp.dot(first[...], lines[:, cut], preferred_element_type=F32)
        for h in range(q * quarter // 128, (q + 1) * quarter // 128):
            lanes = slice(128 * h, 128 * (h + 1))
            uc, us = coarse[0][:, h : h + 1], coarse[1][:, h : h + 1]
            twist[0, :, lanes] = uc * fine[0] - us * fine[1]
            twist[1, :, lanes] = us * fine[0] + uc * fine[1]
        real, imag = both[:a_rows], both[a_rows:]
        cosine, sine = twist[0, :, cut], twist[1, :, cut]
        turned.append((real * cosine + imag * sine, imag * cosine - real * sine))
    mixes = butterflies(turned, -1)
    for copy in copies[6:-1]:
        copy.wait()
    backs = []
    for rho in range(4):
        rc, ic, rs, si = turn(mixes[rho], *pair_of(inner, rho, 0))
        zr, zi = rc + si, ic - rs
        cut = slice(rho * quarter, (rho + 1) * quarter)
        gr = spec[:, 0, :, cut].reshape(-1, quarter).astype(F32)
        gi = spec[:, 1, :, cut].reshape(-1, quarter).astype(F32)
        shaped = (zr * gr - zi * gi, zr * gi + zi * gr)
        rc, ic, rs, si = turn(shaped, *pair_of(inner, rho, 1))
        backs.append((rc - si, ic + rs))
    mixes = butterflies(backs, 1)
    scale = 1.0 / (block * block)
    half = last.shape[0] // 2
    copies[-1].wait()
    for q, (real, imag) in enumerate(mixes):
        cut = slice(q * quarter, (q + 1) * quarter)
        cosine, sine = twist[0, :, cut], twist[1, :, cut]
        pair = jnp.concatenate(
            [
                (real * cosine - imag * sine).astype(BF16),
                (imag * cosine + real * sine).astype(BF16),
            ],
            axis=0,
        )
        out = jnp.dot(last[...], pair, preferred_element_type=F32) * scale
        send[:, :, cut] = out[:half].astype(BF16).reshape(send.shape[0], send.shape[1], quarter)
        keep[:, :, cut] = out[half:].astype(BF16).reshape(keep.shape[0], keep.shape[1], quarter)


def transform(place, pieces, spec, table):
    members, rows_half, block = pieces[0].shape
    a_rows = spec.shape[0] * spec.shape[2]
    out = (2 * members, rows_half, block)
    square = table.shape[1:]
    return pl.pallas_call(
        transform_kernel,
        in_specs=[SMEM] + [ANYWHERE] * (len(pieces) + 1) + [ANY],
        out_specs=[VMEM, VMEM],
        out_shape=[jax.ShapeDtypeStruct(out, BF16)] * 2,
        scratch_shapes=[
            pltpu.VMEM((4 * members, rows_half, block), BF16),
            pltpu.VMEM(spec.shape, BF16),
            pltpu.VMEM(square, BF16),
            pltpu.VMEM(square, BF16),
            pltpu.VMEM((4,) + square, BF16),
            pltpu.VMEM(((table.shape[0] - 12) // 4,) + square, BF16),
            pltpu.VMEM((2, a_rows, block), F32),
            pltpu.SemaphoreType.DMA((len(pieces) + 5,)),
        ],
        compiler_params=pltpu.CompilerParams(vmem_limit_bytes=48 * MIB),
        cost_estimate=SMALL,
    )(place, *pieces, spec, table)


def gate_kernel(core_ref, conv, prod, gate, gate_other, skip, skip_other, weight, keep, send):
    here, _, rows, block = conv.shape
    core = core_ref[0]
    pieces = []
    for side, (values, gains) in enumerate(((gate, skip), (gate_other, skip_other))):
        for n in range(here):
            high = jnp.bitwise_xor(core, side)
            total = conv[n, 2 * high].astype(F32) + conv[here - 1 - n, 2 * high + 1].astype(F32)
            total = total + gains[n] * prod[high * here + n].astype(F32)
            pieces.append((values[n].astype(F32) * total).astype(BF16))
    gated = jnp.concatenate(pieces, axis=0)
    mixed = jnp.dot(weight[...], gated, preferred_element_type=F32)
    outs = keep.shape[0]
    for r in range(rows):
        cut = slice(r * block, (r + 1) * block)
        keep[:, cut] = mixed[r * outs : (r + 1) * outs].astype(BF16)
        send[:, cut] = mixed[(rows + r) * outs : (rows + r + 1) * outs].astype(BF16)


def gate_and_project(core, conv, prod, gate, gate_other, skip, skip_other, weight):
    _, _, rows, block = conv.shape
    outs = weight.shape[0] // (2 * rows)
    return pl.pallas_call(
        gate_kernel,
        out_shape=[jax.ShapeDtypeStruct((outs, rows * block), BF16)] * 2,
        in_specs=[SMEM, VMEM, VMEM, VMEM, VMEM, SMEM, SMEM, VMEM],
        out_specs=[VMEM, VMEM],
        compiler_params=pltpu.CompilerParams(vmem_limit_bytes=16 * MIB),
        cost_estimate=SMALL,
    )(core, conv, prod, gate, gate_other, skip, skip_other, weight)


def halves_kernel(core_ref, kept, came, out, sem):
    half = kept.shape[1]
    copies = []
    for n, (ref, side) in enumerate(((kept, core_ref[0]), (came, 1 - core_ref[0]))):
        target = out.at[:, pl.ds(pl.multiple_of(side * half, half), half)]
        copies.append(pltpu.make_async_copy(ref, target, sem.at[n]))
    for copy in copies:
        copy.start()
    for copy in copies:
        copy.wait()


def place_halves(core, kept, came):
    outs, half = kept.shape
    return pl.pallas_call(
        halves_kernel,
        out_shape=jax.ShapeDtypeStruct((outs, 2 * half), BF16),
        in_specs=[SMEM, VMEM, VMEM],
        out_specs=ANY,
        scratch_shapes=[pltpu.SemaphoreType.DMA((2,))],
        compiler_params=pltpu.CompilerParams(vmem_limit_bytes=4 * MIB),
        cost_estimate=SMALL,
    )(core, kept, came)


def local_channels(k_feature, v_feature, q_feature, spectrum, skip_gain, out_weight):
    channels, tokens = k_feature.shape
    block = spectrum.shape[3]
    ctx_count = lax.axis_size("ctx")
    members = ctx_count // 2
    rows_half = tokens // block // 2
    a_half = spectrum.shape[2] // 2
    ctx, tp = lax.axis_index("ctx"), lax.axis_index("tp")
    core = tp.astype(jnp.int32).reshape(1)
    member = (ctx % members).astype(jnp.int32).reshape(1)
    place = (ctx // members * 2 + tp).astype(jnp.int32).reshape(1)
    tables = {
        name: jnp.asarray(table)
        for name, table in constant_tables(block, members, rows_half, a_half).items()
    }
    halves = [list(range(members)), list(range(members, 2 * members))]
    spread = lambda x: lax.all_to_all(x, "ctx", 0, 0, axis_index_groups=halves, tiled=True)
    across = lambda x: lax.ppermute(
        x, "ctx", [(d, (d + members) % ctx_count) for d in range(ctx_count)]
    )
    swap = lambda x: lax.ppermute(x, "tp", [(0, 1), (1, 0)])

    def joined(own, sent):
        start = ((1 - tp) * channels,) + (0,) * (own.ndim - 1)
        return lax.dynamic_update_slice(own, swap(sent), start)

    own, sent, other_rows = as_rows(core, block, k_feature, v_feature, spectrum=spectrum)
    product = joined(own, sent)
    product, spectrum, other_rows = lax.optimization_barrier((product, spectrum, other_rows))
    xa = spread(product)
    spec = arrange_spectrum(core, spectrum, swap(other_rows), tables["order"])
    xa, spec, q_feature, skip_gain, out_weight = lax.optimization_barrier(
        (xa, spec, q_feature, skip_gain, out_weight)
    )
    xb = swap(xa)
    za = across(xa)
    spec = spread(spec)
    gate, gate_sent = as_rows(core, block, q_feature)
    gate_other = swap(gate_sent)
    skip_other = swap(skip_gain)
    weight = projection(core, out_weight, rows_half)
    za, gate, gate_other, skip_other, weight = lax.optimization_barrier(
        (za, gate, gate_other, skip_other, weight)
    )
    zb = swap(za)

    send, keep = transform(place, (xa, xb, za, zb), spec, tables["transform"])
    total = (keep.astype(F32) + swap(send).astype(F32)).astype(BF16)
    conv = lax.all_to_all(
        total, "ctx", 0, 0, axis_index_groups=[last_order(members)], tiled=True
    ).reshape(channels, 4, rows_half, block)
    kept, sent = gate_and_project(
        core, conv, product, gate, gate_other, skip_gain, skip_other, weight
    )
    return place_halves(core, kept, swap(sent))


def local(k_feature, v_feature, q_feature, spectrum, skip_gain, out_weight):
    channels, tokens = k_feature.shape
    block = spectrum.shape[3]
    ctx_count, tp_count = lax.axis_size("ctx"), lax.axis_size("tp")
    by_channels = (
        tp_count == 2
        and ctx_count == 2 * channels * tp_count
        and tokens * ctx_count * 2 == block * block
        and tokens % (32 * block) == 0
        and spectrum.shape[2] % 32 == 0
        and block % 512 == 0
        and out_weight.shape[1] % 16 == 0
    )
    plan = local_channels if by_channels else local_general
    return plan(k_feature, v_feature, q_feature, spectrum, skip_gain, out_weight)


def solution(mesh):
    placed = (
        P("tp", "ctx"),
        P("tp", "ctx"),
        P("tp", "ctx"),
        P(None, "tp", "ctx", None),
        P("tp"),
        P(),
    )
    return jax.shard_map(
        local, mesh=mesh, in_specs=placed, out_specs=P("tp", "ctx"), check_vma=False
    )
```

```python
import functools
import math

import numpy as np
import ml_dtypes
import jax
import jax.numpy as jnp
from jax import lax
from jax.experimental import pallas as pl
from jax.experimental.pallas import tpu as pltpu
from jax.sharding import PartitionSpec as P

F32 = jnp.float32
BF16 = jnp.bfloat16
VMEM = pl.BlockSpec(memory_space=pltpu.VMEM)
SMEM = pl.BlockSpec(memory_space=pltpu.SMEM)
ANY = pl.BlockSpec(memory_space=pltpu.HBM)
ANYWHERE = pl.BlockSpec(memory_space=pl.ANY)
MIB = 1 << 20
SMALL = pl.CostEstimate(flops=1, bytes_accessed=1, transcendentals=0)


def fourier_tables(length_all):
    positions = jnp.arange(length_all, dtype=jnp.int32)
    phase_index = positions[:, None] * positions[None, :] % length_all
    angles = phase_index.astype(jnp.float32) * (2.0 * math.pi / length_all)
    return (jnp.cos(angles).astype(jnp.bfloat16), jnp.sin(angles).astype(jnp.bfloat16))


def twist_tables(left_index, right_index, length_all):
    phase_index = left_index[:, None] * right_index[None, :] % length_all
    angles = phase_index.astype(jnp.float32) * (2.0 * math.pi / length_all)
    return (jnp.cos(angles), jnp.sin(angles))


def contract(form, left, right):
    return jnp.einsum(form, left, right, preferred_element_type=jnp.float32)


def local_general(k_feature, v_feature, q_feature, spectrum, skip_gain, out_weight):
    channels, tokens = k_feature.shape
    block_order = spectrum.shape[3]
    length_all = block_order * block_order
    ctx_count = lax.axis_size("ctx")
    slab_width = block_order // ctx_count
    rows_here = tokens // block_order
    ctx_index = lax.axis_index("ctx")
    product = (k_feature.astype(jnp.float32) * v_feature.astype(jnp.float32)).astype(jnp.bfloat16)
    cosine_full, sine_full = fourier_tables(block_order)
    cosine_half = cosine_full[: block_order // 2]
    sine_half = sine_full[: block_order // 2]
    positions = jnp.arange(block_order, dtype=jnp.int32)
    local_ticks = ctx_index * slab_width + jnp.arange(slab_width, dtype=jnp.int32)
    grid_rows = lax.all_to_all(
        product.reshape(channels, rows_here, block_order),
        "ctx",
        split_axis=2,
        concat_axis=1,
        tiled=True,
    )
    first_real = contract("cij,ia->caj", grid_rows, cosine_half)
    first_imag = -contract("cij,ia->caj", grid_rows, sine_half)
    twist_cosine, twist_sine = twist_tables(positions, local_ticks, length_all)
    spread_real = (first_real * twist_cosine + first_imag * twist_sine).astype(jnp.bfloat16)
    spread_imag = (first_imag * twist_cosine - first_real * twist_sine).astype(jnp.bfloat16)
    block_real, block_imag = (
        lax.all_to_all(spread_real, "ctx", split_axis=1, concat_axis=2, tiled=True),
        lax.all_to_all(spread_imag, "ctx", split_axis=1, concat_axis=2, tiled=True),
    )
    freq_real = contract("caj,jb->cab", block_real, cosine_full) + contract(
        "caj,jb->cab", block_imag, sine_full
    )
    freq_imag = contract("caj,jb->cab", block_imag, cosine_full) - contract(
        "caj,jb->cab", block_real, sine_full
    )
    resp_real = spectrum[0].astype(jnp.float32)
    resp_imag = spectrum[1].astype(jnp.float32)
    shaped_real = (freq_real * resp_real - freq_imag * resp_imag).astype(jnp.bfloat16)
    shaped_imag = (freq_real * resp_imag + freq_imag * resp_real).astype(jnp.bfloat16)
    inner_real = contract("cab,bj->caj", shaped_real, cosine_full) - contract(
        "cab,bj->caj", shaped_imag, sine_full
    )
    inner_imag = contract("cab,bj->caj", shaped_imag, cosine_full) + contract(
        "cab,bj->caj", shaped_real, sine_full
    )
    twist_cosine, twist_sine = twist_tables(local_ticks, positions, length_all)
    back_real = (inner_real * twist_cosine - inner_imag * twist_sine).astype(jnp.bfloat16)
    back_imag = (inner_imag * twist_cosine + inner_real * twist_sine).astype(jnp.bfloat16)
    summed = contract(
        "ia,caj->cij",
        cosine_half,
        lax.all_to_all(back_real, "ctx", split_axis=2, concat_axis=1, tiled=True),
    ) - contract(
        "ia,caj->cij",
        sine_half,
        lax.all_to_all(back_imag, "ctx", split_axis=2, concat_axis=1, tiled=True),
    )
    spatial = (summed * (1.0 / length_all)).astype(jnp.bfloat16)
    convolved = lax.all_to_all(spatial, "ctx", split_axis=1, concat_axis=2, tiled=True).reshape(
        channels, tokens
    )
    gated_rows = (
        q_feature.astype(jnp.float32)
        * (convolved.astype(jnp.float32) + skip_gain[:, None] * product.astype(jnp.float32))
    ).astype(jnp.bfloat16)
    tp_index = lax.axis_index("tp")
    my_weight = lax.dynamic_slice_in_dim(out_weight, tp_index * channels, channels, 0)
    return lax.psum_scatter(
        jnp.dot(my_weight.T, gated_rows, preferred_element_type=jnp.float32).astype(jnp.bfloat16),
        "tp",
        scatter_dimension=0,
        tiled=True,
    )


def cosine_sine(product, length):
    angles = (product % length).astype(np.float64) * (2.0 * np.pi / length)
    return np.cos(angles), np.sin(angles)


def last_order(members):
    size = members // 2
    turns = lambda n: (2 * size + n, size - 1 - n, 3 * size + n, 2 * size - 1 - n)
    return [device for n in range(size) for device in turns(n)]


@functools.lru_cache(maxsize=None)
def constant_tables(block, members, rows_half, a_half):
    quarter = block // 4
    firsts, lasts, coarses, fines = [], [], [], []
    part = np.arange(members)
    for g in range(2):
        for s in range(2):
            a = (
                (g * members + part)[:, None] * 2 * a_half
                + s * a_half
                + np.arange(a_half)[None, :]
            ).reshape(-1)

            def rows(group, core):
                device = group * members + part
                i = device[:, None] * 2 * rows_half + core * rows_half
                return (i + np.arange(rows_half)[None, :]).reshape(-1)

            i_in = np.concatenate([rows(g, s), rows(g, 1 - s), rows(1 - g, s), rows(1 - g, 1 - s)])
            cosine, sine = cosine_sine(a[:, None] * i_in[None, :], block)
            firsts.append(np.concatenate([cosine, -sine], 0))
            place = last_order(members)

            def by_place(core):
                i = np.concatenate([rows(0, core), rows(1, core)])
                return i.reshape(2 * members, -1)[place].reshape(-1)

            i_out = np.concatenate([by_place(1 - s), by_place(s)])
            cosine, sine = cosine_sine(i_out[:, None] * a[None, :], block)
            lasts.append(np.concatenate([cosine, -sine], 1) / (block * block))
            coarse = 128 * (np.arange(128) % (block // 128))
            coarses.append(np.stack(cosine_sine(a[:, None] * coarse[None, :], block * block)))
            fines.append(np.stack(cosine_sine(a[:, None] * np.arange(128)[None, :], block * block)))
    inner = []
    for rho in range(4):
        cosine, sine = cosine_sine(
            np.arange(quarter)[:, None] * (4 * np.arange(quarter) + rho)[None, :], block
        )
        inner.append(np.stack([cosine, sine, cosine.T, sine.T]))
    order = np.zeros((quarter, quarter), np.float32)
    b = np.arange(quarter)
    order[b, (b % 4) * (quarter // 4) + b // 4] = 1.0
    narrow = lambda x: np.asarray(x, np.float32).astype(ml_dtypes.bfloat16)
    rest = np.stack([coarses, fines], 1).astype(np.float32)
    turns = []
    for _ in range(3):
        turns.append(narrow(rest))
        rest = rest - turns[-1].astype(np.float32)
    turns = np.stack(turns + [np.zeros_like(turns[0])], 1).transpose(0, 2, 4, 1, 3, 5)
    turns = turns.reshape(4, 2 * turns.shape[2], 2, 2 * quarter).transpose(0, 2, 1, 3)
    square = (-1, 2 * quarter, 2 * quarter)
    entries = [np.stack(firsts), np.stack(lasts), np.stack(inner).reshape(square)]
    return dict(
        transform=np.concatenate([narrow(x) for x in entries] + [turns.reshape(square)]),
        order=narrow(order),
    )


def product_kernel(block, count, core_ref, *refs):
    ins, outs, scratch, sem = refs[:count], refs[count:-1 - count], refs[-1 - count : -1], refs[-1]
    copies = [pltpu.make_async_copy(ins[n], scratch[n], sem.at[n]) for n in range(count)]
    for copy in copies:
        copy.start()
    rows_copy = None
    if len(outs) == 4:
        spectrum, own, send, other_rows = outs
        a_half = other_rows.shape[2]
        at = pl.ds(pl.multiple_of((1 - core_ref[0]) * a_half, a_half), a_half)
        rows_copy = pltpu.make_async_copy(spectrum.at[:, :, at, :], other_rows, sem.at[count])
        rows_copy.start()
    else:
        own, send = outs
    core = core_ref[0]
    channels, tokens = ins[0].shape
    place = 0 if own.shape[0] == channels else channels * core
    rows = tokens // block
    half = rows // 2
    to = lax.broadcasted_iota(jnp.int32, (channels * rows, channels * rows), 0)
    at = lax.broadcasted_iota(jnp.int32, (channels * rows, channels * rows), 1)
    side = jnp.bitwise_xor(to // (channels * half), core)
    source = (side * half + to % half) * channels + (to // half) % channels
    order = jnp.where(at == source, 1.0, 0.0).astype(BF16)
    for copy in copies:
        copy.wait()
    pieces = []
    for i in range(rows):
        cut = slice(i * block, (i + 1) * block)
        piece = scratch[0][:, cut].astype(F32)
        for other in scratch[1:]:
            piece = piece * other[:, cut].astype(F32)
        pieces.append(piece)
    stacked = jnp.concatenate(pieces, axis=0).astype(BF16)
    ordered = jnp.dot(order, stacked, preferred_element_type=F32).astype(BF16)
    ordered = ordered.reshape(2, channels, half, block)
    own[pl.ds(place, channels)] = ordered[0]
    send[...] = ordered[1]
    if rows_copy is not None:
        rows_copy.wait()


def as_rows(core, block, *arrays, spectrum=None):
    channels, tokens = arrays[0].shape
    half = tokens // block // 2
    room, extra, shapes = 1, [], []
    if spectrum is not None:
        two, _, a_here, _ = spectrum.shape
        room, extra = 2, [spectrum]
        shapes = [jax.ShapeDtypeStruct((two, channels, a_here // 2, block), BF16)]
    return pl.pallas_call(
        functools.partial(product_kernel, block, len(arrays)),
        out_shape=[
            jax.ShapeDtypeStruct((room * channels, half, block), BF16),
            jax.ShapeDtypeStruct((channels, half, block), BF16),
        ]
        + shapes,
        in_specs=[SMEM] + [ANY] * len(arrays + tuple(extra)),
        out_specs=[VMEM] * (2 + len(shapes)),
        scratch_shapes=[pltpu.VMEM((channels, tokens), BF16)] * len(arrays)
        + [pltpu.SemaphoreType.DMA((len(arrays) + 1,))],
        cost_estimate=SMALL,
    )(core, *arrays, *extra)


def spectrum_kernel(core_ref, in_ref, came_ref, order_ref, *refs):
    moved, rows, came, order, sem = refs
    core = core_ref[0]
    two, channels, a_half, block = rows.shape
    at = pl.ds(pl.multiple_of(core * a_half, a_half), a_half)
    copies = [
        pltpu.make_async_copy(order_ref, order, sem.at[0]),
        pltpu.make_async_copy(in_ref.at[:, :, at, :], rows, sem.at[1]),
        pltpu.make_async_copy(came_ref, came, sem.at[2]),
    ]
    for copy in copies:
        copy.start()
    copies[0].wait()
    quarter = block // 4
    step = quarter // 4
    for side, ref in ((core, rows), (1 - core, came)):
        copies[1 if ref is rows else 2].wait()
        flat = jnp.concatenate([ref[n, c] for c in range(channels) for n in range(two)], 0)
        parts = [
            jnp.dot(flat[:, q * quarter : (q + 1) * quarter], order[...], preferred_element_type=F32)
            for q in range(4)
        ]
        for rho in range(4):
            columns = [part[:, rho * step : (rho + 1) * step] for part in parts]
            columns = jnp.concatenate(columns, axis=1).astype(BF16)
            moved[pl.ds(channels * side, channels), :, :, rho * quarter : (rho + 1) * quarter] = (
                columns.reshape(channels, two, a_half, quarter)
            )


def arrange_spectrum(core, spectrum, came, order):
    two, channels, a_half, block = came.shape
    return pl.pallas_call(
        spectrum_kernel,
        out_shape=jax.ShapeDtypeStruct((2 * channels, two, a_half, block), BF16),
        in_specs=[SMEM, ANY, ANY, ANY],
        out_specs=VMEM,
        scratch_shapes=[
            pltpu.VMEM(came.shape, BF16),
            pltpu.VMEM(came.shape, BF16),
            pltpu.VMEM(order.shape, BF16),
            pltpu.SemaphoreType.DMA((3,)),
        ],
        cost_estimate=SMALL,
    )(core, spectrum, came, order)


def weight_kernel(rows, core_ref, weight, out):
    channels, outs = weight.shape
    half = outs // 2
    core = core_ref[0]
    shape = out.shape
    to = lax.broadcasted_iota(jnp.int32, (shape[0], outs), 0)
    at = lax.broadcasted_iota(jnp.int32, (shape[0], outs), 1)
    column = jnp.bitwise_xor(to // (rows * half), core) * half + to % half
    pick = jnp.where(at == column, 1.0, 0.0).astype(BF16)
    turned = lax.dot_general(
        pick, weight[...], (((1,), (1,)), ((), ())), preferred_element_type=F32
    ).astype(BF16)
    to = lax.broadcasted_iota(jnp.int32, (channels, shape[1]), 0)
    at = lax.broadcasted_iota(jnp.int32, (channels, shape[1]), 1)
    channel = (at // rows + core * (channels // 2)) % channels
    widen = jnp.where(channel == to, 1.0, 0.0).astype(BF16)
    wide = jnp.dot(turned, widen, preferred_element_type=F32)
    to = lax.broadcasted_iota(jnp.int32, shape, 0)
    at = lax.broadcasted_iota(jnp.int32, shape, 1)
    out[...] = jnp.where(at % rows == (to // half) % rows, wide, 0.0).astype(BF16)


def projection(core, weight, rows):
    channels, outs = weight.shape
    return pl.pallas_call(
        functools.partial(weight_kernel, rows),
        out_shape=jax.ShapeDtypeStruct((rows * outs, rows * channels), BF16),
        in_specs=[SMEM, VMEM],
        out_specs=VMEM,
        compiler_params=pltpu.CompilerParams(vmem_limit_bytes=4 * MIB),
    )(core, weight)


def butterflies(values, sign):
    (r0, i0), (r1, i1), (r2, i2), (r3, i3) = values
    er, ei, dr, di = r0 + r2, i0 + i2, r0 - r2, i0 - i2
    fr, fi, hr, hi = r1 + r3, i1 + i3, r1 - r3, i1 - i3
    plus, minus = (dr - hi, di + hr), (dr + hi, di - hr)
    if sign < 0:
        plus, minus = minus, plus
    return [(er + fr, ei + fi), plus, (er - fr, ei - fi), minus]


def turn(values, cosine, sine):
    real, imag = values
    rows = real.shape[0]
    both = jnp.concatenate([real.astype(BF16), imag.astype(BF16)], axis=0)
    with_cosine = jnp.dot(both, cosine, preferred_element_type=F32)
    with_sine = jnp.dot(both, sine, preferred_element_type=F32)
    return with_cosine[:rows], with_cosine[rows:], with_sine[:rows], with_sine[rows:]


def full_turns(turns, rows):
    def whole(kind, which):
        cut = slice(kind * rows, (kind + 1) * rows)
        part = lambda n: turns[n // 2, cut, pl.ds((2 * (n % 2) + which) * 128, 128)].astype(F32)
        return part(0) + part(1) + part(2)

    return (whole(0, 0), whole(0, 1)), (whole(1, 0), whole(1, 1))


def pair_of(inner, rho, way):
    quarter = inner.shape[-1] // 2
    four = inner[rho].reshape(4, quarter, quarter)
    return four[2 * way], four[2 * way + 1]


def transform_kernel(place_ref, *refs):
    ins, (send, keep, signal, spec, first, last, inner, turns, twist, sem) = refs[:-10], refs[-10:]
    *pieces, spec_in, table = ins
    place = place_ref[0]
    count = pieces[0].shape[0]
    size = turns.shape[0]
    moves = [(table.at[place], first)]
    moves += [(ref, signal.at[pl.ds(n * count, count)]) for n, ref in enumerate(pieces)]
    moves += [(table.at[pl.ds(12 + size * place, size)], turns)]
    moves += [(table.at[pl.ds(8, 4)], inner), (spec_in, spec), (table.at[4 + place], last)]
    copies = [pltpu.make_async_copy(*move, sem.at[n]) for n, move in enumerate(moves)]
    for copy in copies:
        copy.start()
    for copy in copies[:6]:
        copy.wait()
    block = signal.shape[-1]
    quarter = block // 4
    lines = signal[...].reshape(-1, block)
    a_rows = first.shape[0] // 2
    coarse, fine = full_turns(turns, a_rows)
    turned = []
    for q in range(4):
        cut = slice(q * quarter, (q + 1) * quarter)
        both = jnp.dot(first[...], lines[:, cut], preferred_element_type=F32)
        for h in range(q * quarter // 128, (q + 1) * quarter // 128):
            lanes = slice(128 * h, 128 * (h + 1))
            uc, us = coarse[0][:, h : h + 1], coarse[1][:, h : h + 1]
            twist[0, :, lanes] = uc * fine[0] - us * fine[1]
            twist[1, :, lanes] = us * fine[0] + uc * fine[1]
        real, imag = both[:a_rows], both[a_rows:]
        cosine, sine = twist[0, :, cut], twist[1, :, cut]
        turned.append((real * cosine + imag * sine, imag * cosine - real * sine))
    mixes = butterflies(turned, -1)
    for copy in copies[6:-1]:
        copy.wait()
    backs = []
    for rho in range(4):
        rc, ic, rs, si = turn(mixes[rho], *pair_of(inner, rho, 0))
        zr, zi = rc + si, ic - rs
        cut = slice(rho * quarter, (rho + 1) * quarter)
        gr = spec[:, 0, :, cut].reshape(-1, quarter).astype(F32)
        gi = spec[:, 1, :, cut].reshape(-1, quarter).astype(F32)
        shaped = (zr * gr - zi * gi, zr * gi + zi * gr)
        rc, ic, rs, si = turn(shaped, *pair_of(inner, rho, 1))
        backs.append((rc - si, ic + rs))
    mixes = butterflies(backs, 1)
    half = last.shape[0] // 2
    copies[-1].wait()
    for q, (real, imag) in enumerate(mixes):
        cut = slice(q * quarter, (q + 1) * quarter)
        cosine, sine = twist[0, :, cut], twist[1, :, cut]
        pair = jnp.concatenate(
            [
                (real * cosine - imag * sine).astype(BF16),
                (imag * cosine + real * sine).astype(BF16),
            ],
            axis=0,
        )
        out = jnp.dot(last[...], pair, preferred_element_type=F32)
        send[:, :, cut] = out[:half].astype(BF16).reshape(send.shape[0], send.shape[1], quarter)
        keep[:, :, cut] = out[half:].astype(BF16).reshape(keep.shape[0], keep.shape[1], quarter)


def transform(place, pieces, spec, table):
    members, rows_half, block = pieces[0].shape
    a_rows = spec.shape[0] * spec.shape[2]
    out = (2 * members, rows_half, block)
    square = table.shape[1:]
    return pl.pallas_call(
        transform_kernel,
        in_specs=[SMEM] + [ANYWHERE] * (len(pieces) + 1) + [ANY],
        out_specs=[VMEM, VMEM],
        out_shape=[jax.ShapeDtypeStruct(out, BF16)] * 2,
        scratch_shapes=[
            pltpu.VMEM((4 * members, rows_half, block), BF16),
            pltpu.VMEM(spec.shape, BF16),
            pltpu.VMEM(square, BF16),
            pltpu.VMEM(square, BF16),
            pltpu.VMEM((4,) + square, BF16),
            pltpu.VMEM(((table.shape[0] - 12) // 4,) + square, BF16),
            pltpu.VMEM((2, a_rows, block), F32),
            pltpu.SemaphoreType.DMA((len(pieces) + 5,)),
        ],
        compiler_params=pltpu.CompilerParams(vmem_limit_bytes=48 * MIB),
        cost_estimate=SMALL,
    )(place, *pieces, spec, table)


def gate_kernel(core_ref, conv, prod, gate, gate_other, skip, skip_other, weight, keep, send):
    here, _, rows, block = conv.shape
    core = core_ref[0]
    pieces = []
    for side, (values, gains) in enumerate(((gate, skip), (gate_other, skip_other))):
        for n in range(here):
            high = jnp.bitwise_xor(core, side)
            total = conv[n, 2 * high].astype(F32) + conv[here - 1 - n, 2 * high + 1].astype(F32)
            total = total + gains[n] * prod[high * here + n].astype(F32)
            pieces.append((values[n].astype(F32) * total).astype(BF16))
    gated = jnp.concatenate(pieces, axis=0)
    mixed = jnp.dot(weight[...], gated, preferred_element_type=F32)
    outs = keep.shape[0]
    for r in range(rows):
        cut = slice(r * block, (r + 1) * block)
        keep[:, cut] = mixed[r * outs : (r + 1) * outs].astype(BF16)
        send[:, cut] = mixed[(rows + r) * outs : (rows + r + 1) * outs].astype(BF16)


def gate_and_project(core, conv, prod, gate, gate_other, skip, skip_other, weight):
    _, _, rows, block = conv.shape
    outs = weight.shape[0] // (2 * rows)
    return pl.pallas_call(
        gate_kernel,
        out_shape=[jax.ShapeDtypeStruct((outs, rows * block), BF16)] * 2,
        in_specs=[SMEM, VMEM, VMEM, VMEM, VMEM, SMEM, SMEM, VMEM],
        out_specs=[VMEM, VMEM],
        compiler_params=pltpu.CompilerParams(vmem_limit_bytes=16 * MIB),
        cost_estimate=SMALL,
    )(core, conv, prod, gate, gate_other, skip, skip_other, weight)


def halves_kernel(core_ref, kept, came, out, sem):
    half = kept.shape[1]
    copies = []
    for n, (ref, side) in enumerate(((kept, core_ref[0]), (came, 1 - core_ref[0]))):
        target = out.at[:, pl.ds(pl.multiple_of(side * half, half), half)]
        copies.append(pltpu.make_async_copy(ref, target, sem.at[n]))
    for copy in copies:
        copy.start()
    for copy in copies:
        copy.wait()


def place_halves(core, kept, came):
    outs, half = kept.shape
    return pl.pallas_call(
        halves_kernel,
        out_shape=jax.ShapeDtypeStruct((outs, 2 * half), BF16),
        in_specs=[SMEM, VMEM, VMEM],
        out_specs=ANY,
        scratch_shapes=[pltpu.SemaphoreType.DMA((2,))],
        compiler_params=pltpu.CompilerParams(vmem_limit_bytes=4 * MIB),
        cost_estimate=SMALL,
    )(core, kept, came)


def local_channels(k_feature, v_feature, q_feature, spectrum, skip_gain, out_weight):
    channels, tokens = k_feature.shape
    block = spectrum.shape[3]
    ctx_count = lax.axis_size("ctx")
    members = ctx_count // 2
    rows_half = tokens // block // 2
    a_half = spectrum.shape[2] // 2
    ctx, tp = lax.axis_index("ctx"), lax.axis_index("tp")
    core = tp.astype(jnp.int32).reshape(1)
    member = (ctx % members).astype(jnp.int32).reshape(1)
    place = (ctx // members * 2 + tp).astype(jnp.int32).reshape(1)
    tables = {
        name: jnp.asarray(table)
        for name, table in constant_tables(block, members, rows_half, a_half).items()
    }
    halves = [list(range(members)), list(range(members, 2 * members))]
    spread = lambda x: lax.all_to_all(x, "ctx", 0, 0, axis_index_groups=halves, tiled=True)
    across = lambda x: lax.ppermute(
        x, "ctx", [(d, (d + members) % ctx_count) for d in range(ctx_count)]
    )
    swap = lambda x: lax.ppermute(x, "tp", [(0, 1), (1, 0)])

    def joined(own, sent):
        start = ((1 - tp) * channels,) + (0,) * (own.ndim - 1)
        return lax.dynamic_update_slice(own, swap(sent), start)

    own, sent, other_rows = as_rows(core, block, k_feature, v_feature, spectrum=spectrum)
    product = joined(own, sent)
    product, spectrum, other_rows = lax.optimization_barrier((product, spectrum, other_rows))
    xa = spread(product)
    spec = arrange_spectrum(core, spectrum, swap(other_rows), tables["order"])
    xa, spec, q_feature, skip_gain, out_weight = lax.optimization_barrier(
        (xa, spec, q_feature, skip_gain, out_weight)
    )
    xb = swap(xa)
    za = across(xa)
    spec = spread(spec)
    gate, gate_sent = as_rows(core, block, q_feature)
    gate_other = swap(gate_sent)
    skip_other = swap(skip_gain)
    weight = projection(core, out_weight, rows_half)
    za, gate, gate_other, skip_other, weight = lax.optimization_barrier(
        (za, gate, gate_other, skip_other, weight)
    )
    zb = swap(za)

    send, keep = transform(place, (xa, xb, za, zb), spec, tables["transform"])
    total = (keep.astype(F32) + swap(send).astype(F32)).astype(BF16)
    conv = lax.all_to_all(
        total, "ctx", 0, 0, axis_index_groups=[last_order(members)], tiled=True
    ).reshape(channels, 4, rows_half, block)
    kept, sent = gate_and_project(
        core, conv, product, gate, gate_other, skip_gain, skip_other, weight
    )
    return place_halves(core, kept, swap(sent))


def local(k_feature, v_feature, q_feature, spectrum, skip_gain, out_weight):
    channels, tokens = k_feature.shape
    block = spectrum.shape[3]
    ctx_count, tp_count = lax.axis_size("ctx"), lax.axis_size("tp")
    by_channels = (
        tp_count == 2
        and ctx_count == 2 * channels * tp_count
        and tokens * ctx_count * 2 == block * block
        and tokens % (32 * block) == 0
        and spectrum.shape[2] % 32 == 0
        and block % 512 == 0
        and out_weight.shape[1] % 16 == 0
    )
    plan = local_channels if by_channels else local_general
    return plan(k_feature, v_feature, q_feature, spectrum, skip_gain, out_weight)


def solution(mesh):
    placed = (
        P("tp", "ctx"),
        P("tp", "ctx"),
        P("tp", "ctx"),
        P(None, "tp", "ctx", None),
        P("tp"),
        P(),
    )
    return jax.shard_map(
        local, mesh=mesh, in_specs=placed, out_specs=P("tp", "ctx"), check_vma=False
    )
```

```python
import functools
import math

import numpy as np
import ml_dtypes
import jax
import jax.numpy as jnp
from jax import lax
from jax.experimental import pallas as pl
from jax.experimental.pallas import tpu as pltpu
from jax.sharding import PartitionSpec as P

F32 = jnp.float32
BF16 = jnp.bfloat16
VMEM = pl.BlockSpec(memory_space=pltpu.VMEM)
SMEM = pl.BlockSpec(memory_space=pltpu.SMEM)
ANY = pl.BlockSpec(memory_space=pltpu.HBM)
ANYWHERE = pl.BlockSpec(memory_space=pl.ANY)
MIB = 1 << 20
SMALL = pl.CostEstimate(flops=1, bytes_accessed=1, transcendentals=0)


def fourier_tables(length_all):
    positions = jnp.arange(length_all, dtype=jnp.int32)
    phase_index = positions[:, None] * positions[None, :] % length_all
    angles = phase_index.astype(jnp.float32) * (2.0 * math.pi / length_all)
    return (jnp.cos(angles).astype(jnp.bfloat16), jnp.sin(angles).astype(jnp.bfloat16))


def twist_tables(left_index, right_index, length_all):
    phase_index = left_index[:, None] * right_index[None, :] % length_all
    angles = phase_index.astype(jnp.float32) * (2.0 * math.pi / length_all)
    return (jnp.cos(angles), jnp.sin(angles))


def contract(form, left, right):
    return jnp.einsum(form, left, right, preferred_element_type=jnp.float32)


def local_general(k_feature, v_feature, q_feature, spectrum, skip_gain, out_weight):
    channels, tokens = k_feature.shape
    block_order = spectrum.shape[3]
    length_all = block_order * block_order
    ctx_count = lax.axis_size("ctx")
    slab_width = block_order // ctx_count
    rows_here = tokens // block_order
    ctx_index = lax.axis_index("ctx")
    product = (k_feature.astype(jnp.float32) * v_feature.astype(jnp.float32)).astype(jnp.bfloat16)
    cosine_full, sine_full = fourier_tables(block_order)
    cosine_half = cosine_full[: block_order // 2]
    sine_half = sine_full[: block_order // 2]
    positions = jnp.arange(block_order, dtype=jnp.int32)
    local_ticks = ctx_index * slab_width + jnp.arange(slab_width, dtype=jnp.int32)
    grid_rows = lax.all_to_all(
        product.reshape(channels, rows_here, block_order),
        "ctx",
        split_axis=2,
        concat_axis=1,
        tiled=True,
    )
    first_real = contract("cij,ia->caj", grid_rows, cosine_half)
    first_imag = -contract("cij,ia->caj", grid_rows, sine_half)
    twist_cosine, twist_sine = twist_tables(positions, local_ticks, length_all)
    spread_real = (first_real * twist_cosine + first_imag * twist_sine).astype(jnp.bfloat16)
    spread_imag = (first_imag * twist_cosine - first_real * twist_sine).astype(jnp.bfloat16)
    block_real, block_imag = (
        lax.all_to_all(spread_real, "ctx", split_axis=1, concat_axis=2, tiled=True),
        lax.all_to_all(spread_imag, "ctx", split_axis=1, concat_axis=2, tiled=True),
    )
    freq_real = contract("caj,jb->cab", block_real, cosine_full) + contract(
        "caj,jb->cab", block_imag, sine_full
    )
    freq_imag = contract("caj,jb->cab", block_imag, cosine_full) - contract(
        "caj,jb->cab", block_real, sine_full
    )
    resp_real = spectrum[0].astype(jnp.float32)
    resp_imag = spectrum[1].astype(jnp.float32)
    shaped_real = (freq_real * resp_real - freq_imag * resp_imag).astype(jnp.bfloat16)
    shaped_imag = (freq_real * resp_imag + freq_imag * resp_real).astype(jnp.bfloat16)
    inner_real = contract("cab,bj->caj", shaped_real, cosine_full) - contract(
        "cab,bj->caj", shaped_imag, sine_full
    )
    inner_imag = contract("cab,bj->caj", shaped_imag, cosine_full) + contract(
        "cab,bj->caj", shaped_real, sine_full
    )
    twist_cosine, twist_sine = twist_tables(local_ticks, positions, length_all)
    back_real = (inner_real * twist_cosine - inner_imag * twist_sine).astype(jnp.bfloat16)
    back_imag = (inner_imag * twist_cosine + inner_real * twist_sine).astype(jnp.bfloat16)
    summed = contract(
        "ia,caj->cij",
        cosine_half,
        lax.all_to_all(back_real, "ctx", split_axis=2, concat_axis=1, tiled=True),
    ) - contract(
        "ia,caj->cij",
        sine_half,
        lax.all_to_all(back_imag, "ctx", split_axis=2, concat_axis=1, tiled=True),
    )
    spatial = (summed * (1.0 / length_all)).astype(jnp.bfloat16)
    convolved = lax.all_to_all(spatial, "ctx", split_axis=1, concat_axis=2, tiled=True).reshape(
        channels, tokens
    )
    gated_rows = (
        q_feature.astype(jnp.float32)
        * (convolved.astype(jnp.float32) + skip_gain[:, None] * product.astype(jnp.float32))
    ).astype(jnp.bfloat16)
    tp_index = lax.axis_index("tp")
    my_weight = lax.dynamic_slice_in_dim(out_weight, tp_index * channels, channels, 0)
    return lax.psum_scatter(
        jnp.dot(my_weight.T, gated_rows, preferred_element_type=jnp.float32).astype(jnp.bfloat16),
        "tp",
        scatter_dimension=0,
        tiled=True,
    )


def cosine_sine(product, length):
    angles = (product % length).astype(np.float64) * (2.0 * np.pi / length)
    return np.cos(angles), np.sin(angles)


def last_order(members):
    size = members // 2
    turns = lambda n: (2 * size + n, 4 * size - 1 - n, n, 2 * size - 1 - n)
    return [device for n in range(size) for device in turns(n)]


@functools.lru_cache(maxsize=None)
def constant_tables(block, members, rows_half, a_half):
    quarter = block // 4
    firsts, lasts, coarses, fines = [], [], [], []
    part = np.arange(members)
    for g in range(2):
        for s in range(2):
            a = (
                (g * members + part)[:, None] * 2 * a_half
                + s * a_half
                + np.arange(a_half)[None, :]
            ).reshape(-1)

            def rows(group, core):
                device = group * members + part
                i = device[:, None] * 2 * rows_half + core * rows_half
                return (i + np.arange(rows_half)[None, :]).reshape(-1)

            i_in = np.concatenate([rows(g, s), rows(g, 1 - s), rows(1 - g, s), rows(1 - g, 1 - s)])
            cosine, sine = cosine_sine(a[:, None] * i_in[None, :], block)
            firsts.append(np.concatenate([cosine, -sine], 0))
            place = last_order(members)

            def by_place(core):
                i = np.concatenate([rows(0, core), rows(1, core)])
                return i.reshape(2 * members, -1)[place].reshape(-1)

            i_out = np.concatenate([by_place(1 - s), by_place(s)])
            cosine, sine = cosine_sine(i_out[:, None] * a[None, :], block)
            lasts.append(np.concatenate([cosine, -sine], 1))
            coarse = 128 * (np.arange(128) % (block // 128))
            coarses.append(np.stack(cosine_sine(a[:, None] * coarse[None, :], block * block)))
            fines.append(np.stack(cosine_sine(a[:, None] * np.arange(128)[None, :], block * block)))
    inner = []
    for rho in range(4):
        cosine, sine = cosine_sine(
            np.arange(quarter)[:, None] * (4 * np.arange(quarter) + rho)[None, :], block
        )
        inner.append(np.stack([cosine, sine, cosine.T, sine.T]))
    order = np.zeros((quarter, quarter), np.float32)
    b = np.arange(quarter)
    order[b, (b % 4) * (quarter // 4) + b // 4] = 1.0
    narrow = lambda x: np.asarray(x, np.float32).astype(ml_dtypes.bfloat16)
    rest = np.stack([coarses, fines], 1).astype(np.float32)
    turns = []
    for _ in range(3):
        turns.append(narrow(rest))
        rest = rest - turns[-1].astype(np.float32)
    turns = np.stack(turns + [np.zeros_like(turns[0])], 1).transpose(0, 2, 4, 1, 3, 5)
    turns = turns.reshape(4, 2 * turns.shape[2], 2, 2 * quarter).transpose(0, 2, 1, 3)
    square = (-1, 2 * quarter, 2 * quarter)
    entries = [np.stack(firsts), np.stack(lasts), np.stack(inner).reshape(square)]
    return dict(
        transform=np.concatenate([narrow(x) for x in entries] + [turns.reshape(square)]),
        order=narrow(order),
    )


def product_kernel(block, count, core_ref, *refs):
    ins, outs, scratch, sem = refs[:count], refs[count:-1 - count], refs[-1 - count : -1], refs[-1]
    copies = [pltpu.make_async_copy(ins[n], scratch[n], sem.at[n]) for n in range(count)]
    for copy in copies:
        copy.start()
    rows_copy = None
    if len(outs) == 4:
        spectrum, own, send, other_rows = outs
        a_half = other_rows.shape[2]
        at = pl.ds(pl.multiple_of((1 - core_ref[0]) * a_half, a_half), a_half)
        rows_copy = pltpu.make_async_copy(spectrum.at[:, :, at, :], other_rows, sem.at[count])
        rows_copy.start()
    else:
        own, send = outs
    core = core_ref[0]
    channels, tokens = ins[0].shape
    place = 0 if own.shape[0] == channels else channels * core
    rows = tokens // block
    half = rows // 2
    to = lax.broadcasted_iota(jnp.int32, (channels * rows, channels * rows), 0)
    at = lax.broadcasted_iota(jnp.int32, (channels * rows, channels * rows), 1)
    side = jnp.bitwise_xor(to // (channels * half), core)
    source = (side * half + to % half) * channels + (to // half) % channels
    order = jnp.where(at == source, 1.0, 0.0).astype(BF16)
    for copy in copies:
        copy.wait()
    pieces = []
    for i in range(rows):
        cut = slice(i * block, (i + 1) * block)
        piece = scratch[0][:, cut].astype(F32)
        for other in scratch[1:]:
            piece = piece * other[:, cut].astype(F32)
        pieces.append(piece)
    stacked = jnp.concatenate(pieces, axis=0).astype(BF16)
    ordered = jnp.dot(order, stacked, preferred_element_type=F32).astype(BF16)
    ordered = ordered.reshape(2, channels, half, block)
    own[pl.ds(place, channels)] = ordered[0]
    send[...] = ordered[1]
    if rows_copy is not None:
        rows_copy.wait()


def as_rows(core, block, *arrays, spectrum=None):
    channels, tokens = arrays[0].shape
    half = tokens // block // 2
    room, extra, shapes = 1, [], []
    if spectrum is not None:
        two, _, a_here, _ = spectrum.shape
        room, extra = 2, [spectrum]
        shapes = [jax.ShapeDtypeStruct((two, channels, a_here // 2, block), BF16)]
    return pl.pallas_call(
        functools.partial(product_kernel, block, len(arrays)),
        out_shape=[
            jax.ShapeDtypeStruct((room * channels, half, block), BF16),
            jax.ShapeDtypeStruct((channels, half, block), BF16),
        ]
        + shapes,
        in_specs=[SMEM] + [ANY] * len(arrays + tuple(extra)),
        out_specs=[VMEM] * (2 + len(shapes)),
        scratch_shapes=[pltpu.VMEM((channels, tokens), BF16)] * len(arrays)
        + [pltpu.SemaphoreType.DMA((len(arrays) + 1,))],
        cost_estimate=SMALL,
    )(core, *arrays, *extra)


def spectrum_kernel(core_ref, in_ref, came_ref, order_ref, *refs):
    moved, rows, came, order, sem = refs
    core = core_ref[0]
    two, channels, a_half, block = rows.shape
    at = pl.ds(pl.multiple_of(core * a_half, a_half), a_half)
    copies = [
        pltpu.make_async_copy(order_ref, order, sem.at[0]),
        pltpu.make_async_copy(in_ref.at[:, :, at, :], rows, sem.at[1]),
        pltpu.make_async_copy(came_ref, came, sem.at[2]),
    ]
    for copy in copies:
        copy.start()
    copies[0].wait()
    quarter = block // 4
    step = quarter // 4
    for side, ref in ((core, rows), (1 - core, came)):
        copies[1 if ref is rows else 2].wait()
        flat = jnp.concatenate([ref[n, c] for c in range(channels) for n in range(two)], 0)
        parts = [
            jnp.dot(flat[:, q * quarter : (q + 1) * quarter], order[...], preferred_element_type=F32)
            for q in range(4)
        ]
        for rho in range(4):
            columns = [part[:, rho * step : (rho + 1) * step] for part in parts]
            columns = jnp.concatenate(columns, axis=1).astype(BF16)
            moved[pl.ds(channels * side, channels), :, :, rho * quarter : (rho + 1) * quarter] = (
                columns.reshape(channels, two, a_half, quarter)
            )


def arrange_spectrum(core, spectrum, came, order):
    two, channels, a_half, block = came.shape
    return pl.pallas_call(
        spectrum_kernel,
        out_shape=jax.ShapeDtypeStruct((2 * channels, two, a_half, block), BF16),
        in_specs=[SMEM, ANY, ANY, ANY],
        out_specs=VMEM,
        scratch_shapes=[
            pltpu.VMEM(came.shape, BF16),
            pltpu.VMEM(came.shape, BF16),
            pltpu.VMEM(order.shape, BF16),
            pltpu.SemaphoreType.DMA((3,)),
        ],
        cost_estimate=SMALL,
    )(core, spectrum, came, order)


def weight_kernel(rows, core_ref, weight, out):
    channels, outs = weight.shape
    half = outs // 2
    core = core_ref[0]
    shape = out.shape
    to = lax.broadcasted_iota(jnp.int32, (shape[0], outs), 0)
    at = lax.broadcasted_iota(jnp.int32, (shape[0], outs), 1)
    column = jnp.bitwise_xor(to // (rows * half), core) * half + to % half
    pick = jnp.where(at == column, 1.0, 0.0).astype(BF16)
    turned = lax.dot_general(
        pick, weight[...], (((1,), (1,)), ((), ())), preferred_element_type=F32
    ).astype(BF16)
    to = lax.broadcasted_iota(jnp.int32, (channels, shape[1]), 0)
    at = lax.broadcasted_iota(jnp.int32, (channels, shape[1]), 1)
    channel = (at // rows + core * (channels // 2)) % channels
    widen = jnp.where(channel == to, 1.0, 0.0).astype(BF16)
    wide = jnp.dot(turned, widen, preferred_element_type=F32)
    to = lax.broadcasted_iota(jnp.int32, shape, 0)
    at = lax.broadcasted_iota(jnp.int32, shape, 1)
    out[...] = jnp.where(at % rows == (to // half) % rows, wide, 0.0).astype(BF16)


def projection(core, weight, rows):
    channels, outs = weight.shape
    return pl.pallas_call(
        functools.partial(weight_kernel, rows),
        out_shape=jax.ShapeDtypeStruct((rows * outs, rows * channels), BF16),
        in_specs=[SMEM, VMEM],
        out_specs=VMEM,
        compiler_params=pltpu.CompilerParams(vmem_limit_bytes=4 * MIB),
    )(core, weight)


def butterflies(values, sign):
    (r0, i0), (r1, i1), (r2, i2), (r3, i3) = values
    er, ei, dr, di = r0 + r2, i0 + i2, r0 - r2, i0 - i2
    fr, fi, hr, hi = r1 + r3, i1 + i3, r1 - r3, i1 - i3
    plus, minus = (dr - hi, di + hr), (dr + hi, di - hr)
    if sign < 0:
        plus, minus = minus, plus
    return [(er + fr, ei + fi), plus, (er - fr, ei - fi), minus]


def turn(values, cosine, sine):
    real, imag = values
    rows = real.shape[0]
    both = jnp.concatenate([real.astype(BF16), imag.astype(BF16)], axis=0)
    with_cosine = jnp.dot(both, cosine, preferred_element_type=F32)
    with_sine = jnp.dot(both, sine, preferred_element_type=F32)
    return with_cosine[:rows], with_cosine[rows:], with_sine[:rows], with_sine[rows:]


def full_turns(turns, rows):
    def whole(kind, which):
        cut = slice(kind * rows, (kind + 1) * rows)
        part = lambda n: turns[n // 2, cut, pl.ds((2 * (n % 2) + which) * 128, 128)].astype(F32)
        return part(0) + part(1) + part(2)

    return (whole(0, 0), whole(0, 1)), (whole(1, 0), whole(1, 1))


def pair_of(inner, rho, way):
    quarter = inner.shape[-1] // 2
    four = inner[rho].reshape(4, quarter, quarter)
    return four[2 * way], four[2 * way + 1]


def transform_kernel(place_ref, *refs):
    ins, (send, keep, signal, spec, first, last, inner, turns, twist, sem) = refs[:-10], refs[-10:]
    *pieces, spec_in, table = ins
    place = place_ref[0]
    count = pieces[0].shape[0]
    size = turns.shape[0]
    moves = [(table.at[place], first)]
    moves += [(ref, signal.at[pl.ds(n * count, count)]) for n, ref in enumerate(pieces)]
    moves += [(table.at[pl.ds(12 + size * place, size)], turns)]
    moves += [(table.at[pl.ds(8, 4)], inner), (spec_in, spec), (table.at[4 + place], last)]
    copies = [pltpu.make_async_copy(*move, sem.at[n]) for n, move in enumerate(moves)]
    for copy in copies:
        copy.start()
    for copy in copies[:6]:
        copy.wait()
    block = signal.shape[-1]
    quarter = block // 4
    lines = signal[...].reshape(-1, block)
    a_rows = first.shape[0] // 2
    coarse, fine = full_turns(turns, a_rows)
    turned = []
    for q in range(4):
        cut = slice(q * quarter, (q + 1) * quarter)
        both = jnp.dot(first[...], lines[:, cut], preferred_element_type=F32)
        for h in range(q * quarter // 128, (q + 1) * quarter // 128):
            lanes = slice(128 * h, 128 * (h + 1))
            uc, us = coarse[0][:, h : h + 1], coarse[1][:, h : h + 1]
            twist[0, :, lanes] = uc * fine[0] - us * fine[1]
            twist[1, :, lanes] = us * fine[0] + uc * fine[1]
        real, imag = both[:a_rows], both[a_rows:]
        cosine, sine = twist[0, :, cut], twist[1, :, cut]
        turned.append((real * cosine + imag * sine, imag * cosine - real * sine))
    mixes = butterflies(turned, -1)
    for copy in copies[6:-1]:
        copy.wait()
    backs = []
    for rho in range(4):
        rc, ic, rs, si = turn(mixes[rho], *pair_of(inner, rho, 0))
        zr, zi = rc + si, ic - rs
        cut = slice(rho * quarter, (rho + 1) * quarter)
        gr = spec[:, 0, :, cut].reshape(-1, quarter).astype(F32)
        gi = spec[:, 1, :, cut].reshape(-1, quarter).astype(F32)
        shaped = (zr * gr - zi * gi, zr * gi + zi * gr)
        rc, ic, rs, si = turn(shaped, *pair_of(inner, rho, 1))
        backs.append((rc - si, ic + rs))
    mixes = butterflies(backs, 1)
    scale = 1.0 / (block * block)
    half = last.shape[0] // 2
    copies[-1].wait()
    for q, (real, imag) in enumerate(mixes):
        cut = slice(q * quarter, (q + 1) * quarter)
        cosine, sine = twist[0, :, cut], twist[1, :, cut]
        pair = jnp.concatenate(
            [
                (real * cosine - imag * sine).astype(BF16),
                (imag * cosine + real * sine).astype(BF16),
            ],
            axis=0,
        )
        out = jnp.dot(last[...], pair, preferred_element_type=F32) * scale
        send[:, :, cut] = out[:half].astype(BF16).reshape(send.shape[0], send.shape[1], quarter)
        keep[:, :, cut] = out[half:].astype(BF16).reshape(keep.shape[0], keep.shape[1], quarter)


def transform(place, pieces, spec, table):
    members, rows_half, block = pieces[0].shape
    a_rows = spec.shape[0] * spec.shape[2]
    out = (2 * members, rows_half, block)
    square = table.shape[1:]
    return pl.pallas_call(
        transform_kernel,
        in_specs=[SMEM] + [ANYWHERE] * (len(pieces) + 1) + [ANY],
        out_specs=[VMEM, VMEM],
        out_shape=[jax.ShapeDtypeStruct(out, BF16)] * 2,
        scratch_shapes=[
            pltpu.VMEM((4 * members, rows_half, block), BF16),
            pltpu.VMEM(spec.shape, BF16),
            pltpu.VMEM(square, BF16),
            pltpu.VMEM(square, BF16),
            pltpu.VMEM((4,) + square, BF16),
            pltpu.VMEM(((table.shape[0] - 12) // 4,) + square, BF16),
            pltpu.VMEM((2, a_rows, block), F32),
            pltpu.SemaphoreType.DMA((len(pieces) + 5,)),
        ],
        compiler_params=pltpu.CompilerParams(vmem_limit_bytes=48 * MIB),
        cost_estimate=SMALL,
    )(place, *pieces, spec, table)


def gate_kernel(core_ref, conv, prod, gate, gate_other, skip, skip_other, weight, keep, send):
    here, _, rows, block = conv.shape
    core = core_ref[0]
    pieces = []
    for side, (values, gains) in enumerate(((gate, skip), (gate_other, skip_other))):
        for n in range(here):
            high = jnp.bitwise_xor(core, side)
            at = jnp.where(high == 0, n, here - 1 - n)
            total = conv[at, high].astype(F32) + conv[at, 2 + high].astype(F32)
            total = total + gains[n] * prod[high * here + n].astype(F32)
            pieces.append((values[n].astype(F32) * total).astype(BF16))
    gated = jnp.concatenate(pieces, axis=0)
    mixed = jnp.dot(weight[...], gated, preferred_element_type=F32)
    outs = keep.shape[0]
    for r in range(rows):
        cut = slice(r * block, (r + 1) * block)
        keep[:, cut] = mixed[r * outs : (r + 1) * outs].astype(BF16)
        send[:, cut] = mixed[(rows + r) * outs : (rows + r + 1) * outs].astype(BF16)


def gate_and_project(core, conv, prod, gate, gate_other, skip, skip_other, weight):
    _, _, rows, block = conv.shape
    outs = weight.shape[0] // (2 * rows)
    return pl.pallas_call(
        gate_kernel,
        out_shape=[jax.ShapeDtypeStruct((outs, rows * block), BF16)] * 2,
        in_specs=[SMEM, VMEM, VMEM, VMEM, VMEM, SMEM, SMEM, VMEM],
        out_specs=[VMEM, VMEM],
        compiler_params=pltpu.CompilerParams(vmem_limit_bytes=16 * MIB),
        cost_estimate=SMALL,
    )(core, conv, prod, gate, gate_other, skip, skip_other, weight)


def halves_kernel(core_ref, kept, came, out, sem):
    half = kept.shape[1]
    copies = []
    for n, (ref, side) in enumerate(((kept, core_ref[0]), (came, 1 - core_ref[0]))):
        target = out.at[:, pl.ds(pl.multiple_of(side * half, half), half)]
        copies.append(pltpu.make_async_copy(ref, target, sem.at[n]))
    for copy in copies:
        copy.start()
    for copy in copies:
        copy.wait()


def place_halves(core, kept, came):
    outs, half = kept.shape
    return pl.pallas_call(
        halves_kernel,
        out_shape=jax.ShapeDtypeStruct((outs, 2 * half), BF16),
        in_specs=[SMEM, VMEM, VMEM],
        out_specs=ANY,
        scratch_shapes=[pltpu.SemaphoreType.DMA((2,))],
        compiler_params=pltpu.CompilerParams(vmem_limit_bytes=4 * MIB),
        cost_estimate=SMALL,
    )(core, kept, came)


def local_channels(k_feature, v_feature, q_feature, spectrum, skip_gain, out_weight):
    channels, tokens = k_feature.shape
    block = spectrum.shape[3]
    ctx_count = lax.axis_size("ctx")
    members = ctx_count // 2
    rows_half = tokens // block // 2
    a_half = spectrum.shape[2] // 2
    ctx, tp = lax.axis_index("ctx"), lax.axis_index("tp")
    core = tp.astype(jnp.int32).reshape(1)
    member = (ctx % members).astype(jnp.int32).reshape(1)
    place = (ctx // members * 2 + tp).astype(jnp.int32).reshape(1)
    tables = {
        name: jnp.asarray(table)
        for name, table in constant_tables(block, members, rows_half, a_half).items()
    }
    halves = [list(range(members)), list(range(members, 2 * members))]
    spread = lambda x: lax.all_to_all(x, "ctx", 0, 0, axis_index_groups=halves, tiled=True)
    across = lambda x: lax.ppermute(
        x, "ctx", [(d, (d + members) % ctx_count) for d in range(ctx_count)]
    )
    swap = lambda x: lax.ppermute(x, "tp", [(0, 1), (1, 0)])

    def joined(own, sent):
        start = ((1 - tp) * channels,) + (0,) * (own.ndim - 1)
        return lax.dynamic_update_slice(own, swap(sent), start)

    own, sent, other_rows = as_rows(core, block, k_feature, v_feature, spectrum=spectrum)
    product = joined(own, sent)
    product, spectrum, other_rows = lax.optimization_barrier((product, spectrum, other_rows))
    xa = spread(product)
    spec = arrange_spectrum(core, spectrum, swap(other_rows), tables["order"])
    xa, spec, q_feature, skip_gain, out_weight = lax.optimization_barrier(
        (xa, spec, q_feature, skip_gain, out_weight)
    )
    xb = swap(xa)
    za = across(xa)
    spec = spread(spec)
    gate, gate_sent = as_rows(core, block, q_feature)
    gate_other = swap(gate_sent)
    skip_other = swap(skip_gain)
    weight = projection(core, out_weight, rows_half)
    za, gate, gate_other, skip_other, weight = lax.optimization_barrier(
        (za, gate, gate_other, skip_other, weight)
    )
    zb = swap(za)

    send, keep = transform(place, (xa, xb, za, zb), spec, tables["transform"])
    total = (keep.astype(F32) + swap(send).astype(F32)).astype(BF16)
    conv = lax.all_to_all(
        total, "ctx", 0, 0, axis_index_groups=[last_order(members)], tiled=True
    ).reshape(channels, 4, rows_half, block)
    kept, sent = gate_and_project(
        core, conv, product, gate, gate_other, skip_gain, skip_other, weight
    )
    return place_halves(core, kept, swap(sent))


def local(k_feature, v_feature, q_feature, spectrum, skip_gain, out_weight):
    channels, tokens = k_feature.shape
    block = spectrum.shape[3]
    ctx_count, tp_count = lax.axis_size("ctx"), lax.axis_size("tp")
    by_channels = (
        tp_count == 2
        and ctx_count == 2 * channels * tp_count
        and tokens * ctx_count * 2 == block * block
        and tokens % (32 * block) == 0
        and spectrum.shape[2] % 32 == 0
        and block % 512 == 0
        and out_weight.shape[1] % 16 == 0
    )
    plan = local_channels if by_channels else local_general
    return plan(k_feature, v_feature, q_feature, spectrum, skip_gain, out_weight)


def solution(mesh):
    placed = (
        P("tp", "ctx"),
        P("tp", "ctx"),
        P("tp", "ctx"),
        P(None, "tp", "ctx", None),
        P("tp"),
        P(),
    )
    return jax.shard_map(
        local, mesh=mesh, in_specs=placed, out_specs=P("tp", "ctx"), check_vma=False
    )
```
